128 devices in a mesh: dp: 4 (over x), shard: 32 (over y, z, core).
Axes of the slice: x: 4, y: 4, z: 4, core: 2. Of those that a mesh axis runs over, the one named last changes fastest.
Arguments:
- inputs: bfloat16 [2, 128, 128, 768], P(None, ('dp', 'shard')), may hold values from -6 to 6
- lengths: int32 [2, 128], P(None, ('dp', 'shard')), may hold values from 1 to 128, 9830 in all within a row
- cotangent: float32 [2, 128, 64, 768], P(None, ('dp', 'shard')), may hold values from -6 to 6
- proj_in_one: bfloat16 [768, 2304], P(('dp', 'shard')), may hold values from -0.21875 to 0.21875
- proj_out_one: bfloat16 [768, 768], P(('dp', 'shard')), may hold values from -1.25 to 1.25
- up_one: bfloat16 [768, 3072], P(('dp', 'shard')), may hold values from -0.21875 to 0.21875
- down_one: bfloat16 [3072, 768], P(('dp', 'shard')), may hold values from -0.109375 to 0.109375
- vectors_one: bfloat16 [768, 13], P(('dp', 'shard')), may hold values from -4 to 4, as said below
- proj_in_two: bfloat16 [768, 2304], P(('dp', 'shard')), may hold values from -0.21875 to 0.21875
- proj_out_two: bfloat16 [768, 768], P(('dp', 'shard')), may hold values from -1.25 to 1.25
- up_two: bfloat16 [768, 3072], P(('dp', 'shard')), may hold values from -0.21875 to 0.21875
- down_two: bfloat16 [3072, 768], P(('dp', 'shard')), may hold values from -0.109375 to 0.109375
- vectors_two: bfloat16 [768, 13], P(('dp', 'shard')), may hold values from -4 to 4, as said below
Outputs:
- activations: bfloat16 [2, 128, 64, 768], P(None, ('dp', 'shard'))
- input_grad: float32 [2, 128, 128, 768], P(None, ('dp', 'shard'))
- proj_in_one_grad: float32 [768, 2304], P(('dp', 'shard'))
- proj_out_one_grad: float32 [768, 768], P(('dp', 'shard'))
- up_one_grad: float32 [768, 3072], P(('dp', 'shard'))
- down_one_grad: float32 [3072, 768], P(('dp', 'shard'))
- vectors_one_grad: float32 [768, 13], P(('dp', 'shard'))
- proj_in_two_grad: float32 [768, 2304], P(('dp', 'shard'))
- proj_out_two_grad: float32 [768, 768], P(('dp', 'shard'))
- up_two_grad: float32 [768, 3072], P(('dp', 'shard'))
- down_two_grad: float32 [3072, 768], P(('dp', 'shard'))
- vectors_two_grad: float32 [768, 13], P(('dp', 'shard'))
The draws below stay inside these ranges and needn't reach their ends.
Inputs may be any that keep to these rules, and one draw needn't show every extreme that they name: `lengths`: each entry is the length of one sequence row; the 128 entries of one micro-batch (one line of this array) sum to 9830 together, and the longest of them is exactly 128. `vectors_one`: columns 3 and 6 lie within 0.8 to 1.2. `vectors_two`: columns 3 and 6 lie within 0.8 to 1.2.
All inputs are finite; a program needn't handle non-finite values. No bound on the sum of `lengths` on one device may be relied on, other than what follows from the above.
Results may differ from the reference program's by a relative error of at most 0.023.
Values may be sent and summed in bfloat16 or wider, within the bound.
No kernel may reach another device: no remote copies, remote signals or barrier semaphores. Data moves between devices by JAX's collectives and lax.ppermute only.
A program may use at most 256 MiB of HBM per device.

```python
import math
import jax
import jax.numpy as jnp
import numpy as np
from jax import lax

D = 768
HEADS = 12
HEAD_DIM = 64
FF = 3072
DISTANCE_BUCKETS = 64
MICRO = 2
SEQ = 128
ROWS = 128


def vector_table(key):
    normal_draw = jax.random.truncated_normal(key, -4.0, 4.0, (D, 13), jnp.float32)
    column = jnp.arange(13)[None, :]
    spread = jnp.where(column == 12, 1.0, 0.3)
    gain_column = (column == 3) | (column == 6)
    return jnp.where(gain_column, 1.0 + 0.05 * normal_draw, spread * normal_draw).astype(jnp.bfloat16)


def draw_vectors_one(key, part):
    key = jax.random.fold_in(key, 11)
    return vector_table(key)


def draw_vectors_two(key, part):
    key = jax.random.fold_in(key, 12)
    return vector_table(key)


def block_scale(own_key, shape, cuts, least, largest):
    def one(position, blocks):
        draws = jax.random.uniform(jax.random.fold_in(jax.random.fold_in(own_key, 6), position), (blocks,), jnp.float32, least / len(cuts), largest / len(cuts))
        return jnp.repeat(jnp.exp(draws), shape[position] // blocks).reshape((-1,) + (1,) * (len(shape) - position - 1))

    level = one(*cuts[0])
    for cut in cuts[1:]:
        level = level * one(*cut)
    return level


def split_up(amount, total, limit, lean):
    portions = [(1 << 20) // math.isqrt(rank ** lean) + 1 for rank in range(2, amount + 1)]
    rest, given = total - limit - (amount - 1), [1] * (amount - 1)
    while rest > 0:
        candidates = [i for i in range(amount - 1) if given[i] < limit]
        whole, budget = sum([portions[i] for i in candidates]), rest
        for i in candidates:
            addition = min(limit - given[i], max(1, budget * portions[i] // whole), rest)
            given[i] = given[i] + addition
            rest = rest - addition
    return np.array([limit] + given)


def uneven_parts(own_key, count, total, reach, slope):
    if count == 2:
        one = jax.random.randint(own_key, (), max(1, total - reach), min(reach, total - 1) + 1)
        return jnp.stack([one, total - one])
    sizes = jnp.asarray(split_up(count, total, reach, slope), jnp.int32)
    couples = (count - 1) // 2
    source_of, receiver = sizes[1:1 + 2 * couples:2], sizes[2:2 + 2 * couples:2]
    room = jnp.minimum(source_of - 1, reach - receiver)
    moved = jax.random.randint(jax.random.fold_in(own_key, 1), (couples,), 0, 1 << 20) % (room + 1)
    sizes = sizes.at[1:1 + 2 * couples:2].set(source_of - moved).at[2:2 + 2 * couples:2].set(receiver + moved)
    return sizes[jax.random.permutation(jax.random.fold_in(own_key, 2), count)]


def centred(rng, extent, scale, bound, split=(), held_as=jnp.bfloat16):
    level = block_scale(rng, extent, split, -0.22, 0.18) if split else 1.0
    result = jax.random.normal(rng, extent, jnp.float32) * scale * level
    return jnp.minimum(jnp.maximum(result, -bound), bound).astype(held_as)


def setup_inputs(seed: int = 0) -> dict:
    streams_of = jax.random.split(jax.random.key(seed), 14)
    inputs = centred(streams_of[0], (MICRO, ROWS, SEQ, D), 1.0, 6.0, ((1, 128),))
    lengths = jax.vmap(lambda own: uneven_parts(own, ROWS, ROWS * SEQ * 3 // 5, SEQ, 2))(jax.random.split(streams_of[1], MICRO)).reshape((MICRO, ROWS)).astype(jnp.int32)
    cotangent = centred(streams_of[2], (MICRO, ROWS, SEQ // 2, D), 1.0, 6.0, ((1, 128),), jnp.float32)
    proj_in_one = centred(streams_of[3], (D, 3 * D), D ** -0.5, 0.21875, ((0, 128),))
    proj_out_one = centred(streams_of[4], (D, D), (D // 32) ** -0.5, 1.25, ((0, 128),))
    up_one = centred(streams_of[5], (D, FF), D ** -0.5, 0.21875, ((0, 128),))
    down_one = centred(streams_of[6], (FF, D), FF ** -0.5, 0.109375, ((0, 128),))
    vectors_one = draw_vectors_one(jax.random.fold_in(streams_of[13], 71), 0)
    proj_in_two = centred(streams_of[8], (D, 3 * D), D ** -0.5, 0.21875, ((0, 128),))
    proj_out_two = centred(streams_of[9], (D, D), (D // 32) ** -0.5, 1.25, ((0, 128),))
    up_two = centred(streams_of[10], (D, FF), D ** -0.5, 0.21875, ((0, 128),))
    down_two = centred(streams_of[11], (FF, D), FF ** -0.5, 0.109375, ((0, 128),))
    vectors_two = draw_vectors_two(jax.random.fold_in(streams_of[13], 71), 0)
    return {"inputs": inputs, "lengths": lengths, "cotangent": cotangent, "proj_in_one": proj_in_one, "proj_out_one": proj_out_one, "up_one": up_one, "down_one": down_one, "vectors_one": vectors_one, "proj_in_two": proj_in_two, "proj_out_two": proj_out_two, "up_two": up_two, "down_two": down_two, "vectors_two": vectors_two}


@jax.custom_vjp
def low(v):
    return lax.optimization_barrier(v.astype(jnp.bfloat16)).astype(jnp.float32)

@jax.custom_vjp
def low_back(v):
    return v

def low_keep(v):
    return (low(v), None)

def low_pass(kept, grad):
    return (grad,)

def back_keep(v):
    return (v, None)

def back_low(kept, grad):
    return (low(grad),)
low.defvjp(low_keep, low_pass)
low_back.defvjp(back_keep, back_low)
EPSILON = 1e-06
NEGATIVE = -1000000000.0
FULL_PRECISION = lax.Precision.HIGHEST

def matmul_high(left, right):
    return jnp.dot(left, right, precision=FULL_PRECISION)

def layer_norm(summed, gain, shift):
    centered = summed - lax.optimization_barrier(jnp.mean(summed, -1, keepdims=True))
    return centered * lax.rsqrt(lax.optimization_barrier(jnp.mean(centered * centered, -1, keepdims=True)) + EPSILON) * gain + shift

def bucket_index(query_count, key_count, stride):
    relative = jnp.arange(key_count)[None, :] - stride * jnp.arange(query_count)[:, None]
    return jnp.clip(relative + DISTANCE_BUCKETS // 2, 0, DISTANCE_BUCKETS - 1)

def funnel_layer(query_source, query_input, key_input, weights, key_valid, stride):
    proj_in, output_projection, up_weight, down_weight, vectors = weights
    query_count = query_input.shape[0]
    key_count = key_input.shape[0]
    columns = [vectors[:, column] for column in range(8)]
    hidden_bias = vectors[:, 8:12].reshape(-1)
    relative_bias_table = vectors[:, 12].reshape(HEADS, DISTANCE_BUCKETS)
    queries = low(low_back(matmul_high(query_input, proj_in[:, :D]) + columns[0]))
    queries = queries.reshape(query_count, HEADS, HEAD_DIM)
    pair_bias = jnp.concatenate([jnp.zeros_like(columns[1]), columns[1]])
    keys_values = low(low_back(matmul_high(key_input, proj_in[:, D:]) + pair_bias))
    keys = keys_values[:, :D].reshape(key_count, HEADS, HEAD_DIM)
    values = keys_values[:, D:].reshape(key_count, HEADS, HEAD_DIM)
    relative_position_bias = relative_bias_table[:, bucket_index(query_count, key_count, stride)]
    scores = jnp.einsum('qhe,khe->hqk', queries, keys, precision=FULL_PRECISION) * 0.125 + relative_position_bias
    scores = low_back(jnp.where(key_valid[None, None, :], scores, NEGATIVE))
    attention = low(jax.nn.softmax(scores, axis=-1))
    context = jnp.einsum('hqk,khe->qhe', attention, values, precision=FULL_PRECISION).reshape(query_count, D)
    context = low(low_back(context))
    attended = low_back(matmul_high(context, output_projection) + columns[2])
    normed = layer_norm(query_source + attended, columns[3], columns[4])
    hidden_pre = low_back(matmul_high(low(normed), up_weight) + hidden_bias)
    hidden_low = low(jax.nn.gelu(hidden_pre))
    feed_out = low_back(matmul_high(hidden_low, down_weight) + columns[5])
    return layer_norm(normed + feed_out, columns[6], columns[7])

def funnel_row(row_input, length, layer_one, layer_two):
    pooled = 0.5 * (row_input[0::2] + row_input[1::2])
    middle = funnel_layer(pooled, low(pooled), low(row_input), layer_one, jnp.arange(SEQ) < length, 2)
    middle_low = low(middle)
    return funnel_layer(middle, middle_low, middle_low, layer_two, jnp.arange(SEQ // 2) < (length + 1) // 2, 1)

def reference(inputs, lengths, cotangent, proj_in_one, proj_out_one, up_one, down_one, vectors_one, proj_in_two, proj_out_two, up_two, down_two, vectors_two):
    weights = tuple((weight.astype(jnp.float32) for weight in (proj_in_one, proj_out_one, up_one, down_one, vectors_one, proj_in_two, proj_out_two, up_two, down_two, vectors_two)))
    flat_inputs = inputs.astype(jnp.float32).reshape(MICRO * ROWS, SEQ, D)
    row_lengths = lengths.reshape(MICRO * ROWS).astype(jnp.int32)

    def forward(flat_rows, all_weights):
        row_step = jax.checkpoint(lambda row_input, length: funnel_row(row_input, length, all_weights[:5], all_weights[5:]))

        def scan_step(carried, row_pair):
            return (carried, row_step(row_pair[0], row_pair[1]))
        _, results = lax.scan(scan_step, jnp.zeros((), jnp.float32), (flat_rows, row_lengths))
        return results
    results, pullback = jax.vjp(forward, flat_inputs, weights)
    input_grad, weight_grads = pullback(cotangent.reshape(results.shape).astype(jnp.float32))
    return (results.reshape(MICRO, ROWS, SEQ // 2, D).astype(jnp.bfloat16), input_grad.reshape(MICRO, ROWS, SEQ, D), weight_grads[0], weight_grads[1], weight_grads[2], weight_grads[3], weight_grads[4], weight_grads[5], weight_grads[6], weight_grads[7], weight_grads[8], weight_grads[9])
```

```python
import jax
import jax.numpy as jnp
from jax import lax
from jax.experimental import pallas as pl
from jax.experimental.pallas import tpu as pltpu
from jax.sharding import PartitionSpec as P

AXES = ("dp", "shard")
F32, BF16 = jnp.float32, jnp.bfloat16
D, HEADS, HEAD_DIM, FF, BUCKETS = 768, 12, 64, 3072, 64
SEQ, HALF, TOKENS = 128, 64, 128
PAIRS = HEADS // 2
EPSILON = 1e-06
NEGATIVE = -1000000000.0
WRAP = 256

ROW = 6
CHUNK = 96
OUT_AT, UP_AT, VEC_AT, A_WIDTH, B_WIDTH = 2304, 3072, 6144, 6272, 3072
WIDTH = A_WIDTH + B_WIDTH

VMEM_LIMIT = 56 * 1024 * 1024


def place(virtual):
    core, block, v2, v1 = virtual // 64, virtual // 16 % 4, virtual // 4 % 4, virtual % 4
    z = (block - v1) % 4
    x, y = (v1, v2) if core == 0 else (v2, v1)
    return ((x * 4 + y) * 4 + z) * 2 + core


def moved(virtual, level, step):
    unit = 4 ** (level - 1)
    digit = virtual // unit % 4
    return virtual + ((digit + step) % 4 - digit) * unit


def spread_pairs(step):
    return [(f, place(moved(f, 1, -step))) for f in range(128)]


def line_pairs(step):
    return [(place(v), place(moved(v, 2, step))) for v in range(128)]


def along(axis_of_core, step):
    pairs = []
    for f in range(128):
        at = [f // 32, f // 8 % 4, f // 2 % 4]
        axis = axis_of_core[f % 2]
        at[axis] = (at[axis] + step) % 4
        pairs.append((f, ((at[0] * 4 + at[1]) * 4 + at[2]) * 2 + f % 2))
    return pairs


A_AXES, B_AXES = (0, 1), (2, 2)
SWAP = [(f, f ^ 1) for f in range(128)]


def permute(value, pairs):
    return lax.ppermute(value, AXES, pairs)


def back(pairs):
    return [(b, a) for a, b in pairs]


def place_scalars():
    x, inner = lax.axis_index("dp"), lax.axis_index("shard")
    y, z, core = inner // 8, inner // 2 % 4, inner % 2
    first = core == 0
    block = jnp.where(first, x + z, y + z) % 4
    other = jnp.where(first, y + z, x + z) % 4
    v2, v1 = jnp.where(first, y, x), jnp.where(first, x, y)
    return [core, block, other, v2, v1]


def mm(a, b):
    return lax.dot_general(a, b, (((1,), (0,)), ((), ())), preferred_element_type=F32)


def mm_nt(a, b):
    return lax.dot_general(a, b, (((1,), (1,)), ((), ())), preferred_element_type=F32)


def mm_tn(a, b):
    return lax.dot_general(a, b, (((0,), (0,)), ((), ())), preferred_element_type=F32)


def exact(a, b):
    return lax.dot_general(
        a, b, (((1,), (0,)), ((), ())), precision=lax.Precision.HIGHEST, preferred_element_type=F32
    )


def iota(shape, axis):
    return lax.broadcasted_iota(jnp.int32, shape, axis)


def onehot(condition):
    return condition.astype(F32).astype(BF16)


def split_hidden():
    source, out = iota((512, 512), 0), iota((512, 512), 1)
    return onehot((source // 4 == out % 128) & (source % 4 == out // 128))


def vmem(n):
    return [pl.BlockSpec(memory_space=pltpu.VMEM)] * n


def anyspace(n):
    return [pl.BlockSpec(memory_space=pl.ANY)] * n


SMEM = pl.BlockSpec(memory_space=pltpu.SMEM)


def params(limit=VMEM_LIMIT):
    return pltpu.CompilerParams(vmem_limit_bytes=limit)


def shape(*dims, dtype=BF16):
    return jax.ShapeDtypeStruct(dims, dtype)


def prepare_kernel(*refs):
    shards, out = refs[:10], refs[10]
    pad = onehot(iota((8, ROW), 0) == iota((8, ROW), 1))
    split = split_hidden()
    for layer in range(2):
        proj_in, proj_out, up, down, vectors = shards[5 * layer : 5 * layer + 5]
        at = WIDTH * layer
        out[:, at : at + OUT_AT] = mm(pad, proj_in[...]).astype(BF16)
        out[:, at + OUT_AT : at + UP_AT] = mm(pad, proj_out[...]).astype(BF16)
        for group in range(6):
            part = mm(pad, up[:, 512 * group : 512 * group + 512]).astype(BF16)
            part = mm(part, split).astype(BF16)
            for c in range(4):
                lane = at + UP_AT + 768 * c + 128 * group
                out[:, lane : lane + 128] = part[:, 128 * c : 128 * c + 128]
        out[:, at + VEC_AT : at + A_WIDTH] = jnp.zeros((8, 128), BF16)
        out[:, at + VEC_AT : at + VEC_AT + 13] = mm(pad, vectors[...]).astype(BF16)
        for c in range(4):
            rows = onehot(iota((8, 24), 1) == 4 * iota((8, 24), 0) + c)
            lane = at + A_WIDTH + 768 * c
            out[:, lane : lane + 768] = mm(rows, down[...]).astype(BF16)


def prepare(shards):
    return pl.pallas_call(
        prepare_kernel,
        out_shape=shape(8, 2 * WIDTH),
        in_specs=vmem(10),
        out_specs=vmem(1)[0],
        compiler_params=params(),
    )(*shards[0], *shards[1])


def block_of(out_rows, in_rows, rows, digit, k):
    wanted = iota((out_rows, in_rows), 0) - rows * lax.rem(digit + k, 4)
    source = iota((out_rows, in_rows), 1)
    return onehot((wanted == source) & (source < rows))


def widen_kernel(index, *refs):
    parts, outs = refs[:4], refs[4:]
    places = [block_of(24, 8, ROW, index[4], k) for k in range(4)]
    for layer in range(2):
        total = None
        for k in range(4):
            piece = mm(places[k], parts[k][:, WIDTH * layer : WIDTH * (layer + 1)])
            total = piece if total is None else total + piece
        outs[layer][...] = total.astype(BF16)


def widen(index, parts):
    return pl.pallas_call(
        widen_kernel,
        out_shape=[shape(24, WIDTH)] * 2,
        in_specs=[SMEM] + vmem(4),
        out_specs=vmem(2),
        compiler_params=params(),
    )(index, *parts)


def widen_more_kernel(index, *refs):
    parts, (out_a, out_b) = refs[:4], refs[4:]
    places = [block_of(CHUNK, 24, 24, index[3], k) for k in range(4)]
    for out, start, width in ((out_a, 0, A_WIDTH), (out_b, A_WIDTH, B_WIDTH)):
        total = None
        for k in range(4):
            piece = mm(places[k], parts[k][:, start : start + width])
            total = piece if total is None else total + piece
        out[...] = total.astype(BF16)


def widen_more(index, parts):
    return pl.pallas_call(
        widen_more_kernel,
        out_shape=[shape(CHUNK, A_WIDTH), shape(CHUNK, B_WIDTH)],
        in_specs=[SMEM] + vmem(4),
        out_specs=vmem(2),
        compiler_params=params(),
    )(index, *parts)


def gather_large(chunk_a, chunk_b):
    own_a, own_b = [chunk_a], [chunk_b]
    for k in (1, 3, 2):
        own_a.append(permute(chunk_a, along(A_AXES, -k)))
        own_b.append(permute(chunk_b, along(B_AXES, -k)))
    own_a, own_b = [[v[i] for i in (0, 1, 3, 2)] for v in (own_a, own_b)]
    other_a = [permute(v, SWAP) for v in own_a]
    other_b = [permute(v, SWAP) for v in own_b]
    return own_a + other_a + own_b + other_b


def narrow_kernel(index, in_a, in_b, *outs):
    places = [block_of(CHUNK, 24, 24, index[3], k) for k in range(4)]
    for k in range(4):
        outs[k][:, :A_WIDTH] = mm_tn(places[k], in_a[...]).astype(BF16)
        outs[k][:, A_WIDTH:] = mm_tn(places[k], in_b[...]).astype(BF16)


def narrow(index, in_a, in_b):
    return pl.pallas_call(
        narrow_kernel,
        out_shape=[shape(24, WIDTH)] * 4,
        in_specs=[SMEM] + vmem(2),
        out_specs=vmem(4),
        compiler_params=params(),
    )(index, in_a, in_b)


def wide(value):
    return value.astype(F32)


def narrow_more_kernel(index, *refs):
    parts, outs = refs[:8], refs[8:]
    places = [block_of(24, 8, ROW, index[4], k) for k in range(4)]
    split = split_hidden()
    for layer in range(2):
        one, two, three, four = parts[4 * layer : 4 * layer + 4]
        total = (wide(one[...]) + wide(two[...])) + (wide(three[...]) + wide(four[...]))
        total = total.astype(BF16)
        at = WIDTH * layer
        natural = []
        for group in range(6):
            lanes = [UP_AT + 768 * c + 128 * group for c in range(4)]
            part = jnp.concatenate([total[:, lane : lane + 128] for lane in lanes], 1)
            natural.append(mm_nt(part, split).astype(BF16))
        for k in range(4):
            outs[k][:, at : at + UP_AT] = mm_tn(places[k], total[:, :UP_AT]).astype(BF16)
            for group in range(6):
                lane = at + UP_AT + 512 * group
                outs[k][:, lane : lane + 512] = mm_tn(places[k], natural[group]).astype(BF16)
            outs[k][:, at + VEC_AT : at + WIDTH] = mm_tn(places[k], total[:, VEC_AT:]).astype(BF16)


def narrow_more(index, parts_one, parts_two):
    return pl.pallas_call(
        narrow_more_kernel,
        out_shape=[shape(8, 2 * WIDTH)] * 4,
        in_specs=[SMEM] + vmem(8),
        out_specs=vmem(4),
        compiler_params=params(),
    )(index, *parts_one, *parts_two)


def finish_kernel(*refs):
    parts, outs = refs[:4], refs[4:]
    for layer in range(2):
        proj_in, proj_out, up, down, vectors = outs[5 * layer : 5 * layer + 5]

        def total(start, stop):
            one, two, three, four = [
                wide(part[:, WIDTH * layer + start : WIDTH * layer + stop]) for part in parts
            ]
            return (one + two) + (three + four)

        proj_in[...] = total(0, OUT_AT)[:ROW]
        proj_out[...] = total(OUT_AT, UP_AT)[:ROW]
        up[...] = total(UP_AT, VEC_AT)[:ROW]
        vectors[...] = total(VEC_AT, A_WIDTH)[:ROW, :13]
        rows = None
        for c in range(4):
            place_rows = (iota((24, 8), 0) == 4 * iota((24, 8), 1) + c).astype(F32)
            lane = A_WIDTH + 768 * c
            piece = exact(place_rows, total(lane, lane + 768))
            rows = piece if rows is None else rows + piece
        down[...] = rows


def finish(parts):
    one = [shape(ROW, n, dtype=F32) for n in (2304, 768, 3072)]
    one += [shape(24, 768, dtype=F32), shape(ROW, 13, dtype=F32)]
    return pl.pallas_call(
        finish_kernel,
        out_shape=one + one,
        in_specs=vmem(4),
        out_specs=vmem(10),
        compiler_params=params(),
    )(*parts)


def reduce_large(theirs_a, mine_a, theirs_b, mine_b):
    out = []
    for theirs, mine, axes in ((theirs_a, mine_a, A_AXES), (theirs_b, mine_b, B_AXES)):
        total = (wide(mine) + wide(permute(theirs, SWAP))).astype(BF16)
        parts = [total[CHUNK * k : CHUNK * (k + 1)] for k in range(4)]
        got = [permute(parts[k], along(axes, k)) for k in (1, 3, 2)]
        out.append(
            ((wide(parts[0]) + wide(got[0])) + (wide(got[1]) + wide(got[2]))).astype(BF16)
        )
    return out


class Weights:
    def __init__(self, index, chunks, scratch, sems):
        self.w_in, self.w_out, self.w_up, self.w_down, self.vec = scratch
        own_a, other_a, own_b, other_b = (chunks[4 * i : 4 * i + 4] for i in range(4))
        self.copies = [[] for _ in range(8)]
        for side in range(2):
            core = index[0] if side == 0 else 1 - index[0]
            first = index[1] if side == 0 else index[2]
            a_refs, b_refs = ((own_a, own_b), (other_a, other_b))[side]
            for k in range(4):
                row = pl.multiple_of(384 * core + CHUNK * lax.rem(first + k, 4), 32)
                sem = 4 * side + k
                targets = [
                    (a_refs[k], VEC_AT, 128, self.vec, row),
                    (a_refs[k], 0, 2304, self.w_in, row),
                    (a_refs[k], OUT_AT, 768, self.w_out, row),
                    (a_refs[k], UP_AT, 3072, self.w_up, row),
                ]
                for c in range(4):
                    target = pl.multiple_of(768 * c + row, 32)
                    targets.append((b_refs[k], 768 * c, 768, self.w_down, target))
                for group, (ref, lane, width, out, at) in enumerate(targets):
                    self.copies[group].append(
                        pltpu.make_async_copy(
                            ref.at[:, lane : lane + width],
                            out.at[pl.ds(at, CHUNK), :],
                            sems.at[group, sem],
                        )
                    )

    def start(self, groups):
        for group in groups:
            for copy in self.copies[group]:
                copy.start()

    def wait(self, *groups):
        for group in groups:
            for copy in self.copies[group]:
                copy.wait()


VEC, IN, OUT, UP, DOWN = 0, 1, 2, 3, 4
WEIGHT_SCRATCH = [
    pltpu.VMEM((768, 2304), BF16),
    pltpu.VMEM((768, 768), BF16),
    pltpu.VMEM((768, 3072), BF16),
    pltpu.VMEM((3072, 768), BF16),
    pltpu.VMEM((768, 128), BF16),
    pltpu.SemaphoreType.DMA((8, 8)),
]


def bucket_rows(sign=1):
    lane = iota((D, WRAP), 1)
    lane = lane if sign > 0 else lax.rem(WRAP - lane, WRAP)
    distance = jnp.where(lane < WRAP // 2, lane, lane - WRAP)
    bucket = jnp.clip(distance + BUCKETS // 2, 0, BUCKETS - 1)
    return lax.rem(iota((D, WRAP), 0), BUCKETS) == bucket


def head_mask():
    return iota((16, D), 1) // BUCKETS == iota((16, D), 0)


def position_bias(table, stride, keys, bias_ref):
    per_head = jnp.where(head_mask(), table, 0.0).astype(BF16)
    extended = mm(per_head, onehot(bucket_rows()))
    for head in range(HEADS):
        row = jnp.broadcast_to(extended[head : head + 1], (HALF, WRAP))
        rolled = pltpu.roll(row, 0, 1, stride=stride, stride_axis=0)
        bias_ref[head // 2, HALF * (head % 2) : HALF * (head % 2 + 1), :] = rolled[:, :keys]


def by_head(value):
    low = iota(value.shape, 1) < HEAD_DIM
    zero = jnp.zeros_like(value)
    return jnp.concatenate([jnp.where(low, value, zero), jnp.where(low, zero, value)], 0)


def join_heads(value):
    top, bottom = value[:HALF], value[HALF:]
    return jnp.where(iota(top.shape, 1) < HEAD_DIM, top, bottom)


def norm_forward(summed, gain, shift):
    centered = summed - jnp.mean(summed, -1, keepdims=True)
    inverse = lax.rsqrt(jnp.mean(centered * centered, -1, keepdims=True) + EPSILON)
    normal = centered * inverse
    return normal * gain + shift, normal, inverse


def norm_backward(upstream, normal, inverse, gain):
    scaled = upstream * gain
    bracket = (
        scaled
        - jnp.mean(scaled, -1, keepdims=True)
        - normal * jnp.mean(scaled * normal, -1, keepdims=True)
    )
    return inverse * bracket, rowsum(upstream * normal), rowsum(upstream)


def rowsum(value):
    return jnp.sum(value, 0, keepdims=True)


GELU_A, GELU_B = 0.7978845608028654, 0.044715


def gelu(x):
    return 0.5 * x * (1.0 + jnp.tanh(GELU_A * (x + GELU_B * (x * x * x))))


def gelu_slope(x):
    square = x * x
    t = jnp.tanh(GELU_A * (x + GELU_B * (square * x)))
    inner = GELU_A * (1.0 + 3.0 * GELU_B * square)
    return 0.5 * (1.0 + t) + 0.5 * x * (1.0 - t * t) * inner


KEPT = ("q", "k", "v", "prob", "context", "normal1", "inverse1", "low1", "pre", "hidden", "normal2", "inverse2")


def kept_shapes(keys):
    return {
        "q": ((TOKENS, D), BF16),
        "k": ((2 * keys, D), BF16),
        "v": ((2 * keys, D), BF16),
        "prob": ((2 * PAIRS, 128, keys), F32),
        "context": ((TOKENS, D), BF16),
        "normal1": ((TOKENS, D), F32),
        "inverse1": ((TOKENS, 128), F32),
        "low1": ((TOKENS, D), BF16),
        "pre": ((TOKENS, FF), F32),
        "hidden": ((TOKENS, FF), BF16),
        "normal2": ((TOKENS, D), F32),
        "inverse2": ((TOKENS, 128), F32),
    }


def transpose_vectors(w, vt):
    w.wait(VEC)
    vt[...] = jnp.transpose(w.vec[...].astype(F32))[:16]


def layer_forward(w, kept, vt, bias, x_query, x_key, source, valid, stride, keys):
    transpose_vectors(w, vt)
    position_bias(vt[12:13, :], stride, keys, bias)
    w.wait(IN)
    query_low = x_query[...]
    kept["q"][...] = (mm(query_low, w.w_in[:, :D]) + vt[0:1, :]).astype(BF16)
    key_low = x_key[...]
    kept["k"][...] = mm(key_low, w.w_in[:, D : 2 * D]).astype(BF16)
    kept["v"][...] = (mm(key_low, w.w_in[:, 2 * D :]) + vt[1:2, :]).astype(BF16)
    for row in range(2):
        usable = iota((128, keys), 1) < valid[row]
        for pair in range(PAIRS):
            lanes = slice(128 * pair, 128 * pair + 128)
            q = by_head(kept["q"][HALF * row : HALF * (row + 1), lanes])
            k = kept["k"][keys * row : keys * (row + 1), lanes]
            scores = mm_nt(q, k) * 0.125 + bias[pair]
            scores = jnp.where(usable, scores, NEGATIVE)
            unnormed = jnp.exp(scores - jnp.max(scores, -1, keepdims=True))
            prob = unnormed / jnp.sum(unnormed, -1, keepdims=True)
            kept["prob"][PAIRS * row + pair] = prob
            v = kept["v"][keys * row : keys * (row + 1), lanes]
            context = join_heads(mm(prob.astype(BF16), v))
            kept["context"][HALF * row : HALF * (row + 1), lanes] = context.astype(BF16)
    w.wait(OUT)
    attended = mm(kept["context"][...], w.w_out[...]) + vt[2:3, :]
    normed, normal, inverse = norm_forward(source + attended, vt[3:4, :], vt[4:5, :])
    kept["normal1"][...] = normal
    kept["inverse1"][...] = jnp.broadcast_to(inverse, (TOKENS, 128))
    normed_low = normed.astype(BF16)
    kept["low1"][...] = normed_low
    w.wait(UP)
    feed = normed + vt[5:6, :]
    for c in range(4):
        lanes = slice(D * c, D * (c + 1))
        pre = mm(normed_low, w.w_up[:, lanes]) + vt[8 + c : 9 + c, :]
        kept["pre"][:, lanes] = pre
        hidden = gelu(pre).astype(BF16)
        kept["hidden"][:, lanes] = hidden
        w.wait(DOWN + c)
        feed = feed + mm(hidden, w.w_down[lanes, :])
    result, normal, inverse = norm_forward(feed, vt[6:7, :], vt[7:8, :])
    kept["normal2"][...] = normal
    kept["inverse2"][...] = jnp.broadcast_to(inverse, (TOKENS, 128))
    return result


class GradientWriter:
    SLOTS = 3

    def __init__(self, stage, sems):
        self.stage, self.sems, self.flying, self.count = stage, sems, [None] * self.SLOTS, 0

    def write(self, value, theirs, mine, lane):
        slot = self.count % self.SLOTS
        self.count += 1
        self.wait(slot)
        width = value.shape[1]
        self.stage[slot, :, :width] = value.astype(BF16)
        self.flying[slot] = [
            pltpu.make_async_copy(
                self.stage.at[slot, pl.ds(384 * half, 384), pl.ds(0, width)],
                target.at[:, lane : lane + width],
                self.sems.at[slot, half],
            )
            for half, target in enumerate((theirs, mine))
        ]
        for copy in self.flying[slot]:
            copy.start()

    def wait(self, slot):
        for copy in self.flying[slot] or ():
            copy.wait()
        self.flying[slot] = None

    def finish(self):
        for slot in range(self.SLOTS):
            self.wait(slot)


def reorder(index, source, target):
    for side in range(2):
        core = 1 - index[0] if side == 0 else index[0]
        first = index[2] if side == 0 else index[1]
        for k in range(4):
            row = pl.multiple_of(384 * core + CHUNK * lax.rem(first + k, 4), 32)
            at = 384 * side + CHUNK * k
            target[at : at + CHUNK, :] = source[pl.ds(row, CHUNK), :]


def turned(index, value, plain, ordered):
    width = value.shape[0]
    plain[:, :width] = jnp.transpose(value)
    reorder(index, plain, ordered)
    return ordered[:, :width]


BACKWARD_SCRATCH = [
    pltpu.VMEM((768, 256), BF16),
    pltpu.VMEM((768, 256), BF16),
    pltpu.VMEM((768, 128), F32),
    pltpu.VMEM((768, 128), F32),
    pltpu.VMEM((16, WRAP), F32),
    pltpu.VMEM((3, 768, 768), BF16),
    pltpu.SemaphoreType.DMA((3, 2)),
]


def layer_backward(w, kept, vt, index, x_query, x_key, upstream, stride, keys, grads, work, scratch):
    theirs_a, mine_a, theirs_b, mine_b = grads
    dq, dk, dv = work
    plain, ordered, plain_vec, ordered_vec, table, stage, sems = scratch
    writer = GradientWriter(stage, sems)
    dsum2, gain2, shift2 = norm_backward(
        upstream, kept["normal2"][...], kept["inverse2"][:, :1], vt[6:7, :]
    )
    feed_grad = dsum2.astype(BF16)
    down_bias = rowsum(wide(feed_grad))
    normed_grad = dsum2
    w.wait(UP)
    hidden_bias = []
    pre_grads = []
    for c in range(4):
        lanes = slice(D * c, D * (c + 1))
        w.wait(DOWN + c)
        hidden_grad = mm_nt(feed_grad, w.w_down[lanes, :])
        pre_grad = (gelu_slope(kept["pre"][:, lanes]) * hidden_grad).astype(BF16)
        hidden_bias.append(rowsum(wide(pre_grad)))
        normed_grad = normed_grad + mm_nt(pre_grad, w.w_up[:, lanes])
        pre_grads.append(pre_grad)
        hidden = turned(index, kept["hidden"][:, lanes], plain, ordered)
        writer.write(mm(hidden, feed_grad), theirs_b, mine_b, D * c)
    low1 = turned(index, kept["low1"][...], plain, ordered)
    for c in range(4):
        writer.write(mm(low1, pre_grads[c]), theirs_a, mine_a, UP_AT + D * c)
    dsum1, gain1, shift1 = norm_backward(
        normed_grad, kept["normal1"][...], kept["inverse1"][:, :1], vt[3:4, :]
    )
    attended_grad = dsum1.astype(BF16)
    out_bias = rowsum(wide(attended_grad))
    context = turned(index, kept["context"][...], plain, ordered)
    writer.write(mm(context, attended_grad), theirs_a, mine_a, OUT_AT)
    w.wait(OUT)
    context_grad = mm_nt(attended_grad, w.w_out[...]).astype(BF16)
    table[...] = jnp.zeros((16, WRAP), F32)
    mirror = (2 * keys, WRAP)
    mirror = onehot(lax.rem(lax.rem(iota(mirror, 0), keys) + iota(mirror, 1), WRAP) == 0)
    for pair in range(PAIRS):
        lanes = slice(128 * pair, 128 * pair + 128)
        pair_scores = []
        for row in range(2):
            here = slice(HALF * row, HALF * (row + 1))
            there = slice(keys * row, keys * (row + 1))
            grad = by_head(context_grad[here, lanes])
            prob = kept["prob"][PAIRS * row + pair]
            v = kept["v"][there, lanes]
            prob_grad = mm_nt(grad, v)
            dv[there, lanes] = mm_tn(prob.astype(BF16), grad).astype(BF16)
            score = prob * (prob_grad - jnp.sum(prob_grad * prob, -1, keepdims=True))
            score = score.astype(BF16)
            q = by_head(kept["q"][here, lanes])
            k = kept["k"][there, lanes]
            dq[here, lanes] = (0.125 * join_heads(mm(score, k))).astype(BF16)
            dk[there, lanes] = (0.125 * mm_tn(score, q)).astype(BF16)
            pair_scores.append(score)
        spread = mm(jnp.concatenate(pair_scores, 1), mirror)
        for half in range(2):
            rolled = pltpu.roll(
                spread[HALF * half : HALF * (half + 1)], 0, 1, stride=stride, stride_axis=0
            )
            table[2 * pair + half : 2 * pair + half + 1, :] = rowsum(rolled)
    dq_low, dk_low, dv_low = dq[...], dk[...], dv[...]
    w.wait(IN)
    source_grad = dsum1 + mm_nt(dq_low, w.w_in[:, :D])
    key_side = mm_nt(dk_low, w.w_in[:, D : 2 * D]) + mm_nt(dv_low, w.w_in[:, 2 * D :])
    writer.write(mm(turned(index, x_query[...], plain, ordered), dq_low), theirs_a, mine_a, 0)
    key_rows = turned(index, x_key[...], plain, ordered)
    writer.write(mm(key_rows, dk_low), theirs_a, mine_a, D)
    writer.write(mm(key_rows, dv_low), theirs_a, mine_a, 2 * D)
    buckets = lax.dot_general(
        table[...],
        bucket_rows(-1).astype(F32),
        (((1,), (1,)), ((), ())),
        precision=lax.Precision.HIGHEST,
        preferred_element_type=F32,
    )
    table_grad = rowsum(jnp.where(head_mask(), buckets, 0.0))
    rows = [rowsum(wide(dq_low)), rowsum(wide(dv_low)), out_bias, gain1, shift1, down_bias]
    rows += [gain2, shift2] + hidden_bias + [table_grad]
    rows.append(jnp.zeros((128 - len(rows), D), F32))
    plain_vec[...] = jnp.transpose(jnp.concatenate(rows, 0))
    reorder(index, plain_vec, ordered_vec)
    writer.write(ordered_vec[...], theirs_a, mine_a, VEC_AT)
    writer.finish()
    return source_grad, key_side


GRAD_SHAPES = [shape(384, A_WIDTH)] * 2 + [shape(384, B_WIDTH)] * 2


def pooling():
    return 0.5 * (iota((TOKENS, 2 * SEQ), 1) // 2 == iota((TOKENS, 2 * SEQ), 0)).astype(F32)


def one_forward_kernel(index, tokens, *refs):
    chunks, refs = refs[:16], refs[16:]
    middle, pooled_low = refs[:2]
    kept = dict(zip(KEPT, refs[2:14]))
    vt, bias, *scratch = refs[14:]
    w = Weights(index, chunks, scratch[:5], scratch[5])
    w.start(range(8))
    pooled = mm(pooling().astype(BF16), tokens[...])
    pooled_low[...] = pooled.astype(BF16)
    valid = [index[5], index[6]]
    middle[...] = layer_forward(w, kept, vt, bias, pooled_low, tokens, pooled, valid, 2, SEQ)


def one_forward(index, tokens, chunks):
    kept = [shape(*dims, dtype=dtype) for dims, dtype in kept_shapes(SEQ).values()]
    return pl.pallas_call(
        one_forward_kernel,
        out_shape=[shape(TOKENS, D, dtype=F32), shape(TOKENS, D)] + kept,
        in_specs=[SMEM] + vmem(1) + anyspace(16),
        out_specs=vmem(14),
        scratch_shapes=[pltpu.VMEM((16, D), F32), pltpu.VMEM((PAIRS, 128, SEQ), F32)] + WEIGHT_SCRATCH,
        compiler_params=params(),
    )(index, tokens, *chunks)


def two_kernel(index, middle, cotangent, *refs):
    chunks, refs = refs[:16], refs[16:]
    result, upstream, *grads = refs[:6]
    refs = refs[6:]
    kept = dict(zip(KEPT, refs[:12]))
    vt, bias, middle_low, dq, dk, dv, *scratch = refs[12:]
    w = Weights(index, chunks, scratch[:5], scratch[5])
    w.start(range(8))
    middle_low[...] = middle[...].astype(BF16)
    valid = [(index[5] + 1) // 2, (index[6] + 1) // 2]
    out = layer_forward(w, kept, vt, bias, middle_low, middle_low, middle[...], valid, 1, HALF)
    result[...] = out.astype(BF16)
    w.wait = lambda *groups: None
    source_grad, key_side = layer_backward(
        w, kept, vt, index, middle_low, middle_low, cotangent[...], 1, HALF, grads, (dq, dk, dv), scratch[6:]
    )
    upstream[...] = source_grad + key_side


def two(index, middle, cotangent, chunks):
    kept = [pltpu.VMEM(dims, dtype) for dims, dtype in kept_shapes(HALF).values()]
    return pl.pallas_call(
        two_kernel,
        out_shape=[shape(TOKENS, D), shape(TOKENS, D, dtype=F32)] + GRAD_SHAPES,
        in_specs=[SMEM] + vmem(2) + anyspace(16),
        out_specs=vmem(2) + anyspace(4),
        scratch_shapes=kept
        + [pltpu.VMEM((16, D), F32), pltpu.VMEM((PAIRS, 128, HALF), F32)]
        + [pltpu.VMEM((TOKENS, D), BF16)] * 4
        + WEIGHT_SCRATCH
        + BACKWARD_SCRATCH,
        compiler_params=params(),
    )(index, middle, cotangent, *chunks)


def one_backward_kernel(index, tokens, pooled_low, upstream, *refs):
    kept = dict(zip(KEPT, refs[:12]))
    chunks, refs = refs[12:28], refs[28:]
    input_grad, *grads = refs[:5]
    vt, dq, dk, dv, *scratch = refs[5:]
    w = Weights(index, chunks, scratch[:5], scratch[5])
    w.start((VEC, UP, DOWN, DOWN + 1, DOWN + 2, DOWN + 3, OUT, IN))
    transpose_vectors(w, vt)
    source_grad, key_side = layer_backward(
        w, kept, vt, index, pooled_low, tokens, upstream[...], 2, SEQ, grads, (dq, dk, dv), scratch[6:]
    )
    repeated = lax.dot_general(
        pooling(),
        source_grad,
        (((0,), (0,)), ((), ())),
        precision=lax.Precision.HIGHEST,
        preferred_element_type=F32,
    )
    input_grad[...] = key_side + repeated


def one_backward(index, tokens, pooled_low, upstream, kept, chunks):
    return pl.pallas_call(
        one_backward_kernel,
        out_shape=[shape(2 * SEQ, D, dtype=F32)] + GRAD_SHAPES,
        in_specs=[SMEM] + vmem(15) + anyspace(16),
        out_specs=vmem(1) + anyspace(4),
        scratch_shapes=[pltpu.VMEM((16, D), F32), pltpu.VMEM((TOKENS, D), BF16)]
        + [pltpu.VMEM((2 * SEQ, D), BF16)] * 2
        + WEIGHT_SCRATCH
        + BACKWARD_SCRATCH,
        compiler_params=params(),
    )(index, tokens, pooled_low, upstream, *kept, *chunks)


def local(inputs, lengths, cotangent, *weights):
    index = jnp.stack([*place_scalars(), lengths[0, 0], lengths[1, 0], jnp.zeros((), jnp.int32)])
    tokens = inputs.reshape(2 * SEQ, D)
    blob = prepare((weights[:5], weights[5:]))
    lines = widen(index, [permute(blob, spread_pairs(k)) for k in range(4)])
    chunks = []
    for line in lines:
        parts = [line] + [permute(line, line_pairs(-k)) for k in (1, 2, 3)]
        chunks.append(gather_large(*widen_more(index, parts)))
    middle, pooled_low, *kept = one_forward(index, tokens, chunks[0])
    result, upstream, *grads_two = two(index, middle, cotangent.reshape(TOKENS, D), chunks[1])
    sum_two = reduce_large(*grads_two)
    input_grad, *grads_one = one_backward(index, tokens, pooled_low, upstream, kept, chunks[0])
    sum_one = reduce_large(*grads_one)
    parts = []
    for total in (sum_one, sum_two):
        pieces = narrow(index, *total)
        parts.append([pieces[0]] + [permute(pieces[k], line_pairs(k)) for k in (1, 2, 3)])
    pieces = narrow_more(index, *parts)
    grads = finish([permute(pieces[k], back(spread_pairs(k))) for k in range(4)])
    return (
        result.reshape(2, 1, HALF, D),
        input_grad.reshape(2, 1, SEQ, D),
        *grads,
    )


def solution(mesh):
    rows = P(None, AXES, None, None)
    shard = P(AXES, None)
    return jax.shard_map(
        local,
        mesh=mesh,
        in_specs=(rows, P(None, AXES), rows) + (shard,) * 10,
        out_specs=(rows, rows) + (shard,) * 10,
        check_vma=False,
    )
```

```python
import functools

import jax
import jax.numpy as jnp
from jax import lax
from jax.experimental import pallas as pl
from jax.experimental.pallas import tpu as pltpu
from jax.sharding import PartitionSpec as P

AXES = ("dp", "shard")
F32, BF16 = jnp.float32, jnp.bfloat16
D, HEADS, HEAD_DIM, FF, BUCKETS = 768, 12, 64, 3072, 64
SEQ, HALF, TOKENS = 128, 64, 128
PAIRS = HEADS // 2
EPSILON = 1e-06
NEGATIVE = -1000000000.0
WRAP = 256

ROW = 6
CHUNK = 96
OUT_AT, VEC_AT, UP_AT, DOWN_AT, WIDTH = 2304, 3072, 3200, 6272, 9344
A_WIDTH, B_WIDTH = DOWN_AT, WIDTH - DOWN_AT
ATTN, FEED = UP_AT, WIDTH - UP_AT
LINE_LANES = {ATTN: ATTN, FEED: 3072}

VMEM_LIMIT = 56 * 1024 * 1024


def place(core, block, v2, v1):
    z = (block - v1) % 4
    x, y = (v1, v2) if core == 0 else (v2, v1)
    return ((x * 4 + y) * 4 + z) * 2 + core


def virtual(device):
    x, y, z, half = device // 32, device // 8 % 4, device // 2 % 4, device % 2
    if y % 2 == 0:
        return 0, x, y + half, z
    return 1, x % 2 + 2 * (y // 2), (x + half) % 4, z


def spread_pairs(step):
    pairs = []
    for f in range(128):
        core, block, v2, v1 = virtual(f)
        pairs.append((f, place(core, block, v2, (v1 - step) % 4)))
    return pairs


def line_pairs(step):
    pairs = []
    for v in range(128):
        core, block, v2, v1 = v // 64, v // 16 % 4, v // 4 % 4, v % 4
        pairs.append((place(core, block, v2, v1), place(core, block, (v2 + step) % 4, v1)))
    return pairs


def run_row(core, block, run):
    even = 192 * block + 96 * run
    odd = 192 * lax.rem(block, 2) + 384 * run + 48 + 96 * (block // 2)
    return pl.multiple_of(jnp.where(core == 0, even, odd), 16)


def along(axis_of_core, step):
    pairs = []
    for f in range(128):
        at = [f // 32, f // 8 % 4, f // 2 % 4]
        axis = axis_of_core[f % 2]
        at[axis] = (at[axis] + step) % 4
        pairs.append((f, ((at[0] * 4 + at[1]) * 4 + at[2]) * 2 + f % 2))
    return pairs


A_AXES, B_AXES = (0, 1), (2, 2)
SWAP = [(f, f ^ 1) for f in range(128)]


def permute(value, pairs):
    return lax.ppermute(value, AXES, pairs)


def back(pairs):
    return [(b, a) for a, b in pairs]


def place_scalars():
    x, inner = lax.axis_index("dp"), lax.axis_index("shard")
    y, z, core = inner // 8, inner // 2 % 4, inner % 2
    first = core == 0
    block = jnp.where(first, x + z, y + z) % 4
    other = jnp.where(first, y + z, x + z) % 4
    v2, v1 = jnp.where(first, y, x), jnp.where(first, x, y)
    return [core, block, other, v2, v1]


def mm(a, b):
    return lax.dot_general(a, b, (((1,), (0,)), ((), ())), preferred_element_type=F32)


def mm_nt(a, b):
    return lax.dot_general(a, b, (((1,), (1,)), ((), ())), preferred_element_type=F32)


def mm_tn(a, b):
    return lax.dot_general(a, b, (((0,), (0,)), ((), ())), preferred_element_type=F32)


def exact(a, b):
    return lax.dot_general(
        a, b, (((1,), (0,)), ((), ())), precision=lax.Precision.HIGHEST, preferred_element_type=F32
    )


def iota(shape, axis):
    return lax.broadcasted_iota(jnp.int32, shape, axis)


def onehot(condition):
    return condition.astype(F32).astype(BF16)


def split_hidden():
    source, out = iota((512, 512), 0), iota((512, 512), 1)
    return onehot((source // 4 == out % 128) & (source % 4 == out // 128))


def vmem(n):
    return [pl.BlockSpec(memory_space=pltpu.VMEM)] * n


def anyspace(n):
    return [pl.BlockSpec(memory_space=pl.ANY)] * n


SMEM = pl.BlockSpec(memory_space=pltpu.SMEM)


def params(limit=VMEM_LIMIT):
    return pltpu.CompilerParams(vmem_limit_bytes=limit)


def cost(microseconds):
    return pl.CostEstimate(flops=0, bytes_accessed=int(microseconds * 3.5e6), transcendentals=0)


def shape(*dims, dtype=BF16):
    return jax.ShapeDtypeStruct(dims, dtype)


def prepare_kernel(*refs):
    shards, out = refs[:10], refs[10]
    pad = onehot(iota((8, ROW), 0) == iota((8, ROW), 1))
    split = split_hidden()
    for layer in range(2):
        proj_in, proj_out, up, down, vectors = shards[5 * layer : 5 * layer + 5]
        at = WIDTH * layer
        out[:, at : at + OUT_AT] = mm(pad, proj_in[...]).astype(BF16)
        out[:, at + OUT_AT : at + VEC_AT] = mm(pad, proj_out[...]).astype(BF16)
        for group in range(6):
            part = mm(pad, up[:, 512 * group : 512 * group + 512]).astype(BF16)
            part = mm(part, split).astype(BF16)
            for c in range(4):
                lane = at + UP_AT + 768 * c + 128 * group
                out[:, lane : lane + 128] = part[:, 128 * c : 128 * c + 128]
        out[:, at + VEC_AT : at + UP_AT] = jnp.zeros((8, 128), BF16)
        out[:, at + VEC_AT : at + VEC_AT + 13] = mm(pad, vectors[...]).astype(BF16)
        for c in range(4):
            rows = onehot(iota((8, 24), 1) == 4 * iota((8, 24), 0) + c)
            lane = at + DOWN_AT + 768 * c
            out[:, lane : lane + 768] = mm(rows, down[...]).astype(BF16)


def prepare(shards):
    return pl.pallas_call(
        prepare_kernel,
        out_shape=shape(8, 2 * WIDTH),
        in_specs=vmem(10),
        out_specs=vmem(1)[0],
        compiler_params=params(),
        cost_estimate=cost(4),
    )(*shards[0], *shards[1])


def block_of(out_rows, in_rows, rows, digit, k):
    wanted = iota((out_rows, in_rows), 0) - rows * lax.rem(digit + k, 4)
    source = iota((out_rows, in_rows), 1)
    return onehot((wanted == source) & (source < rows))


def widen_kernel(index, *refs):
    parts, out = refs[:4], refs[4]
    total = None
    for k in range(4):
        piece = mm(block_of(24, 8, ROW, index[4], k), parts[k][...])
        total = piece if total is None else total + piece
    out[...] = total.astype(BF16)


def widen(index, parts):
    return pl.pallas_call(
        widen_kernel,
        out_shape=shape(24, 2 * WIDTH),
        in_specs=[SMEM] + vmem(4),
        out_specs=vmem(1)[0],
        compiler_params=params(),
        cost_estimate=cost(4),
    )(index, *parts)


def line_block(index, k):
    v2 = lax.rem(index[3] + k, 4)
    first = jnp.where(index[0] == 0, 0, lax.rem(index[1], 2))
    unit = lax.rem(v2 - first + 4, 4)
    row, source = iota((CHUNK, 24), 0), iota((CHUNK, 24), 1)
    here = (row // 48 == unit // 2) & (row % 12 // 6 == lax.rem(unit, 2))
    return onehot(here & (source == row % 48 // 12 * 6 + row % 6))


def widen_more_kernel(layer, index, *refs):
    parts, (out_a, out_b, both) = refs[:4], refs[-3:]
    places = [line_block(index, k) for k in range(4)]
    for out, start, width in ((out_a, 0, A_WIDTH), (out_b, A_WIDTH, B_WIDTH)):
        total = None
        for k in range(4):
            at = WIDTH * layer + start
            piece = mm(places[k], parts[k][:, at : at + width])
            total = piece if total is None else total + piece
        total = total.astype(BF16)
        out[...] = total
        both[:, start : start + width] = total


def widen_more(layer, index, parts, after=()):
    return pl.pallas_call(
        functools.partial(widen_more_kernel, layer),
        out_shape=[shape(CHUNK, A_WIDTH), shape(CHUNK, B_WIDTH), shape(CHUNK, WIDTH)],
        in_specs=[SMEM] + vmem(4) + anyspace(len(after)),
        out_specs=vmem(3),
        compiler_params=params(),
        cost_estimate=cost(5),
    )(index, *parts, *after)


def tie(value, *before):
    return lax.optimization_barrier((value, *before))[0]


class Gather:
    def __init__(self, chunk, *before):
        self.a, self.b, both = lax.optimization_barrier((*chunk, *before))[:3]
        self.own_swap = permute(both, SWAP)
        self.near = [permute(self.a, along(A_AXES, -k)) for k in (1, 3)]
        self.near += [permute(self.b, along(B_AXES, -k)) for k in (1, 3)]

    def finish(self, *before):
        far_a, far_b, *near = lax.optimization_barrier(
            (self.a, self.b, *self.near, self.own_swap, *before)
        )
        far = [permute(far_a, along(A_AXES, -2)), permute(far_b, along(B_AXES, -2))]
        swapped = [None, None, permute(near[2], SWAP), permute(near[3], SWAP)]
        for k in range(2):
            swapped[k] = permute(tie(near[k], swapped[k + 2]), SWAP)
        far_a, far_b, *_ = lax.optimization_barrier((*far, *swapped))
        far_swapped = [permute(far_a, SWAP), permute(far_b, SWAP)]
        return [
            *(self.a, self.near[0], far[0], self.near[1]),
            *(swapped[0], far_swapped[0], swapped[1]),
            *(self.b, self.near[2], far[1], self.near[3]),
            *(swapped[2], far_swapped[1], swapped[3]),
            self.own_swap,
        ]


def narrow_kernel(layer, index, *refs):
    parts = refs[:11]
    outs, (stage, sems) = refs[-6:-2], refs[-2:]
    places = [line_block(index, k) for k in range(4)]
    at = 0
    for width in (ATTN, FEED):
        line = LINE_LANES[width]
        count = 4 if line == width else 7
        (base, *got), parts = parts[:count], parts[count:]
        for start, stop, pieces in ((0, line, got[:3]), (line, width, got[3:])):
            if start == stop:
                continue
            one, two, three = [wide(piece[...]) for piece in pieces]
            total = ((wide(base[:, start:stop]) + one) + (two + three)).astype(BF16)
            for k in range(4):
                stage[k, :, at + start : at + stop] = mm_tn(places[k], total).astype(BF16)
        at += width
    copies = []
    for k in range(4):
        target = outs[k].at[:, pl.ds(WIDTH * layer, WIDTH)]
        copies.append(pltpu.make_async_copy(stage.at[k], target, sems.at[k]))
        copies[k].start()
    for copy in copies:
        copy.wait()


def narrow(layer, index, units, onto=()):
    return pl.pallas_call(
        functools.partial(narrow_kernel, layer),
        out_shape=[shape(24, 2 * WIDTH)] * 4,
        in_specs=[SMEM] + vmem(11) + anyspace(len(onto)),
        out_specs=anyspace(4),
        scratch_shapes=[pltpu.VMEM((4, 24, WIDTH), BF16), pltpu.SemaphoreType.DMA((4,))],
        input_output_aliases={12 + k: k for k in range(len(onto))},
        compiler_params=params(),
        cost_estimate=cost(6),
    )(index, *sum(units, []), *onto)


def wide(value):
    return value.astype(F32)


def narrow_more_kernel(index, *refs):
    parts, outs = refs[:4], refs[4:]
    places = [block_of(24, 8, ROW, index[4], k) for k in range(4)]
    split = split_hidden()
    for layer in range(2):
        at = WIDTH * layer
        one, two, three, four = [wide(part[:, at : at + WIDTH]) for part in parts]
        total = ((one + two) + (three + four)).astype(BF16)
        natural = []
        for group in range(6):
            lanes = [UP_AT + 768 * c + 128 * group for c in range(4)]
            part = jnp.concatenate([total[:, lane : lane + 128] for lane in lanes], 1)
            natural.append(mm_nt(part, split).astype(BF16))
        for k in range(4):
            outs[k][:, at : at + UP_AT] = mm_tn(places[k], total[:, :UP_AT]).astype(BF16)
            for group in range(6):
                lane = at + UP_AT + 512 * group
                outs[k][:, lane : lane + 512] = mm_tn(places[k], natural[group]).astype(BF16)
            outs[k][:, at + DOWN_AT : at + WIDTH] = mm_tn(places[k], total[:, DOWN_AT:]).astype(BF16)


def narrow_more(index, parts):
    return pl.pallas_call(
        narrow_more_kernel,
        out_shape=[shape(8, 2 * WIDTH)] * 4,
        in_specs=[SMEM] + vmem(4),
        out_specs=vmem(4),
        compiler_params=params(),
        cost_estimate=cost(6),
    )(index, *parts)


def finish_kernel(*refs):
    parts, outs = refs[:4], refs[4:]
    for layer in range(2):
        proj_in, proj_out, up, down, vectors = outs[5 * layer : 5 * layer + 5]

        def total(start, stop):
            at = WIDTH * layer
            one, two, three, four = [wide(part[:, at + start : at + stop]) for part in parts]
            return (one + two) + (three + four)

        proj_in[...] = total(0, OUT_AT)[:ROW]
        proj_out[...] = total(OUT_AT, VEC_AT)[:ROW]
        up[...] = total(UP_AT, DOWN_AT)[:ROW]
        vectors[...] = total(VEC_AT, UP_AT)[:ROW, :13]
        rows = None
        for c in range(4):
            place_rows = (iota((24, 8), 0) == 4 * iota((24, 8), 1) + c).astype(F32)
            lane = DOWN_AT + 768 * c
            piece = exact(place_rows, total(lane, lane + 768))
            rows = piece if rows is None else rows + piece
        down[...] = rows


def finish(parts):
    one = [shape(ROW, n, dtype=F32) for n in (2304, 768, 3072)]
    one += [shape(24, 768, dtype=F32), shape(ROW, 13, dtype=F32)]
    return pl.pallas_call(
        finish_kernel,
        out_shape=one + one,
        in_specs=vmem(4),
        out_specs=vmem(10),
        compiler_params=params(),
        cost_estimate=cost(4),
    )(*parts)


def add_kernel(mine, theirs, *refs):
    line = LINE_LANES[mine.shape[1]]
    base, *outs = refs[-7:] if line < mine.shape[1] else refs[-4:]
    for k in range(4):
        rows = slice(CHUNK * k, CHUNK * (k + 1))
        total = (wide(mine[rows]) + wide(theirs[rows])).astype(BF16)
        if k == 0:
            base[...] = total
        else:
            outs[k - 1][...] = total[:, :line]
            if len(outs) > 3:
                outs[k + 2][...] = total[:, line:]


def add_halves(mine, theirs, after=()):
    width = mine.shape[1]
    line = LINE_LANES[width]
    out = [shape(CHUNK, width)] + [shape(CHUNK, line)] * 3
    if line < width:
        out += [shape(CHUNK, width - line)] * 3
    return pl.pallas_call(
        add_kernel,
        out_shape=out,
        in_specs=vmem(2) + anyspace(len(after)),
        out_specs=vmem(len(out)),
        compiler_params=params(),
        cost_estimate=cost(width / 1000),
    )(mine, theirs, *after)


def send_sums(parts, axes, steps, *before):
    parts = [parts[k - 1] for k in steps]
    if before:
        parts = lax.optimization_barrier((*parts, *before))[: len(steps)]
    return [permute(part, along(axes, k)) for part, k in zip(parts, steps)]


def send_near(sums, *before):
    near = send_sums(sums[1:4], A_AXES, (1, 3), *before)
    return near + (send_sums(sums[4:7], B_AXES, (1, 3), *before) if len(sums) > 4 else [])


def send_far(sums, *before):
    far = send_sums(sums[1:4], A_AXES, (2,), *before)
    return far + (send_sums(sums[4:7], B_AXES, (2,), *before) if len(sums) > 4 else [])


def received(sums, near, far):
    got = [sums[0], near[0], near[1], far[0]]
    return got + [near[2], near[3], far[1]] if len(sums) > 4 else got


class Weights:
    def __init__(self, index, chunks, scratch, sems):
        self.w_in, self.w_out, self.w_up, self.w_down, self.vec = scratch
        own_a, other_a, own_b, other_b = chunks[:4], chunks[4:7], chunks[7:11], chunks[11:14]
        joined = chunks[14]
        other_a = [joined.at[:, :A_WIDTH], *other_a]
        other_b = [joined.at[:, A_WIDTH:WIDTH], *other_b]
        self.copies = [[] for _ in range(8)]
        for side in range(2):
            core = index[0] if side == 0 else 1 - index[0]
            first = index[1] if side == 0 else index[2]
            a_refs, b_refs = ((own_a, own_b), (other_a, other_b))[side]
            for k in range(4):
                block = lax.rem(first + k, 4)
                for run in range(2):
                    row = run_row(core, block, run)
                    rows = pl.ds(48 * run, 48)
                    a, b = a_refs[k], b_refs[k]
                    targets = [
                        (a, VEC_AT, 128, self.vec, row),
                        (a, 0, 2304, self.w_in, row),
                        (a, OUT_AT, 768, self.w_out, row),
                        (a, UP_AT, 3072, self.w_up, row),
                    ]
                    for c in range(4):
                        target = pl.multiple_of(768 * c + row, 16)
                        targets.append((b, 768 * c, 768, self.w_down, target))
                    for group, (ref, lane, width, out, at) in enumerate(targets):
                        self.copies[group].append(
                            (
                                ref.at[rows, pl.ds(lane, width)],
                                out.at[pl.ds(at, 48), :],
                                sems.at[group, 8 * side + 2 * k + run],
                            )
                        )

    def start(self, groups):
        for group in groups:
            self.copies[group] = [pltpu.make_async_copy(*copy) for copy in self.copies[group]]
            for copy in self.copies[group]:
                copy.start()

    def wait(self, *groups):
        for group in groups:
            for copy in self.copies[group]:
                copy.wait()


VEC, IN, OUT, UP, DOWN = 0, 1, 2, 3, 4
WEIGHT_SCRATCH = [
    pltpu.VMEM((768, 2304), BF16),
    pltpu.VMEM((768, 768), BF16),
    pltpu.VMEM((768, 3072), BF16),
    pltpu.VMEM((3072, 768), BF16),
    pltpu.VMEM((768, 128), BF16),
    pltpu.SemaphoreType.DMA((8, 16)),
]


def bucket_rows(sign=1):
    lane = iota((D, WRAP), 1)
    lane = lane if sign > 0 else lax.rem(WRAP - lane, WRAP)
    distance = jnp.where(lane < WRAP // 2, lane, lane - WRAP)
    bucket = jnp.clip(distance + BUCKETS // 2, 0, BUCKETS - 1)
    return lax.rem(iota((D, WRAP), 0), BUCKETS) == bucket


def head_mask():
    return iota((16, D), 1) // BUCKETS == iota((16, D), 0)


def position_bias(table, stride, keys, bias_ref):
    per_head = jnp.where(head_mask(), table, 0.0).astype(BF16)
    extended = mm(per_head, onehot(bucket_rows()))
    for head in range(HEADS):
        row = jnp.broadcast_to(extended[head : head + 1], (HALF, WRAP))
        rolled = pltpu.roll(row, 0, 1, stride=stride, stride_axis=0)
        bias_ref[head // 2, HALF * (head % 2) : HALF * (head % 2 + 1), :] = rolled[:, :keys]


def by_head(value):
    low = iota(value.shape, 1) < HEAD_DIM
    zero = jnp.zeros_like(value)
    return jnp.concatenate([jnp.where(low, value, zero), jnp.where(low, zero, value)], 0)


def join_heads(value):
    top, bottom = value[:HALF], value[HALF:]
    return jnp.where(iota(top.shape, 1) < HEAD_DIM, top, bottom)


def norm_forward(summed, gain, shift):
    centered = summed - jnp.mean(summed, -1, keepdims=True)
    inverse = lax.rsqrt(jnp.mean(centered * centered, -1, keepdims=True) + EPSILON)
    normal = centered * inverse
    return normal * gain + shift, normal, inverse


def norm_backward(upstream, normal, inverse, gain):
    scaled = upstream * gain
    bracket = (
        scaled
        - jnp.mean(scaled, -1, keepdims=True)
        - normal * jnp.mean(scaled * normal, -1, keepdims=True)
    )
    return inverse * bracket, rowsum(upstream * normal), rowsum(upstream)


def rowsum(value):
    return jnp.sum(value, 0, keepdims=True)


GELU_A, GELU_B = 0.7978845608028654, 0.044715


def gelu(x):
    return 0.5 * x * (1.0 + jnp.tanh(GELU_A * (x + GELU_B * (x * x * x))))


def gelu_slope(x):
    square = x * x
    t = jnp.tanh(GELU_A * (x + GELU_B * (square * x)))
    inner = GELU_A * (1.0 + 3.0 * GELU_B * square)
    return 0.5 * (1.0 + t) + 0.5 * x * (1.0 - t * t) * inner


KEPT = ("q", "k", "v", "prob", "context", "normal1", "inverse1", "low1", "pre", "hidden", "normal2", "inverse2")


def kept_shapes(keys):
    return {
        "q": ((TOKENS, D), BF16),
        "k": ((2 * keys, D), BF16),
        "v": ((2 * keys, D), BF16),
        "prob": ((2 * PAIRS, 128, keys), F32),
        "context": ((TOKENS, D), BF16),
        "normal1": ((TOKENS, D), F32),
        "inverse1": ((TOKENS, 128), F32),
        "low1": ((TOKENS, D), BF16),
        "pre": ((TOKENS, FF), F32),
        "hidden": ((TOKENS, FF), BF16),
        "normal2": ((TOKENS, D), F32),
        "inverse2": ((TOKENS, 128), F32),
    }


def transpose_vectors(w, vt):
    w.wait(VEC)
    vt[...] = jnp.transpose(w.vec[...].astype(F32))[:16]


def layer_forward(w, kept, vt, bias, x_query, x_key, source, valid, stride, keys):
    transpose_vectors(w, vt)
    position_bias(vt[12:13, :], stride, keys, bias)
    w.wait(IN)
    query_low = x_query[...]
    kept["q"][...] = (mm(query_low, w.w_in[:, :D]) + vt[0:1, :]).astype(BF16)
    key_low = x_key[...]
    kept["k"][...] = mm(key_low, w.w_in[:, D : 2 * D]).astype(BF16)
    kept["v"][...] = (mm(key_low, w.w_in[:, 2 * D :]) + vt[1:2, :]).astype(BF16)
    for row in range(2):
        usable = iota((128, keys), 1) < valid[row]
        for pair in range(PAIRS):
            lanes = slice(128 * pair, 128 * pair + 128)
            q = by_head(kept["q"][HALF * row : HALF * (row + 1), lanes])
            k = kept["k"][keys * row : keys * (row + 1), lanes]
            scores = mm_nt(q, k) * 0.125 + bias[pair]
            scores = jnp.where(usable, scores, NEGATIVE)
            unnormed = jnp.exp(scores - jnp.max(scores, -1, keepdims=True))
            prob = unnormed / jnp.sum(unnormed, -1, keepdims=True)
            kept["prob"][PAIRS * row + pair] = prob
            v = kept["v"][keys * row : keys * (row + 1), lanes]
            context = join_heads(mm(prob.astype(BF16), v))
            kept["context"][HALF * row : HALF * (row + 1), lanes] = context.astype(BF16)
    w.wait(OUT)
    attended = mm(kept["context"][...], w.w_out[...]) + vt[2:3, :]
    normed, normal, inverse = norm_forward(source + attended, vt[3:4, :], vt[4:5, :])
    kept["normal1"][...] = normal
    kept["inverse1"][...] = jnp.broadcast_to(inverse, (TOKENS, 128))
    normed_low = normed.astype(BF16)
    kept["low1"][...] = normed_low
    w.wait(UP)
    feed = normed + vt[5:6, :]
    for c in range(4):
        lanes = slice(D * c, D * (c + 1))
        pre = mm(normed_low, w.w_up[:, lanes]) + vt[8 + c : 9 + c, :]
        kept["pre"][:, lanes] = pre
        hidden = gelu(pre).astype(BF16)
        kept["hidden"][:, lanes] = hidden
        w.wait(DOWN + c)
        feed = feed + mm(hidden, w.w_down[lanes, :])
    result, normal, inverse = norm_forward(feed, vt[6:7, :], vt[7:8, :])
    kept["normal2"][...] = normal
    kept["inverse2"][...] = jnp.broadcast_to(inverse, (TOKENS, 128))
    return result


class GradientWriter:
    SLOTS = 3

    def __init__(self, stage, sems):
        self.stage, self.sems, self.flying, self.count = stage, sems, [None] * self.SLOTS, 0

    def write(self, value, theirs, mine, lane):
        slot = self.count % self.SLOTS
        self.count += 1
        self.wait(slot)
        width = value.shape[1]
        self.stage[slot, :, :width] = value.astype(BF16)
        self.flying[slot] = [
            pltpu.make_async_copy(
                self.stage.at[slot, pl.ds(384 * half, 384), pl.ds(0, width)],
                target.at[:, lane : lane + width],
                self.sems.at[slot, half],
            )
            for half, target in enumerate((theirs, mine))
        ]
        for copy in self.flying[slot]:
            copy.start()

    def wait(self, slot):
        for copy in self.flying[slot] or ():
            copy.wait()
        self.flying[slot] = None

    def finish(self):
        for slot in range(self.SLOTS):
            self.wait(slot)


def reorder(index, source, target):
    for side in range(2):
        core = 1 - index[0] if side == 0 else index[0]
        first = index[2] if side == 0 else index[1]
        for k in range(4):
            for run in range(2):
                row = run_row(core, lax.rem(first + k, 4), run)
                at = 384 * side + CHUNK * k + 48 * run
                target[at : at + 48, :] = source[pl.ds(row, 48), :]


def turned(index, value, plain, ordered):
    width = value.shape[0]
    plain[:, :width] = jnp.transpose(value)
    reorder(index, plain, ordered)
    return ordered[:, :width]


BACKWARD_SCRATCH = [
    pltpu.VMEM((768, 256), BF16),
    pltpu.VMEM((768, 256), BF16),
    pltpu.VMEM((768, 128), F32),
    pltpu.VMEM((768, 128), F32),
    pltpu.VMEM((16, WRAP), F32),
    pltpu.VMEM((3, 768, 768), BF16),
    pltpu.SemaphoreType.DMA((3, 2)),
]


def feed_backward(w, kept, vt, index, upstream, grads, scratch):
    theirs, mine = grads
    plain, ordered, *_, stage, sems = scratch
    writer = GradientWriter(stage, sems)
    dsum2, gain2, shift2 = norm_backward(
        upstream, kept["normal2"][...], kept["inverse2"][:, :1], vt[6:7, :]
    )
    feed_grad = dsum2.astype(BF16)
    down_bias = rowsum(wide(feed_grad))
    normed_grad = dsum2
    w.wait(UP)
    hidden_bias = []
    pre_grads = []
    for c in range(4):
        lanes = slice(D * c, D * (c + 1))
        w.wait(DOWN + c)
        hidden_grad = mm_nt(feed_grad, w.w_down[lanes, :])
        pre_grad = (gelu_slope(kept["pre"][:, lanes]) * hidden_grad).astype(BF16)
        hidden_bias.append(rowsum(wide(pre_grad)))
        normed_grad = normed_grad + mm_nt(pre_grad, w.w_up[:, lanes])
        pre_grads.append(pre_grad)
        hidden = turned(index, kept["hidden"][:, lanes], plain, ordered)
        writer.write(mm(hidden, feed_grad), theirs, mine, FF + D * c)
    low1 = turned(index, kept["low1"][...], plain, ordered)
    for c in range(4):
        writer.write(mm(low1, pre_grads[c]), theirs, mine, D * c)
    writer.finish()
    zero = jnp.zeros((1, D), F32)
    rows = [zero] * 5 + [down_bias, gain2, shift2] + hidden_bias + [zero] * 4
    return normed_grad, jnp.concatenate(rows, 0)


def attention_backward(
    w, kept, vt, index, x_query, x_key, normed_grad, vector_rows, stride, keys, grads, work, scratch
):
    theirs, mine = grads
    dq, dk, dv = work
    plain, ordered, plain_vec, ordered_vec, table, stage, sems = scratch
    writer = GradientWriter(stage, sems)
    dsum1, gain1, shift1 = norm_backward(
        normed_grad, kept["normal1"][...], kept["inverse1"][:, :1], vt[3:4, :]
    )
    attended_grad = dsum1.astype(BF16)
    out_bias = rowsum(wide(attended_grad))
    context = turned(index, kept["context"][...], plain, ordered)
    writer.write(mm(context, attended_grad), theirs, mine, OUT_AT)
    w.wait(OUT)
    context_grad = mm_nt(attended_grad, w.w_out[...]).astype(BF16)
    table[...] = jnp.zeros((16, WRAP), F32)
    mirror = (2 * keys, WRAP)
    mirror = onehot(lax.rem(lax.rem(iota(mirror, 0), keys) + iota(mirror, 1), WRAP) == 0)
    for pair in range(PAIRS):
        lanes = slice(128 * pair, 128 * pair + 128)
        pair_scores = []
        for row in range(2):
            here = slice(HALF * row, HALF * (row + 1))
            there = slice(keys * row, keys * (row + 1))
            grad = by_head(context_grad[here, lanes])
            prob = kept["prob"][PAIRS * row + pair]
            v = kept["v"][there, lanes]
            prob_grad = mm_nt(grad, v)
            dv[there, lanes] = mm_tn(prob.astype(BF16), grad).astype(BF16)
            score = prob * (prob_grad - jnp.sum(prob_grad * prob, -1, keepdims=True))
            score = score.astype(BF16)
            q = by_head(kept["q"][here, lanes])
            k = kept["k"][there, lanes]
            dq[here, lanes] = (0.125 * join_heads(mm(score, k))).astype(BF16)
            dk[there, lanes] = (0.125 * mm_tn(score, q)).astype(BF16)
            pair_scores.append(score)
        spread = mm(jnp.concatenate(pair_scores, 1), mirror)
        for half in range(2):
            rolled = pltpu.roll(
                spread[HALF * half : HALF * (half + 1)], 0, 1, stride=stride, stride_axis=0
            )
            table[2 * pair + half : 2 * pair + half + 1, :] = rowsum(rolled)
    dq_low, dk_low, dv_low = dq[...], dk[...], dv[...]
    w.wait(IN)
    source_grad = dsum1 + mm_nt(dq_low, w.w_in[:, :D])
    key_side = mm_nt(dk_low, w.w_in[:, D : 2 * D]) + mm_nt(dv_low, w.w_in[:, 2 * D :])
    writer.write(mm(turned(index, x_query[...], plain, ordered), dq_low), theirs, mine, 0)
    key_rows = turned(index, x_key[...], plain, ordered)
    writer.write(mm(key_rows, dk_low), theirs, mine, D)
    writer.write(mm(key_rows, dv_low), theirs, mine, 2 * D)
    buckets = lax.dot_general(
        table[...],
        bucket_rows(-1).astype(F32),
        (((1,), (1,)), ((), ())),
        precision=lax.Precision.HIGHEST,
        preferred_element_type=F32,
    )
    table_grad = rowsum(jnp.where(head_mask(), buckets, 0.0))
    rows = [rowsum(wide(dq_low)), rowsum(wide(dv_low)), out_bias, gain1, shift1]
    rows += [vector_rows[5:12, :], table_grad, jnp.zeros((115, D), F32)]
    plain_vec[...] = jnp.transpose(jnp.concatenate(rows, 0))
    reorder(index, plain_vec, ordered_vec)
    writer.write(ordered_vec[...], theirs, mine, VEC_AT)
    writer.finish()
    return source_grad, key_side


ATTN_GRADS, FEED_GRADS = [shape(384, ATTN)] * 2, [shape(384, FEED)] * 2
FOR_ATTENTION = ("q", "k", "v", "prob", "context", "normal1", "inverse1")
FOR_FEED = ("low1", "pre", "hidden", "normal2", "inverse2")


def pooling():
    return 0.5 * (iota((TOKENS, 2 * SEQ), 1) // 2 == iota((TOKENS, 2 * SEQ), 0)).astype(F32)


def one_forward_kernel(index, tokens, *refs):
    chunks = refs[:15]
    middle, pooled_low, *refs = refs[-22:]
    kept = dict(zip(KEPT, refs[:12]))
    vt, bias, *scratch = refs[12:]
    w = Weights(index, chunks, scratch[:5], scratch[5])
    w.start(range(8))
    pooled = mm(pooling().astype(BF16), tokens[...])
    pooled_low[...] = pooled.astype(BF16)
    valid = [index[5], index[6]]
    middle[...] = layer_forward(w, kept, vt, bias, pooled_low, tokens, pooled, valid, 2, SEQ)


def one_forward(index, tokens, chunks, after):
    kept = [shape(*dims, dtype=dtype) for dims, dtype in kept_shapes(SEQ).values()]
    return pl.pallas_call(
        one_forward_kernel,
        out_shape=[shape(TOKENS, D, dtype=F32), shape(TOKENS, D)] + kept,
        in_specs=[SMEM] + vmem(1) + anyspace(15 + len(after)),
        out_specs=vmem(14),
        scratch_shapes=[pltpu.VMEM((16, D), F32), pltpu.VMEM((PAIRS, 128, SEQ), F32)] + WEIGHT_SCRATCH,
        compiler_params=params(),
        cost_estimate=cost(13),
    )(index, tokens, *chunks, *after)


def two_forward_kernel(index, middle, cotangent, *refs):
    chunks, refs = refs[:15], refs[15:]
    result, normed_grad, vector_rows, theirs, mine = refs[:5]
    kept = dict(zip(FOR_ATTENTION + FOR_FEED, refs[5:17]))
    vt, bias, middle_low, *scratch = refs[17:]
    w = Weights(index, chunks, scratch[:5], scratch[5])
    w.start(range(8))
    middle_low[...] = middle[...].astype(BF16)
    valid = [(index[5] + 1) // 2, (index[6] + 1) // 2]
    out = layer_forward(w, kept, vt, bias, middle_low, middle_low, middle[...], valid, 1, HALF)
    result[...] = out.astype(BF16)
    w.wait = lambda *groups: None
    normed_grad[...], vector_rows[...] = feed_backward(
        w, kept, vt, index, cotangent[...], (theirs, mine), scratch[6:]
    )


def two_forward(index, middle, cotangent, chunks):
    dims = kept_shapes(HALF)
    kept = [shape(*dims[name][0], dtype=dims[name][1]) for name in FOR_ATTENTION]
    scratch = [pltpu.VMEM(*dims[name]) for name in FOR_FEED]
    outs = pl.pallas_call(
        two_forward_kernel,
        out_shape=[shape(TOKENS, D), shape(TOKENS, D, dtype=F32), shape(16, D, dtype=F32)] + FEED_GRADS + kept,
        in_specs=[SMEM] + vmem(2) + anyspace(15),
        out_specs=vmem(3) + anyspace(2) + vmem(7),
        scratch_shapes=scratch
        + [pltpu.VMEM((16, D), F32), pltpu.VMEM((PAIRS, 128, HALF), F32), pltpu.VMEM((TOKENS, D), BF16)]
        + WEIGHT_SCRATCH
        + BACKWARD_SCRATCH,
        compiler_params=params(),
        cost_estimate=cost(19),
    )(index, middle, cotangent, *chunks)
    return outs[:3], outs[3:5], outs[5:]


def two_backward_kernel(index, middle, normed_grad, vector_rows, *refs):
    kept = dict(zip(FOR_ATTENTION, refs[:7]))
    chunks, refs = refs[7:22], refs[22:]
    upstream, *grads = refs[:3]
    vt, middle_low, dq, dk, dv, *scratch = refs[3:]
    w = Weights(index, chunks, scratch[:5], scratch[5])
    w.start((VEC, OUT, IN))
    middle_low[...] = middle[...].astype(BF16)
    transpose_vectors(w, vt)
    source_grad, key_side = attention_backward(
        w, kept, vt, index, middle_low, middle_low, normed_grad[...], vector_rows, 1, HALF, grads, (dq, dk, dv), scratch[6:]
    )
    upstream[...] = source_grad + key_side


def two_backward(index, middle, normed_grad, vector_rows, kept, chunks):
    upstream, *grads = pl.pallas_call(
        two_backward_kernel,
        out_shape=[shape(TOKENS, D, dtype=F32)] + ATTN_GRADS,
        in_specs=[SMEM] + vmem(10) + anyspace(15),
        out_specs=vmem(1) + anyspace(2),
        scratch_shapes=[pltpu.VMEM((16, D), F32)]
        + [pltpu.VMEM((TOKENS, D), BF16)] * 4
        + WEIGHT_SCRATCH
        + BACKWARD_SCRATCH,
        compiler_params=params(),
        cost_estimate=cost(11),
    )(index, middle, normed_grad, vector_rows, *kept, *chunks)
    return upstream, grads


def one_feed_kernel(index, upstream, *refs):
    kept = dict(zip(FOR_FEED, refs[:5]))
    chunks = refs[5:20]
    normed_grad, vector_rows, theirs, mine, vt, *scratch = refs[-18:]
    w = Weights(index, chunks, scratch[:5], scratch[5])
    w.start((VEC, UP, DOWN, DOWN + 1, DOWN + 2, DOWN + 3))
    transpose_vectors(w, vt)
    normed_grad[...], vector_rows[...] = feed_backward(
        w, kept, vt, index, upstream[...], (theirs, mine), scratch[6:]
    )


def one_feed(index, upstream, kept, chunks, after):
    normed_grad, vector_rows, *grads = pl.pallas_call(
        one_feed_kernel,
        out_shape=[shape(TOKENS, D, dtype=F32), shape(16, D, dtype=F32)] + FEED_GRADS,
        in_specs=[SMEM] + vmem(6) + anyspace(15 + len(after)),
        out_specs=vmem(2) + anyspace(2),
        scratch_shapes=[pltpu.VMEM((16, D), F32)] + WEIGHT_SCRATCH + BACKWARD_SCRATCH,
        compiler_params=params(),
        cost_estimate=cost(15),
    )(index, upstream, *kept, *chunks, *after)
    return (normed_grad, vector_rows), grads


def one_backward_kernel(index, tokens, pooled_low, normed_grad, vector_rows, *refs):
    kept = dict(zip(FOR_ATTENTION, refs[:7]))
    chunks = refs[7:22]
    input_grad, *grads = refs[-20:-17]
    vt, dq, dk, dv, *scratch = refs[-17:]
    w = Weights(index, chunks, scratch[:5], scratch[5])
    w.start((VEC, OUT, IN))
    transpose_vectors(w, vt)
    source_grad, key_side = attention_backward(
        w, kept, vt, index, pooled_low, tokens, normed_grad[...], vector_rows, 2, SEQ, grads, (dq, dk, dv), scratch[6:]
    )
    repeated = lax.dot_general(
        pooling(),
        source_grad,
        (((0,), (0,)), ((), ())),
        precision=lax.Precision.HIGHEST,
        preferred_element_type=F32,
    )
    input_grad[...] = key_side + repeated


def one_backward(index, tokens, pooled_low, normed_grad, vector_rows, kept, chunks, after):
    input_grad, *grads = pl.pallas_call(
        one_backward_kernel,
        out_shape=[shape(2 * SEQ, D, dtype=F32)] + ATTN_GRADS,
        in_specs=[SMEM] + vmem(11) + anyspace(15 + len(after)),
        out_specs=vmem(1) + anyspace(2),
        scratch_shapes=[pltpu.VMEM((16, D), F32), pltpu.VMEM((TOKENS, D), BF16)]
        + [pltpu.VMEM((2 * SEQ, D), BF16)] * 2
        + WEIGHT_SCRATCH
        + BACKWARD_SCRATCH,
        compiler_params=params(),
        cost_estimate=cost(13),
    )(index, tokens, pooled_low, normed_grad, vector_rows, *kept, *chunks, *after)
    return input_grad, grads


def local(inputs, lengths, cotangent, *weights):
    index = jnp.stack([*place_scalars(), lengths[0, 0], lengths[1, 0], jnp.zeros((), jnp.int32)])
    tokens = inputs.reshape(2 * SEQ, D)

    blob = prepare((weights[:5], weights[5:]))
    line = widen(index, [permute(blob, spread_pairs(k)) for k in range(4)])
    parts = [line] + [permute(line, line_pairs(-k)) for k in (1, 2, 3)]
    gather_one = Gather(widen_more(0, index, parts))
    chunk_two = widen_more(1, index, parts, (gather_one.near[0],))
    one = gather_one.finish()
    gather_two = Gather(chunk_two, one[2], one[9])
    middle, pooled_low, *kept = one_forward(index, tokens, one, (gather_two.own_swap,))
    kept = dict(zip(KEPT, kept))
    two = gather_two.finish(middle)

    (result, *back_two), grads, kept_two = two_forward(
        index, middle, cotangent.reshape(TOKENS, D), two
    )
    feed_two = permute(grads[0], SWAP), grads[1]
    upstream, grads = two_backward(index, middle, *back_two, kept_two, two)
    attn_two = permute(tie(grads[0], feed_two[0]), SWAP), grads[1]

    feed_two = add_halves(*feed_two, (upstream,))
    near_feed_two = send_near(feed_two)
    back_one, grads = one_feed(
        index, upstream, [kept[name] for name in FOR_FEED], one, (feed_two[0],)
    )
    feed_one = permute(tie(grads[0], *near_feed_two), SWAP), grads[1]
    attn_two = add_halves(*attn_two, (back_one[0], *near_feed_two))
    far_feed_two = send_far(feed_two, *near_feed_two, attn_two[0])
    near_attn_two = send_near(attn_two)
    input_grad, grads = one_backward(
        index,
        tokens,
        pooled_low,
        *back_one,
        [kept[name] for name in FOR_ATTENTION],
        one,
        (attn_two[0],),
    )
    attn_one = permute(tie(grads[0], *far_feed_two, *near_attn_two), SWAP), grads[1]
    feed_one = add_halves(*feed_one, (input_grad, *far_feed_two, *near_attn_two))
    far_attn_two = send_far(attn_two, *near_attn_two, feed_one[0])
    near_feed_one = send_near(feed_one, attn_one[0])
    attn_one = add_halves(*attn_one, (feed_one[0],))
    far_feed_one = send_far(feed_one, *near_feed_one)
    near_attn_one = send_near(attn_one, *near_feed_one, *far_attn_two)
    far_attn_one = send_far(attn_one, *near_attn_one, *far_feed_one)

    units = [received(attn_two, near_attn_two, far_attn_two)]
    units.append(received(feed_two, near_feed_two, far_feed_two))
    pieces = narrow(1, index, units)
    units = [received(attn_one, near_attn_one, far_attn_one)]
    units.append(received(feed_one, near_feed_one, far_feed_one))
    pieces = narrow(0, index, units, pieces)
    pieces = [pieces[0]] + [permute(pieces[k], line_pairs(k)) for k in (1, 2, 3)]
    pieces = narrow_more(index, pieces)
    grads = finish([permute(pieces[k], back(spread_pairs(k))) for k in range(4)])
    return (
        result.reshape(2, 1, HALF, D),
        input_grad.reshape(2, 1, SEQ, D),
        *grads,
    )


def solution(mesh):
    rows = P(None, AXES, None, None)
    shard = P(AXES, None)
    return jax.shard_map(
        local,
        mesh=mesh,
        in_specs=(rows, P(None, AXES), rows) + (shard,) * 10,
        out_specs=(rows, rows) + (shard,) * 10,
        check_vma=False,
    )
```

```python
import functools
import itertools

import jax
import jax.numpy as jnp
from jax import lax
from jax.experimental import pallas as pl
from jax.experimental.pallas import tpu as pltpu
from jax.sharding import PartitionSpec as P

AXES = ("dp", "shard")
F32, BF16 = jnp.float32, jnp.bfloat16
D, HEADS, HEAD_DIM, FF, BUCKETS = 768, 12, 64, 3072, 64
SEQ, HALF, TOKENS = 128, 64, 128
PAIRS = HEADS // 2
EPSILON = 1e-06
NEGATIVE = -1000000000.0
WRAP = 256

ROW = 6
CHUNK = 96
OUT_AT, VEC_AT, UP_AT, DOWN_AT, WIDTH = 2304, 3072, 3200, 6272, 9344
A_WIDTH, B_WIDTH = DOWN_AT, WIDTH - DOWN_AT
ATTN, FEED = UP_AT, WIDTH - UP_AT
FEED_LINE = 4096

VMEM_LIMIT = 56 * 1024 * 1024


def place(core, block, v2, v1):
    z = (block - v1) % 4
    x, y = (v1, v2) if core == 0 else (v2, v1)
    return ((x * 4 + y) * 4 + z) * 2 + core


def virtual(device):
    x, y, z, half = device // 32, device // 8 % 4, device // 2 % 4, device % 2
    if y % 2 == 0:
        return 0, x, y + half, z
    return 1, x % 2 + 2 * (y // 2), (x + half) % 4, z


def latin_squares():
    rows = list(itertools.permutations(range(4)))
    found = []
    for three in itertools.product(rows, repeat=3):
        if all(len({row[i] for row in three}) == 3 for i in range(4)):
            found.append((*three, tuple(6 - sum(row[i] for row in three) for i in range(4))))
    return found


CHOSEN = (37, 82, 157, 37, 214, 52, 174, 394, 384, 493, 432, 70, 186, 264, 256, 523, 141, 364, 399, 489, 205, 175, 408, 508, 390, 358, 335, 34, 286, 179, 230, 263)
SQUARES = [latin_squares()[number] for number in CHOSEN]


def square_of(core, block, v2):
    return SQUARES[16 * core + 4 * block + v2]


def spread_pairs(number):
    pairs = []
    for f in range(128):
        core, block, v2, j = virtual(f)
        v1 = square_of(core, block, v2)[j].index(number)
        pairs.append((f, place(core, block, v2, v1)))
    return pairs


def spread_sources():
    table = [None] * 128
    for v in range(128):
        core, block, v2, v1 = v // 64, v // 16 % 4, v // 4 % 4, v % 4
        column = [row[v1] for row in square_of(core, block, v2)]
        table[place(core, block, v2, v1)] = [column.index(number) for number in range(4)]
    return table


def line_pairs(step):
    pairs = []
    for v in range(128):
        core, block, v2, v1 = v // 64, v // 16 % 4, v // 4 % 4, v % 4
        pairs.append((place(core, block, v2, v1), place(core, block, (v2 + step) % 4, v1)))
    return pairs


def run_row(core, block, run):
    even = 192 * block + 96 * run
    odd = 192 * lax.rem(block, 2) + 384 * run + 48 + 96 * (block // 2)
    return pl.multiple_of(jnp.where(core == 0, even, odd), 16)


def along(axis_of_core, step):
    pairs = []
    for f in range(128):
        at = [f // 32, f // 8 % 4, f // 2 % 4]
        axis = axis_of_core[f % 2]
        at[axis] = (at[axis] + step) % 4
        pairs.append((f, ((at[0] * 4 + at[1]) * 4 + at[2]) * 2 + f % 2))
    return pairs


A_AXES, B_AXES = (0, 1), (2, 2)
SWAP = [(f, f ^ 1) for f in range(128)]


def permute(value, pairs):
    return lax.ppermute(value, AXES, pairs)


def back(pairs):
    return [(b, a) for a, b in pairs]


def place_scalars():
    x, inner = lax.axis_index("dp"), lax.axis_index("shard")
    y, z, core = inner // 8, inner // 2 % 4, inner % 2
    first = core == 0
    block = jnp.where(first, x + z, y + z) % 4
    other = jnp.where(first, y + z, x + z) % 4
    v2, v1 = jnp.where(first, y, x), jnp.where(first, x, y)
    return [core, block, other, v2, v1]


def mm(a, b):
    return lax.dot_general(a, b, (((1,), (0,)), ((), ())), preferred_element_type=F32)


def mm_nt(a, b):
    return lax.dot_general(a, b, (((1,), (1,)), ((), ())), preferred_element_type=F32)


def mm_tn(a, b):
    return lax.dot_general(a, b, (((0,), (0,)), ((), ())), preferred_element_type=F32)


def exact(a, b):
    return lax.dot_general(
        a, b, (((1,), (0,)), ((), ())), precision=lax.Precision.HIGHEST, preferred_element_type=F32
    )


def iota(shape, axis):
    return lax.broadcasted_iota(jnp.int32, shape, axis)


def onehot(condition):
    return condition.astype(F32).astype(BF16)


def split_hidden():
    source, out = iota((512, 512), 0), iota((512, 512), 1)
    return onehot((source // 4 == out % 128) & (source % 4 == out // 128))


def vmem(n):
    return [pl.BlockSpec(memory_space=pltpu.VMEM)] * n


def anyspace(n):
    return [pl.BlockSpec(memory_space=pl.ANY)] * n


SMEM = pl.BlockSpec(memory_space=pltpu.SMEM)


def params(limit=VMEM_LIMIT):
    return pltpu.CompilerParams(vmem_limit_bytes=limit)


def cost(microseconds):
    return pl.CostEstimate(flops=0, bytes_accessed=int(microseconds * 3.5e6), transcendentals=0)


def shape(*dims, dtype=BF16):
    return jax.ShapeDtypeStruct(dims, dtype)


def prepare_kernel(*refs):
    shards, out = refs[:10], refs[10]
    pad = onehot(iota((8, ROW), 0) == iota((8, ROW), 1))
    split = split_hidden()
    for layer in range(2):
        proj_in, proj_out, up, down, vectors = shards[5 * layer : 5 * layer + 5]
        at = WIDTH * layer
        out[:, at : at + OUT_AT] = mm(pad, proj_in[...]).astype(BF16)
        out[:, at + OUT_AT : at + VEC_AT] = mm(pad, proj_out[...]).astype(BF16)
        for group in range(6):
            part = mm(pad, up[:, 512 * group : 512 * group + 512]).astype(BF16)
            part = mm(part, split).astype(BF16)
            for c in range(4):
                lane = at + UP_AT + 768 * c + 128 * group
                out[:, lane : lane + 128] = part[:, 128 * c : 128 * c + 128]
        out[:, at + VEC_AT : at + UP_AT] = jnp.zeros((8, 128), BF16)
        out[:, at + VEC_AT : at + VEC_AT + 13] = mm(pad, vectors[...]).astype(BF16)
        for c in range(4):
            rows = onehot(iota((8, 24), 1) == 4 * iota((8, 24), 0) + c)
            lane = at + DOWN_AT + 768 * c
            out[:, lane : lane + 768] = mm(rows, down[...]).astype(BF16)


def prepare(shards):
    return pl.pallas_call(
        prepare_kernel,
        out_shape=shape(8, 2 * WIDTH),
        in_specs=vmem(10),
        out_specs=vmem(1)[0],
        compiler_params=params(),
        cost_estimate=cost(4),
    )(*shards[0], *shards[1])


def block_at(digit):
    wanted = iota((24, 8), 0) - ROW * digit
    source = iota((24, 8), 1)
    return onehot((wanted == source) & (source < ROW))


def widen_kernel(index, *refs):
    parts, out = refs[:4], refs[4]
    total = None
    for k in range(4):
        piece = mm(block_at(index[8 + k]), parts[k][...])
        total = piece if total is None else total + piece
    out[...] = total.astype(BF16)


def widen(index, parts):
    return pl.pallas_call(
        widen_kernel,
        out_shape=shape(24, 2 * WIDTH),
        in_specs=[SMEM] + vmem(4),
        out_specs=vmem(1)[0],
        compiler_params=params(),
        cost_estimate=cost(4),
    )(index, *parts)


def line_block(index, k):
    v2 = lax.rem(index[3] + k, 4)
    first = jnp.where(index[0] == 0, 0, lax.rem(index[1], 2))
    unit = lax.rem(v2 - first + 4, 4)
    row, source = iota((CHUNK, 24), 0), iota((CHUNK, 24), 1)
    here = (row // 48 == unit // 2) & (row % 12 // 6 == lax.rem(unit, 2))
    return onehot(here & (source == row % 48 // 12 * 6 + row % 6))


def widen_more_kernel(layer, index, *refs):
    parts, (out_a, out_b, both) = refs[:4], refs[-3:]
    places = [line_block(index, k) for k in range(4)]
    for out, start, width in ((out_a, 0, A_WIDTH), (out_b, A_WIDTH, B_WIDTH)):
        total = None
        for k in range(4):
            at = WIDTH * layer + start
            piece = mm(places[k], parts[k][:, at : at + width])
            total = piece if total is None else total + piece
        total = total.astype(BF16)
        out[...] = total
        both[:, start : start + width] = total


def widen_more(layer, index, parts, after=()):
    return pl.pallas_call(
        functools.partial(widen_more_kernel, layer),
        out_shape=[shape(CHUNK, A_WIDTH), shape(CHUNK, B_WIDTH), shape(CHUNK, WIDTH)],
        in_specs=[SMEM] + vmem(4) + anyspace(len(after)),
        out_specs=vmem(3),
        compiler_params=params(),
        cost_estimate=cost(5),
    )(index, *parts, *after)


def tie(value, *before):
    return lax.optimization_barrier((value, *before))[0]


class Gather:
    def __init__(self, chunk, *before):
        self.a, self.b, both = lax.optimization_barrier((*chunk, *before))[:3]
        self.own_swap = permute(both, SWAP)
        self.near = [permute(self.a, along(A_AXES, -k)) for k in (1, 3)]
        self.near += [permute(self.b, along(B_AXES, -k)) for k in (1, 3)]

    def finish(self, *before):
        far_a, far_b, *near = lax.optimization_barrier(
            (self.a, self.b, *self.near, self.own_swap, *before)
        )
        far = [permute(far_a, along(A_AXES, -2)), permute(far_b, along(B_AXES, -2))]
        swapped = [None, None, permute(near[2], SWAP), permute(near[3], SWAP)]
        for k in range(2):
            swapped[k] = permute(tie(near[k], swapped[k + 2]), SWAP)
        far_a, far_b, *_ = lax.optimization_barrier((*far, *swapped))
        far_swapped = [permute(far_a, SWAP), permute(far_b, SWAP)]
        return [
            *(self.a, self.near[0], far[0], self.near[1]),
            *(swapped[0], far_swapped[0], swapped[1]),
            *(self.b, self.near[2], far[1], self.near[3]),
            *(swapped[2], far_swapped[1], swapped[3]),
            self.own_swap,
        ]


def narrow_kernel(at, count, index, *refs):
    base, *got = refs[:count]
    *outs, stage, sems = refs[-6:]
    places = [line_block(index, k) for k in range(4)]
    width, line = base.shape[1], got[0].shape[1]
    for start, stop, pieces in ((0, line, got[:3]), (line, width, got[3:])):
        if start == stop:
            continue
        one, two, three = [wide(piece[...]) for piece in pieces]
        total = ((wide(base[:, start:stop]) + one) + (two + three)).astype(BF16)
        for k in range(4):
            stage[k, :, start:stop] = mm_tn(places[k], total).astype(BF16)
    copies = []
    for k in range(4):
        copies.append(
            pltpu.make_async_copy(stage.at[k], outs[k].at[:, pl.ds(at, width)], sems.at[k])
        )
        copies[k].start()
    for copy in copies:
        copy.wait()


def narrow(at, index, unit, onto=()):
    width, count = unit[0].shape[1], len(unit)
    return pl.pallas_call(
        functools.partial(narrow_kernel, at, count),
        out_shape=[shape(24, 2 * WIDTH)] * 4,
        in_specs=[SMEM] + vmem(count) + anyspace(len(onto)),
        out_specs=anyspace(4),
        scratch_shapes=[pltpu.VMEM((4, 24, width), BF16), pltpu.SemaphoreType.DMA((4,))],
        input_output_aliases={1 + count + k: k for k in range(len(onto))},
        compiler_params=params(),
        cost_estimate=cost(4),
    )(index, *unit, *onto)


def wide(value):
    return value.astype(F32)


def narrow_more_kernel(index, *refs):
    parts, outs = refs[:4], refs[4:]
    places = [block_at(index[8 + k]) for k in range(4)]
    split = split_hidden()
    for layer in range(2):
        at = WIDTH * layer
        one, two, three, four = [wide(part[:, at : at + WIDTH]) for part in parts]
        total = ((one + two) + (three + four)).astype(BF16)
        natural = []
        for group in range(6):
            lanes = [UP_AT + 768 * c + 128 * group for c in range(4)]
            part = jnp.concatenate([total[:, lane : lane + 128] for lane in lanes], 1)
            natural.append(mm_nt(part, split).astype(BF16))
        for k in range(4):
            outs[k][:, at : at + UP_AT] = mm_tn(places[k], total[:, :UP_AT]).astype(BF16)
            for group in range(6):
                lane = at + UP_AT + 512 * group
                outs[k][:, lane : lane + 512] = mm_tn(places[k], natural[group]).astype(BF16)
            outs[k][:, at + DOWN_AT : at + WIDTH] = mm_tn(places[k], total[:, DOWN_AT:]).astype(BF16)


def narrow_more(index, parts):
    return pl.pallas_call(
        narrow_more_kernel,
        out_shape=[shape(8, 2 * WIDTH)] * 4,
        in_specs=[SMEM] + vmem(4),
        out_specs=vmem(4),
        compiler_params=params(),
        cost_estimate=cost(6),
    )(index, *parts)


def finish_kernel(*refs):
    parts, outs = refs[:4], refs[4:]
    for layer in range(2):
        proj_in, proj_out, up, down, vectors = outs[5 * layer : 5 * layer + 5]

        def total(start, stop):
            at = WIDTH * layer
            one, two, three, four = [wide(part[:, at + start : at + stop]) for part in parts]
            return (one + two) + (three + four)

        proj_in[...] = total(0, OUT_AT)[:ROW]
        proj_out[...] = total(OUT_AT, VEC_AT)[:ROW]
        up[...] = total(UP_AT, DOWN_AT)[:ROW]
        vectors[...] = total(VEC_AT, UP_AT)[:ROW, :13]
        rows = None
        for c in range(4):
            place_rows = (iota((24, 8), 0) == 4 * iota((24, 8), 1) + c).astype(F32)
            lane = DOWN_AT + 768 * c
            piece = exact(place_rows, total(lane, lane + 768))
            rows = piece if rows is None else rows + piece
        down[...] = rows


def finish(parts):
    one = [shape(ROW, n, dtype=F32) for n in (2304, 768, 3072)]
    one += [shape(24, 768, dtype=F32), shape(ROW, 13, dtype=F32)]
    return pl.pallas_call(
        finish_kernel,
        out_shape=one + one,
        in_specs=vmem(4),
        out_specs=vmem(10),
        compiler_params=params(),
        cost_estimate=cost(4),
    )(*parts)


def send_sums(parts, axes, steps, *before):
    parts = [parts[k - 1] for k in steps]
    if before:
        parts = lax.optimization_barrier((*parts, *before))[: len(steps)]
    return [permute(part, along(axes, k)) for part, k in zip(parts, steps)]


def send_near(sums, *before):
    near = send_sums(sums[1:4], A_AXES, (1, 3), *before)
    return near + (send_sums(sums[4:7], B_AXES, (1, 3), *before) if len(sums) > 4 else [])


def send_far(sums, *before):
    far = send_sums(sums[1:4], A_AXES, (2,), *before)
    return far + (send_sums(sums[4:7], B_AXES, (2,), *before) if len(sums) > 4 else [])


def received(sums, near, far):
    got = [sums[0], near[0], near[1], far[0]]
    return got + [near[2], near[3], far[1]] if len(sums) > 4 else got


class Weights:
    def __init__(self, index, chunks, scratch, sems):
        self.w_in, self.w_out, self.w_up, self.w_down, self.vec = scratch
        own_a, other_a, own_b, other_b = chunks[:4], chunks[4:7], chunks[7:11], chunks[11:14]
        joined = chunks[14]
        other_a = [joined.at[:, :A_WIDTH], *other_a]
        other_b = [joined.at[:, A_WIDTH:WIDTH], *other_b]
        self.copies = [[] for _ in range(8)]
        for side in range(2):
            core = index[0] if side == 0 else 1 - index[0]
            first = index[1] if side == 0 else index[2]
            a_refs, b_refs = ((own_a, own_b), (other_a, other_b))[side]
            for k in range(4):
                block = lax.rem(first + k, 4)
                for run in range(2):
                    row = run_row(core, block, run)
                    rows = pl.ds(48 * run, 48)
                    a, b = a_refs[k], b_refs[k]
                    targets = [
                        (a, VEC_AT, 128, self.vec, row),
                        (a, 0, 2304, self.w_in, row),
                        (a, OUT_AT, 768, self.w_out, row),
                        (a, UP_AT, 3072, self.w_up, row),
                    ]
                    for c in range(4):
                        target = pl.multiple_of(768 * c + row, 16)
                        targets.append((b, 768 * c, 768, self.w_down, target))
                    for group, (ref, lane, width, out, at) in enumerate(targets):
                        self.copies[group].append(
                            (
                                ref.at[rows, pl.ds(lane, width)],
                                out.at[pl.ds(at, 48), :],
                                sems.at[group, 8 * side + 2 * k + run],
                            )
                        )

    def start(self, groups):
        for group in groups:
            self.copies[group] = [pltpu.make_async_copy(*copy) for copy in self.copies[group]]
            for copy in self.copies[group]:
                copy.start()

    def wait(self, *groups):
        for group in groups:
            for copy in self.copies[group]:
                copy.wait()


VEC, IN, OUT, UP, DOWN = 0, 1, 2, 3, 4
WEIGHT_SCRATCH = [
    pltpu.VMEM((768, 2304), BF16),
    pltpu.VMEM((768, 768), BF16),
    pltpu.VMEM((768, 3072), BF16),
    pltpu.VMEM((3072, 768), BF16),
    pltpu.VMEM((768, 128), BF16),
    pltpu.SemaphoreType.DMA((8, 16)),
]


def bucket_rows(sign=1):
    lane = iota((D, WRAP), 1)
    lane = lane if sign > 0 else lax.rem(WRAP - lane, WRAP)
    distance = jnp.where(lane < WRAP // 2, lane, lane - WRAP)
    bucket = jnp.clip(distance + BUCKETS // 2, 0, BUCKETS - 1)
    return lax.rem(iota((D, WRAP), 0), BUCKETS) == bucket


def head_mask():
    return iota((16, D), 1) // BUCKETS == iota((16, D), 0)


def position_bias(table, stride, keys, bias_ref):
    per_head = jnp.where(head_mask(), table, 0.0).astype(BF16)
    extended = mm(per_head, onehot(bucket_rows()))
    for head in range(HEADS):
        row = jnp.broadcast_to(extended[head : head + 1], (HALF, WRAP))
        rolled = pltpu.roll(row, 0, 1, stride=stride, stride_axis=0)
        bias_ref[head // 2, HALF * (head % 2) : HALF * (head % 2 + 1), :] = rolled[:, :keys]


def by_head(value):
    low = iota(value.shape, 1) < HEAD_DIM
    zero = jnp.zeros_like(value)
    return jnp.concatenate([jnp.where(low, value, zero), jnp.where(low, zero, value)], 0)


def join_heads(value):
    top, bottom = value[:HALF], value[HALF:]
    return jnp.where(iota(top.shape, 1) < HEAD_DIM, top, bottom)


def norm_forward(summed, gain, shift):
    centered = summed - jnp.mean(summed, -1, keepdims=True)
    inverse = lax.rsqrt(jnp.mean(centered * centered, -1, keepdims=True) + EPSILON)
    normal = centered * inverse
    return normal * gain + shift, normal, inverse


def norm_backward(upstream, normal, inverse, gain):
    scaled = upstream * gain
    bracket = (
        scaled
        - jnp.mean(scaled, -1, keepdims=True)
        - normal * jnp.mean(scaled * normal, -1, keepdims=True)
    )
    return inverse * bracket, rowsum(upstream * normal), rowsum(upstream)


def rowsum(value):
    return jnp.sum(value, 0, keepdims=True)


GELU_A, GELU_B = 0.7978845608028654, 0.044715


def gelu(x):
    return 0.5 * x * (1.0 + jnp.tanh(GELU_A * (x + GELU_B * (x * x * x))))


def gelu_slope(x):
    square = x * x
    t = jnp.tanh(GELU_A * (x + GELU_B * (square * x)))
    inner = GELU_A * (1.0 + 3.0 * GELU_B * square)
    return 0.5 * (1.0 + t) + 0.5 * x * (1.0 - t * t) * inner


KEPT = ("q", "k", "v", "prob", "context", "normal1", "inverse1", "low1", "pre", "hidden", "normal2", "inverse2")


def kept_shapes(keys):
    return {
        "q": ((TOKENS, D), BF16),
        "k": ((2 * keys, D), BF16),
        "v": ((2 * keys, D), BF16),
        "prob": ((2 * PAIRS, 128, keys), F32),
        "context": ((TOKENS, D), BF16),
        "normal1": ((TOKENS, D), F32),
        "inverse1": ((TOKENS, 128), F32),
        "low1": ((TOKENS, D), BF16),
        "pre": ((TOKENS, FF), F32),
        "hidden": ((TOKENS, FF), BF16),
        "normal2": ((TOKENS, D), F32),
        "inverse2": ((TOKENS, 128), F32),
    }


def transpose_vectors(w, vt):
    w.wait(VEC)
    vt[...] = jnp.transpose(w.vec[...].astype(F32))[:16]


def layer_forward(w, kept, vt, bias, x_query, x_key, source, valid, stride, keys):
    transpose_vectors(w, vt)
    position_bias(vt[12:13, :], stride, keys, bias)
    w.wait(IN)
    query_low = x_query[...]
    kept["q"][...] = (mm(query_low, w.w_in[:, :D]) + vt[0:1, :]).astype(BF16)
    key_low = x_key[...]
    kept["k"][...] = mm(key_low, w.w_in[:, D : 2 * D]).astype(BF16)
    kept["v"][...] = (mm(key_low, w.w_in[:, 2 * D :]) + vt[1:2, :]).astype(BF16)
    for row in range(2):
        usable = iota((128, keys), 1) < valid[row]
        for pair in range(PAIRS):
            lanes = slice(128 * pair, 128 * pair + 128)
            q = by_head(kept["q"][HALF * row : HALF * (row + 1), lanes])
            k = kept["k"][keys * row : keys * (row + 1), lanes]
            scores = mm_nt(q, k) * 0.125 + bias[pair]
            scores = jnp.where(usable, scores, NEGATIVE)
            unnormed = jnp.exp(scores - jnp.max(scores, -1, keepdims=True))
            prob = unnormed / jnp.sum(unnormed, -1, keepdims=True)
            kept["prob"][PAIRS * row + pair] = prob
            v = kept["v"][keys * row : keys * (row + 1), lanes]
            context = join_heads(mm(prob.astype(BF16), v))
            kept["context"][HALF * row : HALF * (row + 1), lanes] = context.astype(BF16)
    w.wait(OUT)
    attended = mm(kept["context"][...], w.w_out[...]) + vt[2:3, :]
    normed, normal, inverse = norm_forward(source + attended, vt[3:4, :], vt[4:5, :])
    kept["normal1"][...] = normal
    kept["inverse1"][...] = jnp.broadcast_to(inverse, (TOKENS, 128))
    normed_low = normed.astype(BF16)
    kept["low1"][...] = normed_low
    w.wait(UP)
    feed = normed + vt[5:6, :]
    for c in range(4):
        lanes = slice(D * c, D * (c + 1))
        pre = mm(normed_low, w.w_up[:, lanes]) + vt[8 + c : 9 + c, :]
        kept["pre"][:, lanes] = pre
        hidden = gelu(pre).astype(BF16)
        kept["hidden"][:, lanes] = hidden
        w.wait(DOWN + c)
        feed = feed + mm(hidden, w.w_down[lanes, :])
    result, normal, inverse = norm_forward(feed, vt[6:7, :], vt[7:8, :])
    kept["normal2"][...] = normal
    kept["inverse2"][...] = jnp.broadcast_to(inverse, (TOKENS, 128))
    return result


class GradientWriter:
    SLOTS = 3

    def __init__(self, stage, sems):
        self.stage, self.sems, self.flying, self.count = stage, sems, [()] * self.SLOTS, 0

    def write(self, value, line, across, lane):
        slot = self.count % self.SLOTS
        self.count += 1
        self.wait(slot)
        width, limit = value.shape[1], line[1].shape[1]
        self.stage[slot, :, :width] = value.astype(BF16)
        self.flying[slot] = []
        split = min(max(limit - lane, 0), width)
        for k in range(4):
            if k == 0 or split == width:
                parts = [(line[k], 0, width, lane)]
            else:
                parts = [(line[k], 0, split, lane), (across[k], split, width, lane + split - limit)]
            for number, (target, start, stop, at) in enumerate(parts):
                if start == stop:
                    continue
                copy = pltpu.make_async_copy(
                    self.stage.at[slot, pl.ds(CHUNK * k, CHUNK), pl.ds(start, stop - start)],
                    target.at[:, pl.ds(at, stop - start)],
                    self.sems.at[8 * slot + 2 * k + number],
                )
                copy.start()
                self.flying[slot].append(copy)

    def wait(self, slot):
        for copy in self.flying[slot]:
            copy.wait()
        self.flying[slot] = ()

    def finish(self):
        for slot in range(self.SLOTS):
            self.wait(slot)


def turned(index, value, plain, ordered):
    width = value.shape[0]
    plain[:, :width] = jnp.transpose(value)
    for k in range(4):
        for run in range(2):
            row = run_row(index[0], lax.rem(index[1] + k, 4), run)
            at = CHUNK * k + 48 * run
            ordered[at : at + 48, :width] = plain[pl.ds(row, 48), :width]
    return ordered[:, :width]


FEED_ACTS = 2 * D + 2 * FF
ACT_ROWS = TOKENS + 16
ACT_LANES = 4 * D


def feed_gradient_kernel(index, mine, theirs, *refs):
    refs = refs[-14:]
    base, a1, a2, a3, b1, b2, b3, acts, plain, ordered, stage, sems, act_sems = refs[:13]
    line, across = (base, a1, a2, a3), (base, b1, b2, b3)
    copies = []
    for side, ref in enumerate((mine, theirs)):
        target = acts.at[pl.ds(TOKENS * side, TOKENS), :]
        copies.append(pltpu.make_async_copy(ref, target, act_sems.at[side]))
        copies[side].start()
    for copy in copies:
        copy.wait()
    writer = GradientWriter(stage, sems)
    low1 = turned(index, acts[:, :D], plain.at[4], ordered.at[4])
    for c in range(4):
        at = 2 * D + FF + D * c
        writer.write(mm(low1, acts[:, at : at + D]), line, across, D * c)
    feed_grad = acts[:, D + FF : 2 * D + FF]
    for c in range(4):
        hidden = turned(index, acts[:, D + D * c : 2 * D + D * c], plain.at[c], ordered.at[c])
        writer.write(mm(hidden, feed_grad), line, across, FF + D * c)
    writer.finish()


GRADIENT_SCRATCH = [
    pltpu.VMEM((5, 768, 512), BF16),
    pltpu.VMEM((5, 384, 512), BF16),
    pltpu.VMEM((3, 384, 768), BF16),
    pltpu.SemaphoreType.DMA((24,)),
    pltpu.SemaphoreType.DMA((4,)),
]


def feed_gradient(index, mine, theirs, after=()):
    return pl.pallas_call(
        feed_gradient_kernel,
        out_shape=[shape(CHUNK, FEED)] + [shape(CHUNK, FEED_LINE)] * 3 + [shape(CHUNK, FEED - FEED_LINE)] * 3,
        in_specs=[SMEM] + anyspace(2 + len(after)),
        out_specs=anyspace(7),
        scratch_shapes=[pltpu.VMEM((2 * TOKENS, FEED_ACTS), BF16)] + GRADIENT_SCRATCH + [pltpu.VMEM((8, 128), F32)],
        compiler_params=params(),
        cost_estimate=cost(7),
    )(index, mine, theirs, *after)


def attention_gradient_kernel(keys, outs, index, mine, theirs, *refs):
    refs, scratch = refs[-10 - outs : -10], refs[-10:]
    queries, vectors, keyed, plain, ordered, stage, sems, act_sems, plain_vec, ordered_vec = scratch
    targets = refs[:4], (refs[0], *refs[4:])
    copies = []
    for side, ref in enumerate((mine, theirs)):
        for at, rows, target, sem in (
            (0, TOKENS, queries, act_sems.at[side]),
            (TOKENS, 16, vectors, act_sems.at[2 + side]),
            (ACT_ROWS, keys, keyed, sems.at[side]),
        ):
            lanes = target.shape[1]
            source = ref.at[pl.ds(at, rows), pl.ds(0, lanes)]
            copies.append(pltpu.make_async_copy(source, target.at[pl.ds(rows * side, rows), :], sem))
    for copy in copies:
        copy.start()
    for copy in copies:
        copy.wait()
    writer = GradientWriter(stage, sems)
    context = turned(index, queries[:, :D], plain.at[0], ordered.at[0])
    writer.write(mm(context, queries[:, D : 2 * D]), *targets, OUT_AT)
    query_rows = turned(index, queries[:, 2 * D : 3 * D], plain.at[1], ordered.at[1])
    writer.write(mm(query_rows, queries[:, 3 * D :]), *targets, 0)
    key_rows = turned(index, keyed[:, :D], plain.at[2], ordered.at[2])
    writer.write(mm(key_rows, keyed[:, D : 2 * D]), *targets, D)
    writer.write(mm(key_rows, keyed[:, 2 * D :]), *targets, 2 * D)
    rows = wide(vectors[:16, :]) + wide(vectors[16:, :])
    rows = jnp.concatenate([rows, jnp.zeros((112, D), F32)], 0)
    plain_vec[...] = jnp.transpose(rows)
    for k in range(4):
        for run in range(2):
            row = run_row(index[0], lax.rem(index[1] + k, 4), run)
            at = CHUNK * k + 48 * run
            ordered_vec[at : at + 48, :] = plain_vec[pl.ds(row, 48), :]
    writer.write(ordered_vec[...], *targets, VEC_AT)
    writer.finish()


def attention_gradient(index, mine, theirs, after=()):
    out = [shape(CHUNK, ATTN)] * 4
    keys = mine.shape[0] - ACT_ROWS
    scratch = [
        pltpu.VMEM((2 * TOKENS, ACT_LANES), BF16),
        pltpu.VMEM((32, D), BF16),
        pltpu.VMEM((2 * keys, 3 * D), BF16),
    ]
    vectors = [pltpu.VMEM((768, 128), F32), pltpu.VMEM((384, 128), F32)]
    return pl.pallas_call(
        functools.partial(attention_gradient_kernel, keys, len(out)),
        out_shape=out,
        in_specs=[SMEM] + anyspace(2 + len(after)),
        out_specs=anyspace(len(out)),
        scratch_shapes=scratch + GRADIENT_SCRATCH + vectors,
        compiler_params=params(),
        cost_estimate=cost(5),
    )(index, mine, theirs, *after)


def feed_backward(w, kept, vt, upstream, acts):
    dsum2, gain2, shift2 = norm_backward(
        upstream, kept["normal2"][...], kept["inverse2"][:, :1], vt[6:7, :]
    )
    feed_grad = dsum2.astype(BF16)
    acts[:, D + FF : 2 * D + FF] = feed_grad
    down_bias = rowsum(wide(feed_grad))
    normed_grad = dsum2
    hidden_bias = []
    for c in range(4):
        lanes = slice(D * c, D * (c + 1))
        w.wait(DOWN + c)
        hidden_grad = mm_nt(feed_grad, w.w_down[lanes, :])
        pre_grad = (gelu_slope(kept["pre"][:, lanes]) * hidden_grad).astype(BF16)
        at = 2 * D + FF + D * c
        acts[:, at : at + D] = pre_grad
        hidden_bias.append(rowsum(wide(pre_grad)))
        if c == 0:
            w.wait(UP)
        normed_grad = normed_grad + mm_nt(pre_grad, w.w_up[:, lanes])
    acts[:, :D] = kept["low1"][...]
    acts[:, D : D + FF] = kept["hidden"][...]
    zero = jnp.zeros((1, D), F32)
    rows = [zero] * 5 + [down_bias, gain2, shift2] + hidden_bias + [zero] * 4
    return normed_grad, jnp.concatenate(rows, 0)


def attention_backward(
    w, kept, vt, x_query, x_key, normed_grad, vector_rows, stride, keys, acts, work
):
    dq, dk, dv, table = work
    dsum1, gain1, shift1 = norm_backward(
        normed_grad, kept["normal1"][...], kept["inverse1"][:, :1], vt[3:4, :]
    )
    attended_grad = dsum1.astype(BF16)
    out_bias = rowsum(wide(attended_grad))
    acts[:TOKENS, :D] = kept["context"][...]
    acts[:TOKENS, D : 2 * D] = attended_grad
    acts[:TOKENS, 2 * D : 3 * D] = x_query[...]
    w.wait(OUT)
    context_grad = mm_nt(attended_grad, w.w_out[...]).astype(BF16)
    table[...] = jnp.zeros((16, WRAP), F32)
    mirror = (2 * keys, WRAP)
    mirror = onehot(lax.rem(lax.rem(iota(mirror, 0), keys) + iota(mirror, 1), WRAP) == 0)
    for pair in range(PAIRS):
        lanes = slice(128 * pair, 128 * pair + 128)
        pair_scores = []
        for row in range(2):
            here = slice(HALF * row, HALF * (row + 1))
            there = slice(keys * row, keys * (row + 1))
            grad = by_head(context_grad[here, lanes])
            prob = kept["prob"][PAIRS * row + pair]
            v = kept["v"][there, lanes]
            prob_grad = mm_nt(grad, v)
            dv[there, lanes] = mm_tn(prob.astype(BF16), grad).astype(BF16)
            score = prob * (prob_grad - jnp.sum(prob_grad * prob, -1, keepdims=True))
            score = score.astype(BF16)
            q = by_head(kept["q"][here, lanes])
            k = kept["k"][there, lanes]
            dq[here, lanes] = (0.125 * join_heads(mm(score, k))).astype(BF16)
            dk[there, lanes] = (0.125 * mm_tn(score, q)).astype(BF16)
            pair_scores.append(score)
        spread = mm(jnp.concatenate(pair_scores, 1), mirror)
        for half in range(2):
            rolled = pltpu.roll(
                spread[HALF * half : HALF * (half + 1)], 0, 1, stride=stride, stride_axis=0
            )
            table[2 * pair + half : 2 * pair + half + 1, :] = rowsum(rolled)
    dq_low, dk_low, dv_low = dq[...], dk[...], dv[...]
    w.wait(IN)
    source_grad = dsum1 + mm_nt(dq_low, w.w_in[:, :D])
    key_side = mm_nt(dk_low, w.w_in[:, D : 2 * D]) + mm_nt(dv_low, w.w_in[:, 2 * D :])
    acts[:TOKENS, 3 * D :] = dq_low
    acts[ACT_ROWS:, :D] = x_key[...]
    acts[ACT_ROWS:, D : 2 * D] = dk_low
    acts[ACT_ROWS:, 2 * D : 3 * D] = dv_low
    buckets = lax.dot_general(
        table[...],
        bucket_rows(-1).astype(F32),
        (((1,), (1,)), ((), ())),
        precision=lax.Precision.HIGHEST,
        preferred_element_type=F32,
    )
    table_grad = rowsum(jnp.where(head_mask(), buckets, 0.0))
    rows = [rowsum(wide(dq_low)), rowsum(wide(dv_low)), out_bias, gain1, shift1]
    rows += [vector_rows[5:12, :], table_grad, jnp.zeros((3, D), F32)]
    acts[TOKENS:ACT_ROWS, :D] = jnp.concatenate(rows, 0).astype(BF16)
    return source_grad, key_side


FOR_ATTENTION = ("q", "k", "v", "prob", "context", "normal1", "inverse1")
FOR_FEED = ("low1", "pre", "hidden", "normal2", "inverse2")


def pooling():
    return 0.5 * (iota((TOKENS, 2 * SEQ), 1) // 2 == iota((TOKENS, 2 * SEQ), 0)).astype(F32)


def one_forward_kernel(index, tokens, *refs):
    chunks = refs[:15]
    middle, pooled_low, *refs = refs[-22:]
    kept = dict(zip(KEPT, refs[:12]))
    vt, bias, *scratch = refs[12:]
    w = Weights(index, chunks, scratch[:5], scratch[5])
    w.start(range(8))
    pooled = mm(pooling().astype(BF16), tokens[...])
    pooled_low[...] = pooled.astype(BF16)
    valid = [index[5], index[6]]
    middle[...] = layer_forward(w, kept, vt, bias, pooled_low, tokens, pooled, valid, 2, SEQ)


def one_forward(index, tokens, chunks, after):
    kept = [shape(*dims, dtype=dtype) for dims, dtype in kept_shapes(SEQ).values()]
    return pl.pallas_call(
        one_forward_kernel,
        out_shape=[shape(TOKENS, D, dtype=F32), shape(TOKENS, D)] + kept,
        in_specs=[SMEM] + vmem(1) + anyspace(15 + len(after)),
        out_specs=vmem(14),
        scratch_shapes=[pltpu.VMEM((16, D), F32), pltpu.VMEM((PAIRS, 128, SEQ), F32)] + WEIGHT_SCRATCH,
        compiler_params=params(),
        cost_estimate=cost(13),
    )(index, tokens, *chunks, *after)


def two_forward_kernel(index, middle, cotangent, *refs):
    chunks, refs = refs[:15], refs[15:]
    result, normed_grad, vector_rows, acts = refs[:4]
    kept = dict(zip(FOR_ATTENTION + FOR_FEED, refs[4:16]))
    vt, bias, middle_low, *scratch = refs[16:]
    w = Weights(index, chunks, scratch[:5], scratch[5])
    w.start(range(8))
    middle_low[...] = middle[...].astype(BF16)
    valid = [(index[5] + 1) // 2, (index[6] + 1) // 2]
    out = layer_forward(w, kept, vt, bias, middle_low, middle_low, middle[...], valid, 1, HALF)
    result[...] = out.astype(BF16)
    w.wait = lambda *groups: None
    normed_grad[...], vector_rows[...] = feed_backward(w, kept, vt, cotangent[...], acts)


def two_forward(index, middle, cotangent, chunks):
    dims = kept_shapes(HALF)
    kept = [shape(*dims[name][0], dtype=dims[name][1]) for name in FOR_ATTENTION]
    scratch = [pltpu.VMEM(*dims[name]) for name in FOR_FEED]
    out = [shape(TOKENS, D), shape(TOKENS, D, dtype=F32), shape(16, D, dtype=F32)]
    outs = pl.pallas_call(
        two_forward_kernel,
        out_shape=out + [shape(TOKENS, FEED_ACTS)] + kept,
        in_specs=[SMEM] + vmem(2) + anyspace(15),
        out_specs=vmem(11),
        scratch_shapes=scratch
        + [pltpu.VMEM((16, D), F32), pltpu.VMEM((PAIRS, 128, HALF), F32), pltpu.VMEM((TOKENS, D), BF16)]
        + WEIGHT_SCRATCH,
        compiler_params=params(),
        cost_estimate=cost(17),
    )(index, middle, cotangent, *chunks)
    return outs[:3], outs[3], outs[4:]


def two_backward_kernel(index, middle, normed_grad, vector_rows, *refs):
    kept = dict(zip(FOR_ATTENTION, refs[:7]))
    chunks, refs = refs[7:22], refs[22:]
    upstream, acts, vt, middle_low, *work = refs[:8]
    scratch = refs[8:]
    w = Weights(index, chunks, scratch[:5], scratch[5])
    w.start((VEC, OUT, IN))
    middle_low[...] = middle[...].astype(BF16)
    transpose_vectors(w, vt)
    source_grad, key_side = attention_backward(
        w, kept, vt, middle_low, middle_low, normed_grad[...], vector_rows, 1, HALF, acts, work
    )
    upstream[...] = source_grad + key_side


def two_backward(index, middle, normed_grad, vector_rows, kept, chunks):
    return pl.pallas_call(
        two_backward_kernel,
        out_shape=[shape(TOKENS, D, dtype=F32), shape(ACT_ROWS + TOKENS, ACT_LANES)],
        in_specs=[SMEM] + vmem(10) + anyspace(15),
        out_specs=vmem(2),
        scratch_shapes=[pltpu.VMEM((16, D), F32)]
        + [pltpu.VMEM((TOKENS, D), BF16)] * 4
        + [pltpu.VMEM((16, WRAP), F32)]
        + WEIGHT_SCRATCH,
        compiler_params=params(),
        cost_estimate=cost(10),
    )(index, middle, normed_grad, vector_rows, *kept, *chunks)


def one_feed_kernel(index, upstream, *refs):
    kept = dict(zip(FOR_FEED, refs[:5]))
    chunks = refs[5:20]
    normed_grad, vector_rows, acts, vt, *scratch = refs[-10:]
    w = Weights(index, chunks, scratch[:5], scratch[5])
    w.start((VEC, DOWN, DOWN + 1, DOWN + 2, DOWN + 3, UP))
    transpose_vectors(w, vt)
    normed_grad[...], vector_rows[...] = feed_backward(w, kept, vt, upstream[...], acts)


def one_feed(index, upstream, kept, chunks, after):
    normed_grad, vector_rows, acts = pl.pallas_call(
        one_feed_kernel,
        out_shape=[shape(TOKENS, D, dtype=F32), shape(16, D, dtype=F32), shape(TOKENS, FEED_ACTS)],
        in_specs=[SMEM] + vmem(6) + anyspace(15 + len(after)),
        out_specs=vmem(3),
        scratch_shapes=[pltpu.VMEM((16, D), F32)] + WEIGHT_SCRATCH,
        compiler_params=params(),
        cost_estimate=cost(9),
    )(index, upstream, *kept, *chunks, *after)
    return (normed_grad, vector_rows), acts


def one_backward_kernel(index, tokens, pooled_low, normed_grad, vector_rows, *refs):
    kept = dict(zip(FOR_ATTENTION, refs[:7]))
    chunks = refs[7:22]
    input_grad, acts, vt, *refs = refs[-13:]
    work, scratch = refs[:4], refs[4:]
    w = Weights(index, chunks, scratch[:5], scratch[5])
    w.start((VEC, OUT, IN))
    transpose_vectors(w, vt)
    source_grad, key_side = attention_backward(
        w, kept, vt, pooled_low, tokens, normed_grad[...], vector_rows, 2, SEQ, acts, work
    )
    repeated = lax.dot_general(
        pooling(),
        source_grad,
        (((0,), (0,)), ((), ())),
        precision=lax.Precision.HIGHEST,
        preferred_element_type=F32,
    )
    input_grad[...] = key_side + repeated


def one_backward(index, tokens, pooled_low, normed_grad, vector_rows, kept, chunks, after):
    return pl.pallas_call(
        one_backward_kernel,
        out_shape=[shape(2 * SEQ, D, dtype=F32), shape(ACT_ROWS + 2 * SEQ, ACT_LANES)],
        in_specs=[SMEM] + vmem(11) + anyspace(15 + len(after)),
        out_specs=vmem(2),
        scratch_shapes=[pltpu.VMEM((16, D), F32), pltpu.VMEM((TOKENS, D), BF16)]
        + [pltpu.VMEM((2 * SEQ, D), BF16)] * 2
        + [pltpu.VMEM((16, WRAP), F32)]
        + WEIGHT_SCRATCH,
        compiler_params=params(),
        cost_estimate=cost(13),
    )(index, tokens, pooled_low, normed_grad, vector_rows, *kept, *chunks, *after)


def local(inputs, lengths, cotangent, *weights):
    device = lax.axis_index("dp") * 32 + lax.axis_index("shard")
    sources = lax.dynamic_index_in_dim(jnp.array(spread_sources(), jnp.int32), device, 0, False)
    scalars = [*place_scalars(), lengths[0, 0], lengths[1, 0], jnp.zeros((), jnp.int32)]
    index = jnp.concatenate([jnp.stack(scalars), sources])
    tokens = inputs.reshape(2 * SEQ, D)

    blob = prepare((weights[:5], weights[5:]))
    line = widen(index, [permute(blob, spread_pairs(k)) for k in range(4)])
    parts = [line] + [permute(line, line_pairs(-k)) for k in (1, 2, 3)]
    gather_one = Gather(widen_more(0, index, parts))
    chunk_two = widen_more(1, index, parts, (gather_one.near[0],))
    one = gather_one.finish()
    gather_two = Gather(chunk_two, one[2], one[9])
    middle, pooled_low, *kept = one_forward(index, tokens, one, (gather_two.own_swap,))
    kept = dict(zip(KEPT, kept))
    two = gather_two.finish(middle)

    (result, *back_two), acts_feed, kept_two = two_forward(
        index, middle, cotangent.reshape(TOKENS, D), two
    )
    acts_feed = acts_feed, permute(acts_feed, SWAP)
    upstream, acts_attn = two_backward(index, middle, *back_two, kept_two, two)
    acts_attn = acts_attn, permute(tie(acts_attn, acts_feed[1]), SWAP)

    feed_two = feed_gradient(index, *acts_feed, (upstream,))
    near_feed_two = send_near(feed_two)
    back_one, acts_feed = one_feed(
        index, upstream, [kept[name] for name in FOR_FEED], one, (feed_two[0],)
    )
    acts_feed = acts_feed, permute(tie(acts_feed, *near_feed_two), SWAP)
    attn_two = attention_gradient(index, *acts_attn, (back_one[0], *near_feed_two))
    far_feed_two = send_far(feed_two, *near_feed_two, attn_two[0])
    near_attn_two = send_near(attn_two)
    feed_one = feed_gradient(index, *acts_feed, (attn_two[0],))
    sent = (*far_feed_two, *near_attn_two, feed_one[0])
    far_attn_two = send_far(attn_two, *sent)
    near_feed_one = send_near(feed_one, *sent)
    input_grad, acts_attn = one_backward(
        index,
        tokens,
        pooled_low,
        *back_one,
        [kept[name] for name in FOR_ATTENTION],
        one,
        sent,
    )
    acts_attn = acts_attn, permute(tie(acts_attn, *near_feed_one, *far_attn_two), SWAP)
    far_feed_one = send_far(feed_one, *near_feed_one, *far_attn_two)
    pieces = narrow(WIDTH + ATTN, index, received(feed_two, near_feed_two, far_feed_two))
    attn_one = attention_gradient(index, *acts_attn, (pieces[0],))
    near_attn_one = send_near(attn_one, *far_feed_one)
    far_attn_one = send_far(attn_one, *far_feed_one)

    pieces = narrow(WIDTH, index, received(attn_two, near_attn_two, far_attn_two), pieces)
    pieces = narrow(ATTN, index, received(feed_one, near_feed_one, far_feed_one), pieces)
    pieces = narrow(0, index, received(attn_one, near_attn_one, far_attn_one), pieces)
    pieces = [pieces[0]] + [permute(pieces[k], line_pairs(k)) for k in (1, 2, 3)]
    pieces = narrow_more(index, pieces)
    grads = finish([permute(pieces[k], back(spread_pairs(k))) for k in range(4)])
    return (
        result.reshape(2, 1, HALF, D),
        input_grad.reshape(2, 1, SEQ, D),
        *grads,
    )


def solution(mesh):
    rows = P(None, AXES, None, None)
    shard = P(AXES, None)
    return jax.shard_map(
        local,
        mesh=mesh,
        in_specs=(rows, P(None, AXES), rows) + (shard,) * 10,
        out_specs=(rows, rows) + (shard,) * 10,
        check_vma=False,
    )
```

```python
import functools
import itertools

import jax
import jax.numpy as jnp
from jax import lax
from jax.experimental import pallas as pl
from jax.experimental.pallas import tpu as pltpu
from jax.sharding import PartitionSpec as P

AXES = ("dp", "shard")
F32, BF16 = jnp.float32, jnp.bfloat16
D, HEADS, HEAD_DIM, FF, BUCKETS = 768, 12, 64, 3072, 64
SEQ, HALF, TOKENS = 128, 64, 128
PAIRS = HEADS // 2
EPSILON = 1e-06
NEGATIVE = -1000000000.0
WRAP = 256

ROW = 6
CHUNK = 96
OUT_AT, VEC_AT, UP_AT, DOWN_AT, WIDTH = 2304, 3072, 3200, 6272, 9344
A_WIDTH, B_WIDTH = DOWN_AT, WIDTH - DOWN_AT
ATTN, FEED = UP_AT, WIDTH - UP_AT
FEED_LINE = 4096


def place(core, block, v2, v1):
    z = (block - v1) % 4
    x, y = (v1, v2) if core == 0 else (v2, v1)
    return ((x * 4 + y) * 4 + z) * 2 + core


def virtual(device):
    x, y, z, half = device // 32, device // 8 % 4, device // 2 % 4, device % 2
    if y % 2 == 0:
        return 0, x, y + half, z
    return 1, x % 2 + 2 * (y // 2), (x + half) % 4, z


def latin_squares():
    rows = list(itertools.permutations(range(4)))
    found = []
    for three in itertools.product(rows, repeat=3):
        if all(len({row[i] for row in three}) == 3 for i in range(4)):
            found.append((*three, tuple(6 - sum(row[i] for row in three) for i in range(4))))
    return found


CHOSEN = (37, 82, 157, 37, 214, 52, 174, 394, 384, 493, 432, 70, 186, 264, 256, 523, 141, 364, 399, 489, 205, 175, 408, 508, 390, 358, 335, 34, 286, 179, 230, 263)
SQUARES = [latin_squares()[number] for number in CHOSEN]


def square_of(core, block, v2):
    return SQUARES[16 * core + 4 * block + v2]


def spread_pairs(number):
    pairs = []
    for f in range(128):
        core, block, v2, j = virtual(f)
        v1 = square_of(core, block, v2)[j].index(number)
        pairs.append((f, place(core, block, v2, v1)))
    return pairs


def spread_sources():
    table = [None] * 128
    for v in range(128):
        core, block, v2, v1 = v // 64, v // 16 % 4, v // 4 % 4, v % 4
        column = [row[v1] for row in square_of(core, block, v2)]
        table[place(core, block, v2, v1)] = [column.index(number) for number in range(4)]
    return table


def line_pairs(step):
    pairs = []
    for v in range(128):
        core, block, v2, v1 = v // 64, v // 16 % 4, v // 4 % 4, v % 4
        pairs.append((place(core, block, v2, v1), place(core, block, (v2 + step) % 4, v1)))
    return pairs


def run_row(core, block, run):
    even = 192 * block + 96 * run
    odd = 192 * lax.rem(block, 2) + 384 * run + 48 + 96 * (block // 2)
    return pl.multiple_of(jnp.where(core == 0, even, odd), 16)


def along(axis_of_core, step):
    pairs = []
    for f in range(128):
        at = [f // 32, f // 8 % 4, f // 2 % 4]
        axis = axis_of_core[f % 2]
        at[axis] = (at[axis] + step) % 4
        pairs.append((f, ((at[0] * 4 + at[1]) * 4 + at[2]) * 2 + f % 2))
    return pairs


A_AXES, B_AXES = (0, 1), (2, 2)
SWAP = [(f, f ^ 1) for f in range(128)]


def permute(value, pairs):
    return lax.ppermute(value, AXES, pairs)


def back(pairs):
    return [(b, a) for a, b in pairs]


def place_scalars():
    x, inner = lax.axis_index("dp"), lax.axis_index("shard")
    y, z, core = inner // 8, inner // 2 % 4, inner % 2
    first = core == 0
    block = jnp.where(first, x + z, y + z) % 4
    other = jnp.where(first, y + z, x + z) % 4
    v2, v1 = jnp.where(first, y, x), jnp.where(first, x, y)
    return [core, block, other, v2, v1]


def mm(a, b):
    return lax.dot_general(a, b, (((1,), (0,)), ((), ())), preferred_element_type=F32)


def mm_nt(a, b):
    return lax.dot_general(a, b, (((1,), (1,)), ((), ())), preferred_element_type=F32)


def mm_tn(a, b):
    return lax.dot_general(a, b, (((0,), (0,)), ((), ())), preferred_element_type=F32)


def exact(a, b):
    return lax.dot_general(
        a, b, (((1,), (0,)), ((), ())), precision=lax.Precision.HIGHEST, preferred_element_type=F32
    )


def iota(shape, axis):
    return lax.broadcasted_iota(jnp.int32, shape, axis)


def onehot(condition):
    return condition.astype(F32).astype(BF16)


def split_hidden():
    source, out = iota((512, 512), 0), iota((512, 512), 1)
    return onehot((source // 4 == out % 128) & (source % 4 == out // 128))


def vmem(n):
    return [pl.BlockSpec(memory_space=pltpu.VMEM)] * n


def anyspace(n):
    return [pl.BlockSpec(memory_space=pl.ANY)] * n


SMEM = pl.BlockSpec(memory_space=pltpu.SMEM)


def params(mebibytes=56):
    return pltpu.CompilerParams(vmem_limit_bytes=mebibytes * 1024 * 1024)


def cost(microseconds):
    return pl.CostEstimate(flops=0, bytes_accessed=int(microseconds * 3.5e6), transcendentals=0)


def shape(*dims, dtype=BF16):
    return jax.ShapeDtypeStruct(dims, dtype)


def prepare_kernel(*refs):
    shards, out = refs[:10], refs[10]
    pad = onehot(iota((8, ROW), 0) == iota((8, ROW), 1))
    split = split_hidden()
    for layer in range(2):
        proj_in, proj_out, up, down, vectors = shards[5 * layer : 5 * layer + 5]
        at = WIDTH * layer
        out[:, at : at + OUT_AT] = mm(pad, proj_in[...]).astype(BF16)
        out[:, at + OUT_AT : at + VEC_AT] = mm(pad, proj_out[...]).astype(BF16)
        for group in range(6):
            part = mm(pad, up[:, 512 * group : 512 * group + 512]).astype(BF16)
            part = mm(part, split).astype(BF16)
            for c in range(4):
                lane = at + UP_AT + 768 * c + 128 * group
                out[:, lane : lane + 128] = part[:, 128 * c : 128 * c + 128]
        out[:, at + VEC_AT : at + UP_AT] = jnp.zeros((8, 128), BF16)
        out[:, at + VEC_AT : at + VEC_AT + 13] = mm(pad, vectors[...]).astype(BF16)
        for c in range(4):
            rows = onehot(iota((8, 24), 1) == 4 * iota((8, 24), 0) + c)
            lane = at + DOWN_AT + 768 * c
            out[:, lane : lane + 768] = mm(rows, down[...]).astype(BF16)


def prepare(shards):
    return pl.pallas_call(
        prepare_kernel,
        out_shape=shape(8, 2 * WIDTH),
        in_specs=vmem(10),
        out_specs=vmem(1)[0],
        compiler_params=params(),
        cost_estimate=cost(4),
    )(*shards[0], *shards[1])


def block_at(digit):
    wanted = iota((24, 8), 0) - ROW * digit
    source = iota((24, 8), 1)
    return onehot((wanted == source) & (source < ROW))


def widen_kernel(index, *refs):
    parts, out = refs[:4], refs[4]
    total = None
    for k in range(4):
        piece = mm(block_at(index[8 + k]), parts[k][...])
        total = piece if total is None else total + piece
    out[...] = total.astype(BF16)


def widen(index, parts):
    return pl.pallas_call(
        widen_kernel,
        out_shape=shape(24, 2 * WIDTH),
        in_specs=[SMEM] + vmem(4),
        out_specs=vmem(1)[0],
        compiler_params=params(24),
        cost_estimate=cost(4),
    )(index, *parts)


def line_block(index, k):
    v2 = lax.rem(index[3] + k, 4)
    first = jnp.where(index[0] == 0, 0, lax.rem(index[1], 2))
    unit = lax.rem(v2 - first + 4, 4)
    row, source = iota((CHUNK, 24), 0), iota((CHUNK, 24), 1)
    here = (row // 48 == unit // 2) & (row % 12 // 6 == lax.rem(unit, 2))
    return onehot(here & (source == row % 48 // 12 * 6 + row % 6))


def widen_more_kernel(layer, index, *refs):
    parts, (out_a, out_b, both) = refs[:4], refs[-3:]
    places = [line_block(index, k) for k in range(4)]
    for out, start, width in ((out_a, 0, A_WIDTH), (out_b, A_WIDTH, B_WIDTH)):
        total = None
        for k in range(4):
            at = WIDTH * layer + start
            piece = mm(places[k], parts[k][:, at : at + width])
            total = piece if total is None else total + piece
        total = total.astype(BF16)
        out[...] = total
        both[:, start : start + width] = total


def widen_more(layer, index, parts, after=()):
    return pl.pallas_call(
        functools.partial(widen_more_kernel, layer),
        out_shape=[shape(CHUNK, A_WIDTH), shape(CHUNK, B_WIDTH), shape(CHUNK, WIDTH)],
        in_specs=[SMEM] + vmem(4) + anyspace(len(after)),
        out_specs=vmem(3),
        compiler_params=params(24),
        cost_estimate=cost(5),
    )(index, *parts, *after)


def tie(value, *before):
    return lax.optimization_barrier((value, *before))[0]


class Gather:
    def __init__(self, chunk, *before):
        self.a, self.b, both = lax.optimization_barrier((*chunk, *before))[:3]
        self.own_swap = permute(both, SWAP)
        self.near = [permute(self.a, along(A_AXES, -k)) for k in (1, 3)]
        self.near += [permute(self.b, along(B_AXES, -k)) for k in (1, 3)]

    def finish(self, *before):
        far_a, far_b, *near = lax.optimization_barrier(
            (self.a, self.b, *self.near, self.own_swap, *before)
        )
        far = [permute(far_a, along(A_AXES, -2)), permute(far_b, along(B_AXES, -2))]
        swapped = [None, None, permute(near[2], SWAP), permute(near[3], SWAP)]
        for k in range(2):
            swapped[k] = permute(tie(near[k], swapped[k + 2]), SWAP)
        far_a, far_b, *_ = lax.optimization_barrier((*far, *swapped))
        far_swapped = [permute(far_a, SWAP), permute(far_b, SWAP)]
        return [
            *(self.a, self.near[0], far[0], self.near[1]),
            *(swapped[0], far_swapped[0], swapped[1]),
            *(self.b, self.near[2], far[1], self.near[3]),
            *(swapped[2], far_swapped[1], swapped[3]),
            self.own_swap,
        ]


def narrow_kernel(at, count, index, *refs):
    base, *got = refs[:count]
    *outs, stage, sems = refs[-6:]
    places = [line_block(index, k) for k in range(4)]
    width, line = base.shape[1], got[0].shape[1]
    for start, stop, pieces in ((0, line, got[:3]), (line, width, got[3:])):
        if start == stop:
            continue
        one, two, three = [wide(piece[...]) for piece in pieces]
        total = ((wide(base[:, start:stop]) + one) + (two + three)).astype(BF16)
        for k in range(4):
            stage[k, :, start:stop] = mm_tn(places[k], total).astype(BF16)
    copies = []
    for k in range(4):
        copies.append(
            pltpu.make_async_copy(stage.at[k], outs[k].at[:, pl.ds(at, width)], sems.at[k])
        )
        copies[k].start()
    for copy in copies:
        copy.wait()


def narrow(at, index, unit, onto=()):
    width, count = unit[0].shape[1], len(unit)
    return pl.pallas_call(
        functools.partial(narrow_kernel, at, count),
        out_shape=[shape(24, 2 * WIDTH)] * 4,
        in_specs=[SMEM] + vmem(count) + anyspace(len(onto)),
        out_specs=anyspace(4),
        scratch_shapes=[pltpu.VMEM((4, 24, width), BF16), pltpu.SemaphoreType.DMA((4,))],
        input_output_aliases={1 + count + k: k for k in range(len(onto))},
        compiler_params=params(24),
        cost_estimate=cost(4),
    )(index, *unit, *onto)


def wide(value):
    return value.astype(F32)


def narrow_more_kernel(index, *refs):
    parts, outs = refs[:4], refs[4:]
    places = [block_at(index[8 + k]) for k in range(4)]
    split = split_hidden()
    for layer in range(2):
        at = WIDTH * layer
        one, two, three, four = [wide(part[:, at : at + WIDTH]) for part in parts]
        total = ((one + two) + (three + four)).astype(BF16)
        natural = []
        for group in range(6):
            lanes = [UP_AT + 768 * c + 128 * group for c in range(4)]
            part = jnp.concatenate([total[:, lane : lane + 128] for lane in lanes], 1)
            natural.append(mm_nt(part, split).astype(BF16))
        for k in range(4):
            outs[k][:, at : at + UP_AT] = mm_tn(places[k], total[:, :UP_AT]).astype(BF16)
            for group in range(6):
                lane = at + UP_AT + 512 * group
                outs[k][:, lane : lane + 512] = mm_tn(places[k], natural[group]).astype(BF16)
            outs[k][:, at + DOWN_AT : at + WIDTH] = mm_tn(places[k], total[:, DOWN_AT:]).astype(BF16)


def narrow_more(index, parts):
    return pl.pallas_call(
        narrow_more_kernel,
        out_shape=[shape(8, 2 * WIDTH)] * 4,
        in_specs=[SMEM] + vmem(4),
        out_specs=vmem(4),
        compiler_params=params(24),
        cost_estimate=cost(6),
    )(index, *parts)


def finish_kernel(*refs):
    parts, outs = refs[:4], refs[4:]
    for layer in range(2):
        proj_in, proj_out, up, down, vectors = outs[5 * layer : 5 * layer + 5]

        def total(start, stop):
            at = WIDTH * layer
            one, two, three, four = [wide(part[:, at + start : at + stop]) for part in parts]
            return (one + two) + (three + four)

        proj_in[...] = total(0, OUT_AT)[:ROW]
        proj_out[...] = total(OUT_AT, VEC_AT)[:ROW]
        up[...] = total(UP_AT, DOWN_AT)[:ROW]
        vectors[...] = total(VEC_AT, UP_AT)[:ROW, :13]
        rows = None
        for c in range(4):
            place_rows = (iota((24, 8), 0) == 4 * iota((24, 8), 1) + c).astype(F32)
            lane = DOWN_AT + 768 * c
            piece = exact(place_rows, total(lane, lane + 768))
            rows = piece if rows is None else rows + piece
        down[...] = rows


def finish(parts):
    one = [shape(ROW, n, dtype=F32) for n in (2304, 768, 3072)]
    one += [shape(24, 768, dtype=F32), shape(ROW, 13, dtype=F32)]
    return pl.pallas_call(
        finish_kernel,
        out_shape=one + one,
        in_specs=vmem(4),
        out_specs=vmem(10),
        compiler_params=params(24),
        cost_estimate=cost(4),
    )(*parts)


def send_sums(parts, axes, steps, *before):
    parts = [parts[k - 1] for k in steps]
    if before:
        parts = lax.optimization_barrier((*parts, *before))[: len(steps)]
    return [permute(part, along(axes, k)) for part, k in zip(parts, steps)]


def send_near(sums, *before):
    near = send_sums(sums[1:4], A_AXES, (1, 3), *before)
    return near + (send_sums(sums[4:7], B_AXES, (1, 3), *before) if len(sums) > 4 else [])


def send_far(sums, *before):
    far = send_sums(sums[1:4], A_AXES, (2,), *before)
    return far + (send_sums(sums[4:7], B_AXES, (2,), *before) if len(sums) > 4 else [])


def received(sums, near, far):
    got = [sums[0], near[0], near[1], far[0]]
    return got + [near[2], near[3], far[1]] if len(sums) > 4 else got


class Weights:
    def __init__(self, index, chunks, scratch, sems):
        self.w_in, self.w_out, self.w_up, self.w_down, self.vec = scratch
        own_a, other_a, own_b, other_b = chunks[:4], chunks[4:7], chunks[7:11], chunks[11:14]
        joined = chunks[14]
        other_a = [joined.at[:, :A_WIDTH], *other_a]
        other_b = [joined.at[:, A_WIDTH:WIDTH], *other_b]
        self.copies = [[] for _ in range(8)]
        for side in range(2):
            core = index[0] if side == 0 else 1 - index[0]
            first = index[1] if side == 0 else index[2]
            a_refs, b_refs = ((own_a, own_b), (other_a, other_b))[side]
            for k in range(4):
                block = lax.rem(first + k, 4)
                for run in range(2):
                    row = run_row(core, block, run)
                    rows = pl.ds(48 * run, 48)
                    a, b = a_refs[k], b_refs[k]
                    targets = [
                        (a, VEC_AT, 128, self.vec, row),
                        (a, 0, 2304, self.w_in, row),
                        (a, OUT_AT, 768, self.w_out, row),
                        (a, UP_AT, 3072, self.w_up, row),
                    ]
                    for c in range(4):
                        target = pl.multiple_of(768 * c + row, 16)
                        targets.append((b, 768 * c, 768, self.w_down, target))
                    for group, (ref, lane, width, out, at) in enumerate(targets):
                        self.copies[group].append(
                            (
                                ref.at[rows, pl.ds(lane, width)],
                                out.at[pl.ds(at, 48), :],
                                sems.at[group, 8 * side + 2 * k + run],
                            )
                        )

    def start(self, groups):
        for group in groups:
            self.copies[group] = [pltpu.make_async_copy(*copy) for copy in self.copies[group]]
            for copy in self.copies[group]:
                copy.start()

    def wait(self, *groups):
        for group in groups:
            for copy in self.copies[group]:
                copy.wait()


VEC, IN, OUT, UP, DOWN = 0, 1, 2, 3, 4
WEIGHT_SCRATCH = [
    pltpu.VMEM((768, 2304), BF16),
    pltpu.VMEM((768, 768), BF16),
    pltpu.VMEM((768, 3072), BF16),
    pltpu.VMEM((3072, 768), BF16),
    pltpu.VMEM((768, 128), BF16),
    pltpu.SemaphoreType.DMA((8, 16)),
]


def bucket_rows(sign=1):
    lane = iota((D, WRAP), 1)
    lane = lane if sign > 0 else lax.rem(WRAP - lane, WRAP)
    distance = jnp.where(lane < WRAP // 2, lane, lane - WRAP)
    bucket = jnp.clip(distance + BUCKETS // 2, 0, BUCKETS - 1)
    return lax.rem(iota((D, WRAP), 0), BUCKETS) == bucket


def head_mask():
    return iota((16, D), 1) // BUCKETS == iota((16, D), 0)


def position_bias(table, stride, keys, bias_ref):
    per_head = jnp.where(head_mask(), table, 0.0).astype(BF16)
    extended = mm(per_head, onehot(bucket_rows()))
    for head in range(HEADS):
        row = jnp.broadcast_to(extended[head : head + 1], (HALF, WRAP))
        rolled = pltpu.roll(row, 0, 1, stride=stride, stride_axis=0)
        bias_ref[head // 2, HALF * (head % 2) : HALF * (head % 2 + 1), :] = rolled[:, :keys]


def by_head(value):
    low = iota(value.shape, 1) < HEAD_DIM
    zero = jnp.zeros_like(value)
    return jnp.concatenate([jnp.where(low, value, zero), jnp.where(low, zero, value)], 0)


def join_heads(value):
    top, bottom = value[:HALF], value[HALF:]
    return jnp.where(iota(top.shape, 1) < HEAD_DIM, top, bottom)


def norm_forward(summed, gain, shift):
    centered = summed - jnp.mean(summed, -1, keepdims=True)
    inverse = lax.rsqrt(jnp.mean(centered * centered, -1, keepdims=True) + EPSILON)
    normal = centered * inverse
    return normal * gain + shift, normal, inverse


def norm_backward(upstream, normal, inverse, gain):
    scaled = upstream * gain
    bracket = (
        scaled
        - jnp.mean(scaled, -1, keepdims=True)
        - normal * jnp.mean(scaled * normal, -1, keepdims=True)
    )
    return inverse * bracket, rowsum(upstream * normal), rowsum(upstream)


def rowsum(value):
    return jnp.sum(value, 0, keepdims=True)


GELU_A, GELU_B = 0.7978845608028654, 0.044715


def gelu(x):
    return 0.5 * x * (1.0 + jnp.tanh(GELU_A * (x + GELU_B * (x * x * x))))


def gelu_slope(x):
    square = x * x
    t = jnp.tanh(GELU_A * (x + GELU_B * (square * x)))
    inner = GELU_A * (1.0 + 3.0 * GELU_B * square)
    return 0.5 * (1.0 + t) + 0.5 * x * (1.0 - t * t) * inner


KEPT = ("q", "k", "v", "prob", "context", "normal1", "inverse1", "low1", "pre", "hidden", "normal2", "inverse2")


def kept_shapes(keys):
    return {
        "q": ((TOKENS, D), BF16),
        "k": ((2 * keys, D), BF16),
        "v": ((2 * keys, D), BF16),
        "prob": ((2 * PAIRS, 128, keys), F32),
        "context": ((TOKENS, D), BF16),
        "normal1": ((TOKENS, D), F32),
        "inverse1": ((TOKENS, 128), F32),
        "low1": ((TOKENS, D), BF16),
        "pre": ((TOKENS, FF), F32),
        "hidden": ((TOKENS, FF), BF16),
        "normal2": ((TOKENS, D), F32),
        "inverse2": ((TOKENS, 128), F32),
    }


def transpose_vectors(w, vt):
    w.wait(VEC)
    vt[...] = jnp.transpose(w.vec[...].astype(F32))[:16]


def layer_forward(w, kept, vt, bias, x_query, x_key, source, valid, stride, keys):
    transpose_vectors(w, vt)
    position_bias(vt[12:13, :], stride, keys, bias)
    w.wait(IN)
    query_low = x_query[...]
    kept["q"][...] = (mm(query_low, w.w_in[:, :D]) + vt[0:1, :]).astype(BF16)
    key_low = x_key[...]
    kept["k"][...] = mm(key_low, w.w_in[:, D : 2 * D]).astype(BF16)
    kept["v"][...] = (mm(key_low, w.w_in[:, 2 * D :]) + vt[1:2, :]).astype(BF16)
    for row in range(2):
        usable = iota((128, keys), 1) < valid[row]
        for pair in range(PAIRS):
            lanes = slice(128 * pair, 128 * pair + 128)
            q = by_head(kept["q"][HALF * row : HALF * (row + 1), lanes])
            k = kept["k"][keys * row : keys * (row + 1), lanes]
            scores = mm_nt(q, k) * 0.125 + bias[pair]
            scores = jnp.where(usable, scores, NEGATIVE)
            unnormed = jnp.exp(scores - jnp.max(scores, -1, keepdims=True))
            prob = unnormed / jnp.sum(unnormed, -1, keepdims=True)
            kept["prob"][PAIRS * row + pair] = prob
            v = kept["v"][keys * row : keys * (row + 1), lanes]
            context = join_heads(mm(prob.astype(BF16), v))
            kept["context"][HALF * row : HALF * (row + 1), lanes] = context.astype(BF16)
    w.wait(OUT)
    attended = mm(kept["context"][...], w.w_out[...]) + vt[2:3, :]
    normed, normal, inverse = norm_forward(source + attended, vt[3:4, :], vt[4:5, :])
    kept["normal1"][...] = normal
    kept["inverse1"][...] = jnp.broadcast_to(inverse, (TOKENS, 128))
    normed_low = normed.astype(BF16)
    kept["low1"][...] = normed_low
    w.wait(UP)
    feed = normed + vt[5:6, :]
    for c in range(4):
        lanes = slice(D * c, D * (c + 1))
        pre = mm(normed_low, w.w_up[:, lanes]) + vt[8 + c : 9 + c, :]
        kept["pre"][:, lanes] = pre
        hidden = gelu(pre).astype(BF16)
        kept["hidden"][:, lanes] = hidden
        w.wait(DOWN + c)
        feed = feed + mm(hidden, w.w_down[lanes, :])
    result, normal, inverse = norm_forward(feed, vt[6:7, :], vt[7:8, :])
    kept["normal2"][...] = normal
    kept["inverse2"][...] = jnp.broadcast_to(inverse, (TOKENS, 128))
    return result


class GradientWriter:
    SLOTS = 3

    def __init__(self, stage, sems):
        self.stage, self.sems, self.flying, self.count = stage, sems, [()] * self.SLOTS, 0

    def write(self, value, line, across, lane):
        slot = self.count % self.SLOTS
        self.count += 1
        self.wait(slot)
        width, limit = value.shape[1], line[1].shape[1]
        self.stage[slot, :, :width] = value.astype(BF16)
        self.flying[slot] = []
        split = min(max(limit - lane, 0), width)
        for k in range(4):
            if k == 0 or split == width:
                parts = [(line[k], 0, width, lane)]
            else:
                parts = [(line[k], 0, split, lane), (across[k], split, width, lane + split - limit)]
            for number, (target, start, stop, at) in enumerate(parts):
                if start == stop:
                    continue
                copy = pltpu.make_async_copy(
                    self.stage.at[slot, pl.ds(CHUNK * k, CHUNK), pl.ds(start, stop - start)],
                    target.at[:, pl.ds(at, stop - start)],
                    self.sems.at[8 * slot + 2 * k + number],
                )
                copy.start()
                self.flying[slot].append(copy)

    def wait(self, slot):
        for copy in self.flying[slot]:
            copy.wait()
        self.flying[slot] = ()

    def finish(self):
        for slot in range(self.SLOTS):
            self.wait(slot)


def turned(index, value, plain, ordered):
    width = value.shape[0]
    plain[:, :width] = jnp.transpose(value)
    for k in range(4):
        for run in range(2):
            row = run_row(index[0], lax.rem(index[1] + k, 4), run)
            at = CHUNK * k + 48 * run
            ordered[at : at + 48, :width] = plain[pl.ds(row, 48), :width]
    return ordered[:, :width]


FEED_ACTS = 2 * D + 2 * FF
ACT_ROWS = TOKENS + 16
ACT_LANES = 4 * D


def feed_gradient_kernel(index, mine, theirs, *refs):
    refs = refs[-14:]
    base, a1, a2, a3, b1, b2, b3, acts, plain, ordered, stage, sems, act_sems = refs[:13]
    line, across = (base, a1, a2, a3), (base, b1, b2, b3)
    copies = []
    for side, ref in enumerate((mine, theirs)):
        target = acts.at[pl.ds(TOKENS * side, TOKENS), :]
        copies.append(pltpu.make_async_copy(ref, target, act_sems.at[side]))
        copies[side].start()
    for copy in copies:
        copy.wait()
    writer = GradientWriter(stage, sems)
    low1 = turned(index, acts[:, :D], plain.at[4], ordered.at[4])
    for c in range(4):
        at = 2 * D + FF + D * c
        writer.write(mm(low1, acts[:, at : at + D]), line, across, D * c)
    feed_grad = acts[:, D + FF : 2 * D + FF]
    for c in range(4):
        hidden = turned(index, acts[:, D + D * c : 2 * D + D * c], plain.at[c], ordered.at[c])
        writer.write(mm(hidden, feed_grad), line, across, FF + D * c)
    writer.finish()


GRADIENT_SCRATCH = [
    pltpu.VMEM((5, 768, 512), BF16),
    pltpu.VMEM((5, 384, 512), BF16),
    pltpu.VMEM((3, 384, 768), BF16),
    pltpu.SemaphoreType.DMA((24,)),
    pltpu.SemaphoreType.DMA((4,)),
]


def feed_gradient(index, mine, theirs, after=()):
    return pl.pallas_call(
        feed_gradient_kernel,
        out_shape=[shape(CHUNK, FEED)] + [shape(CHUNK, FEED_LINE)] * 3 + [shape(CHUNK, FEED - FEED_LINE)] * 3,
        in_specs=[SMEM] + anyspace(2 + len(after)),
        out_specs=anyspace(7),
        scratch_shapes=[pltpu.VMEM((2 * TOKENS, FEED_ACTS), BF16)] + GRADIENT_SCRATCH + [pltpu.VMEM((8, 128), F32)],
        compiler_params=params(28),
        cost_estimate=cost(7),
    )(index, mine, theirs, *after)


def attention_gradient_kernel(keys, outs, index, mine, theirs, *refs):
    refs, scratch = refs[-10 - outs : -10], refs[-10:]
    queries, vectors, keyed, plain, ordered, stage, sems, act_sems, plain_vec, ordered_vec = scratch
    targets = refs[:4], (refs[0], *refs[4:])
    copies = []
    for side, ref in enumerate((mine, theirs)):
        for at, rows, target, sem in (
            (0, TOKENS, queries, act_sems.at[side]),
            (TOKENS, 16, vectors, act_sems.at[2 + side]),
            (ACT_ROWS, keys, keyed, sems.at[side]),
        ):
            lanes = target.shape[1]
            source = ref.at[pl.ds(at, rows), pl.ds(0, lanes)]
            copies.append(pltpu.make_async_copy(source, target.at[pl.ds(rows * side, rows), :], sem))
    for copy in copies:
        copy.start()
    for copy in copies:
        copy.wait()
    writer = GradientWriter(stage, sems)
    context = turned(index, queries[:, :D], plain.at[0], ordered.at[0])
    writer.write(mm(context, queries[:, D : 2 * D]), *targets, OUT_AT)
    query_rows = turned(index, queries[:, 2 * D : 3 * D], plain.at[1], ordered.at[1])
    writer.write(mm(query_rows, queries[:, 3 * D :]), *targets, 0)
    key_rows = turned(index, keyed[:, :D], plain.at[2], ordered.at[2])
    writer.write(mm(key_rows, keyed[:, D : 2 * D]), *targets, D)
    writer.write(mm(key_rows, keyed[:, 2 * D :]), *targets, 2 * D)
    rows = wide(vectors[:16, :]) + wide(vectors[16:, :])
    rows = jnp.concatenate([rows, jnp.zeros((112, D), F32)], 0)
    plain_vec[...] = jnp.transpose(rows)
    for k in range(4):
        for run in range(2):
            row = run_row(index[0], lax.rem(index[1] + k, 4), run)
            at = CHUNK * k + 48 * run
            ordered_vec[at : at + 48, :] = plain_vec[pl.ds(row, 48), :]
    writer.write(ordered_vec[...], *targets, VEC_AT)
    writer.finish()


def attention_gradient(index, mine, theirs, after=()):
    out = [shape(CHUNK, ATTN)] * 4
    keys = mine.shape[0] - ACT_ROWS
    scratch = [
        pltpu.VMEM((2 * TOKENS, ACT_LANES), BF16),
        pltpu.VMEM((32, D), BF16),
        pltpu.VMEM((2 * keys, 3 * D), BF16),
    ]
    vectors = [pltpu.VMEM((768, 128), F32), pltpu.VMEM((384, 128), F32)]
    return pl.pallas_call(
        functools.partial(attention_gradient_kernel, keys, len(out)),
        out_shape=out,
        in_specs=[SMEM] + anyspace(2 + len(after)),
        out_specs=anyspace(len(out)),
        scratch_shapes=scratch + GRADIENT_SCRATCH + vectors,
        compiler_params=params(28),
        cost_estimate=cost(5),
    )(index, mine, theirs, *after)


def feed_backward(w, kept, vt, upstream, acts):
    dsum2, gain2, shift2 = norm_backward(
        upstream, kept["normal2"][...], kept["inverse2"][:, :1], vt[6:7, :]
    )
    feed_grad = dsum2.astype(BF16)
    acts[:, D + FF : 2 * D + FF] = feed_grad
    down_bias = rowsum(wide(feed_grad))
    normed_grad = dsum2
    hidden_bias = []
    for c in range(4):
        lanes = slice(D * c, D * (c + 1))
        w.wait(DOWN + c)
        hidden_grad = mm_nt(feed_grad, w.w_down[lanes, :])
        pre_grad = (gelu_slope(kept["pre"][:, lanes]) * hidden_grad).astype(BF16)
        at = 2 * D + FF + D * c
        acts[:, at : at + D] = pre_grad
        hidden_bias.append(rowsum(wide(pre_grad)))
        if c == 0:
            w.wait(UP)
        normed_grad = normed_grad + mm_nt(pre_grad, w.w_up[:, lanes])
    acts[:, :D] = kept["low1"][...]
    acts[:, D : D + FF] = kept["hidden"][...]
    zero = jnp.zeros((1, D), F32)
    rows = [zero] * 5 + [down_bias, gain2, shift2] + hidden_bias + [zero] * 4
    return normed_grad, jnp.concatenate(rows, 0)


def attention_backward(
    w, kept, vt, x_query, x_key, normed_grad, vector_rows, stride, keys, acts, work
):
    dq, dk, dv, table = work
    dsum1, gain1, shift1 = norm_backward(
        normed_grad, kept["normal1"][...], kept["inverse1"][:, :1], vt[3:4, :]
    )
    attended_grad = dsum1.astype(BF16)
    out_bias = rowsum(wide(attended_grad))
    acts[:TOKENS, :D] = kept["context"][...]
    acts[:TOKENS, D : 2 * D] = attended_grad
    acts[:TOKENS, 2 * D : 3 * D] = x_query[...]
    w.wait(OUT)
    context_grad = mm_nt(attended_grad, w.w_out[...]).astype(BF16)
    table[...] = jnp.zeros((16, WRAP), F32)
    mirror = (2 * keys, WRAP)
    mirror = onehot(lax.rem(lax.rem(iota(mirror, 0), keys) + iota(mirror, 1), WRAP) == 0)
    for pair in range(PAIRS):
        lanes = slice(128 * pair, 128 * pair + 128)
        pair_scores = []
        for row in range(2):
            here = slice(HALF * row, HALF * (row + 1))
            there = slice(keys * row, keys * (row + 1))
            grad = by_head(context_grad[here, lanes])
            prob = kept["prob"][PAIRS * row + pair]
            v = kept["v"][there, lanes]
            prob_grad = mm_nt(grad, v)
            dv[there, lanes] = mm_tn(prob.astype(BF16), grad).astype(BF16)
            score = prob * (prob_grad - jnp.sum(prob_grad * prob, -1, keepdims=True))
            score = score.astype(BF16)
            q = by_head(kept["q"][here, lanes])
            k = kept["k"][there, lanes]
            dq[here, lanes] = (0.125 * join_heads(mm(score, k))).astype(BF16)
            dk[there, lanes] = (0.125 * mm_tn(score, q)).astype(BF16)
            pair_scores.append(score)
        spread = mm(jnp.concatenate(pair_scores, 1), mirror)
        for half in range(2):
            rolled = pltpu.roll(
                spread[HALF * half : HALF * (half + 1)], 0, 1, stride=stride, stride_axis=0
            )
            table[2 * pair + half : 2 * pair + half + 1, :] = rowsum(rolled)
    dq_low, dk_low, dv_low = dq[...], dk[...], dv[...]
    w.wait(IN)
    source_grad = dsum1 + mm_nt(dq_low, w.w_in[:, :D])
    key_side = mm_nt(dk_low, w.w_in[:, D : 2 * D]) + mm_nt(dv_low, w.w_in[:, 2 * D :])
    acts[:TOKENS, 3 * D :] = dq_low
    acts[ACT_ROWS:, :D] = x_key[...]
    acts[ACT_ROWS:, D : 2 * D] = dk_low
    acts[ACT_ROWS:, 2 * D : 3 * D] = dv_low
    buckets = lax.dot_general(
        table[...],
        bucket_rows(-1).astype(F32),
        (((1,), (1,)), ((), ())),
        precision=lax.Precision.HIGHEST,
        preferred_element_type=F32,
    )
    table_grad = rowsum(jnp.where(head_mask(), buckets, 0.0))
    rows = [rowsum(wide(dq_low)), rowsum(wide(dv_low)), out_bias, gain1, shift1]
    rows += [vector_rows[5:12, :], table_grad, jnp.zeros((3, D), F32)]
    acts[TOKENS:ACT_ROWS, :D] = jnp.concatenate(rows, 0).astype(BF16)
    return source_grad, key_side


FOR_ATTENTION = ("q", "k", "v", "prob", "context", "normal1", "inverse1")
FOR_FEED = ("low1", "pre", "hidden", "normal2", "inverse2")


def pooling():
    return 0.5 * (iota((TOKENS, 2 * SEQ), 1) // 2 == iota((TOKENS, 2 * SEQ), 0)).astype(F32)


def one_forward_kernel(index, tokens, *refs):
    chunks = refs[:15]
    middle, pooled_low, *refs = refs[-22:]
    kept = dict(zip(KEPT, refs[:12]))
    vt, bias, *scratch = refs[12:]
    w = Weights(index, chunks, scratch[:5], scratch[5])
    w.start(range(8))
    pooled = mm(pooling().astype(BF16), tokens[...])
    pooled_low[...] = pooled.astype(BF16)
    valid = [index[5], index[6]]
    middle[...] = layer_forward(w, kept, vt, bias, pooled_low, tokens, pooled, valid, 2, SEQ)


def one_forward(index, tokens, chunks, after):
    kept = [shape(*dims, dtype=dtype) for dims, dtype in kept_shapes(SEQ).values()]
    return pl.pallas_call(
        one_forward_kernel,
        out_shape=[shape(TOKENS, D, dtype=F32), shape(TOKENS, D)] + kept,
        in_specs=[SMEM] + vmem(1) + anyspace(15 + len(after)),
        out_specs=vmem(14),
        scratch_shapes=[pltpu.VMEM((16, D), F32), pltpu.VMEM((PAIRS, 128, SEQ), F32)] + WEIGHT_SCRATCH,
        compiler_params=params(),
        cost_estimate=cost(13),
    )(index, tokens, *chunks, *after)


def two_forward_kernel(index, middle, cotangent, *refs):
    chunks, refs = refs[:15], refs[15:]
    result, normed_grad, vector_rows, acts = refs[:4]
    kept = dict(zip(FOR_ATTENTION + FOR_FEED, refs[4:16]))
    vt, bias, middle_low, *scratch = refs[16:]
    w = Weights(index, chunks, scratch[:5], scratch[5])
    w.start(range(8))
    middle_low[...] = middle[...].astype(BF16)
    valid = [(index[5] + 1) // 2, (index[6] + 1) // 2]
    out = layer_forward(w, kept, vt, bias, middle_low, middle_low, middle[...], valid, 1, HALF)
    result[...] = out.astype(BF16)
    w.wait = lambda *groups: None
    normed_grad[...], vector_rows[...] = feed_backward(w, kept, vt, cotangent[...], acts)


def two_forward(index, middle, cotangent, chunks):
    dims = kept_shapes(HALF)
    kept = [shape(*dims[name][0], dtype=dims[name][1]) for name in FOR_ATTENTION]
    scratch = [pltpu.VMEM(*dims[name]) for name in FOR_FEED]
    out = [shape(TOKENS, D), shape(TOKENS, D, dtype=F32), shape(16, D, dtype=F32)]
    outs = pl.pallas_call(
        two_forward_kernel,
        out_shape=out + [shape(TOKENS, FEED_ACTS)] + kept,
        in_specs=[SMEM] + vmem(2) + anyspace(15),
        out_specs=vmem(11),
        scratch_shapes=scratch
        + [pltpu.VMEM((16, D), F32), pltpu.VMEM((PAIRS, 128, HALF), F32), pltpu.VMEM((TOKENS, D), BF16)]
        + WEIGHT_SCRATCH,
        compiler_params=params(),
        cost_estimate=cost(17),
    )(index, middle, cotangent, *chunks)
    return outs[:3], outs[3], outs[4:]


def two_backward_kernel(index, middle, normed_grad, vector_rows, *refs):
    kept = dict(zip(FOR_ATTENTION, refs[:7]))
    chunks, refs = refs[7:22], refs[22:]
    upstream, acts, vt, middle_low, *work = refs[:8]
    scratch = refs[8:]
    w = Weights(index, chunks, scratch[:5], scratch[5])
    w.start((VEC, OUT, IN))
    middle_low[...] = middle[...].astype(BF16)
    transpose_vectors(w, vt)
    source_grad, key_side = attention_backward(
        w, kept, vt, middle_low, middle_low, normed_grad[...], vector_rows, 1, HALF, acts, work
    )
    upstream[...] = source_grad + key_side


def two_backward(index, middle, normed_grad, vector_rows, kept, chunks):
    return pl.pallas_call(
        two_backward_kernel,
        out_shape=[shape(TOKENS, D, dtype=F32), shape(ACT_ROWS + TOKENS, ACT_LANES)],
        in_specs=[SMEM] + vmem(10) + anyspace(15),
        out_specs=vmem(2),
        scratch_shapes=[pltpu.VMEM((16, D), F32)]
        + [pltpu.VMEM((TOKENS, D), BF16)] * 4
        + [pltpu.VMEM((16, WRAP), F32)]
        + WEIGHT_SCRATCH,
        compiler_params=params(),
        cost_estimate=cost(10),
    )(index, middle, normed_grad, vector_rows, *kept, *chunks)


def one_feed_kernel(index, upstream, *refs):
    kept = dict(zip(FOR_FEED, refs[:5]))
    chunks = refs[5:20]
    normed_grad, vector_rows, acts, vt, *scratch = refs[-10:]
    w = Weights(index, chunks, scratch[:5], scratch[5])
    w.start((VEC, DOWN, DOWN + 1, DOWN + 2, DOWN + 3, UP))
    transpose_vectors(w, vt)
    normed_grad[...], vector_rows[...] = feed_backward(w, kept, vt, upstream[...], acts)


def one_feed(index, upstream, kept, chunks, after):
    normed_grad, vector_rows, acts = pl.pallas_call(
        one_feed_kernel,
        out_shape=[shape(TOKENS, D, dtype=F32), shape(16, D, dtype=F32), shape(TOKENS, FEED_ACTS)],
        in_specs=[SMEM] + vmem(6) + anyspace(15 + len(after)),
        out_specs=vmem(3),
        scratch_shapes=[pltpu.VMEM((16, D), F32)] + WEIGHT_SCRATCH,
        compiler_params=params(),
        cost_estimate=cost(9),
    )(index, upstream, *kept, *chunks, *after)
    return (normed_grad, vector_rows), acts


def one_backward_kernel(index, tokens, pooled_low, normed_grad, vector_rows, *refs):
    kept = dict(zip(FOR_ATTENTION, refs[:7]))
    chunks = refs[7:22]
    input_grad, acts, vt, *refs = refs[-13:]
    work, scratch = refs[:4], refs[4:]
    w = Weights(index, chunks, scratch[:5], scratch[5])
    w.start((VEC, OUT, IN))
    transpose_vectors(w, vt)
    source_grad, key_side = attention_backward(
        w, kept, vt, pooled_low, tokens, normed_grad[...], vector_rows, 2, SEQ, acts, work
    )
    repeated = lax.dot_general(
        pooling(),
        source_grad,
        (((0,), (0,)), ((), ())),
        precision=lax.Precision.HIGHEST,
        preferred_element_type=F32,
    )
    input_grad[...] = key_side + repeated


def one_backward(index, tokens, pooled_low, normed_grad, vector_rows, kept, chunks, after):
    return pl.pallas_call(
        one_backward_kernel,
        out_shape=[shape(2 * SEQ, D, dtype=F32), shape(ACT_ROWS + 2 * SEQ, ACT_LANES)],
        in_specs=[SMEM] + vmem(11) + anyspace(15 + len(after)),
        out_specs=vmem(2),
        scratch_shapes=[pltpu.VMEM((16, D), F32), pltpu.VMEM((TOKENS, D), BF16)]
        + [pltpu.VMEM((2 * SEQ, D), BF16)] * 2
        + [pltpu.VMEM((16, WRAP), F32)]
        + WEIGHT_SCRATCH,
        compiler_params=params(),
        cost_estimate=cost(13),
    )(index, tokens, pooled_low, normed_grad, vector_rows, *kept, *chunks, *after)


def local(inputs, lengths, cotangent, *weights):
    device = lax.axis_index("dp") * 32 + lax.axis_index("shard")
    sources = lax.dynamic_index_in_dim(jnp.array(spread_sources(), jnp.int32), device, 0, False)
    scalars = [*place_scalars(), lengths[0, 0], lengths[1, 0], jnp.zeros((), jnp.int32)]
    index = jnp.concatenate([jnp.stack(scalars), sources])
    tokens = inputs.reshape(2 * SEQ, D)

    blob = prepare((weights[:5], weights[5:]))
    line = widen(index, [permute(blob, spread_pairs(k)) for k in range(4)])
    parts = [line] + [permute(line, line_pairs(-k)) for k in (1, 2, 3)]
    gather_one = Gather(widen_more(0, index, parts))
    chunk_two = widen_more(1, index, parts, (gather_one.near[0],))
    one = gather_one.finish()
    gather_two = Gather(chunk_two, one[2], one[9])
    middle, pooled_low, *kept = one_forward(index, tokens, one, (gather_two.own_swap,))
    kept = dict(zip(KEPT, kept))
    two = gather_two.finish(middle)

    (result, *back_two), acts_feed, kept_two = two_forward(
        index, middle, cotangent.reshape(TOKENS, D), two
    )
    acts_feed = acts_feed, permute(acts_feed, SWAP)
    upstream, acts_attn = two_backward(index, middle, *back_two, kept_two, two)
    acts_attn = acts_attn, permute(tie(acts_attn, acts_feed[1]), SWAP)

    feed_two = feed_gradient(index, *acts_feed, (upstream,))
    near_feed_two = send_near(feed_two)
    back_one, acts_feed = one_feed(
        index, upstream, [kept[name] for name in FOR_FEED], one, (feed_two[0],)
    )
    acts_feed = acts_feed, permute(tie(acts_feed, *near_feed_two), SWAP)
    attn_two = attention_gradient(index, *acts_attn, (back_one[0], *near_feed_two))
    far_feed_two = send_far(feed_two, *near_feed_two, attn_two[0])
    near_attn_two = send_near(attn_two)
    feed_one = feed_gradient(index, *acts_feed, (attn_two[0],))
    sent = (*far_feed_two, *near_attn_two, feed_one[0])
    far_attn_two = send_far(attn_two, *sent)
    near_feed_one = send_near(feed_one, *sent)
    input_grad, acts_attn = one_backward(
        index,
        tokens,
        pooled_low,
        *back_one,
        [kept[name] for name in FOR_ATTENTION],
        one,
        sent,
    )
    acts_attn = acts_attn, permute(tie(acts_attn, *near_feed_one, *far_attn_two), SWAP)
    far_feed_one = send_far(feed_one, *near_feed_one, *far_attn_two)
    pieces = narrow(WIDTH + ATTN, index, received(feed_two, near_feed_two, far_feed_two))
    attn_one = attention_gradient(index, *acts_attn, (pieces[0],))
    near_attn_one = send_near(attn_one, *far_feed_one)
    far_attn_one = send_far(attn_one, *far_feed_one)

    pieces = narrow(WIDTH, index, received(attn_two, near_attn_two, far_attn_two), pieces)
    pieces = narrow(ATTN, index, received(feed_one, near_feed_one, far_feed_one), pieces)
    pieces = narrow(0, index, received(attn_one, near_attn_one, far_attn_one), pieces)
    pieces = [pieces[0]] + [permute(pieces[k], line_pairs(k)) for k in (1, 2, 3)]
    pieces = narrow_more(index, pieces)
    grads = finish([permute(pieces[k], back(spread_pairs(k))) for k in range(4)])
    return (
        result.reshape(2, 1, HALF, D),
        input_grad.reshape(2, 1, SEQ, D),
        *grads,
    )


def solution(mesh):
    rows = P(None, AXES, None, None)
    shard = P(AXES, None)
    return jax.shard_map(
        local,
        mesh=mesh,
        in_specs=(rows, P(None, AXES), rows) + (shard,) * 10,
        out_specs=(rows, rows) + (shard,) * 10,
        check_vma=False,
    )
```

```python
import functools
import itertools

import jax
import jax.numpy as jnp
from jax import lax
from jax.experimental import pallas as pl
from jax.experimental.pallas import tpu as pltpu
from jax.sharding import PartitionSpec as P

AXES = ("dp", "shard")
F32, BF16 = jnp.float32, jnp.bfloat16
D, HEADS, HEAD_DIM, FF, BUCKETS = 768, 12, 64, 3072, 64
SEQ, HALF, TOKENS = 128, 64, 128
PAIRS = HEADS // 2
EPSILON = 1e-06
NEGATIVE = -1000000000.0
WRAP = 256

ROW = 6
CHUNK = 96
OUT_AT, VEC_AT, UP_AT, DOWN_AT, WIDTH = 2304, 3072, 3200, 6272, 9344
A_WIDTH, B_WIDTH = DOWN_AT, WIDTH - DOWN_AT
PACKED = 4736
ATTN, FEED = UP_AT, WIDTH - UP_AT
FEED_LINE = 4096


def place(core, block, v2, v1):
    z = (block - v1) % 4
    x, y = (v1, v2) if core == 0 else (v2, v1)
    return ((x * 4 + y) * 4 + z) * 2 + core


def virtual(device):
    x, y, z, half = device // 32, device // 8 % 4, device // 2 % 4, device % 2
    if y % 2 == 0:
        return 0, x, y + half, z
    return 1, x % 2 + 2 * (y // 2), (x + half) % 4, z


def latin_squares():
    rows = list(itertools.permutations(range(4)))
    found = []
    for three in itertools.product(rows, repeat=3):
        if all(len({row[i] for row in three}) == 3 for i in range(4)):
            found.append((*three, tuple(6 - sum(row[i] for row in three) for i in range(4))))
    return found


CHOSEN = (37, 82, 157, 37, 214, 52, 174, 394, 384, 493, 432, 70, 186, 264, 256, 523, 141, 364, 399, 489, 205, 175, 408, 508, 390, 358, 335, 34, 286, 179, 230, 263)
SQUARES = [latin_squares()[number] for number in CHOSEN]


def square_of(core, block, v2):
    return SQUARES[16 * core + 4 * block + v2]


def spread_pairs(number):
    pairs = []
    for f in range(128):
        core, block, v2, j = virtual(f)
        v1 = square_of(core, block, v2)[j].index(number)
        pairs.append((f, place(core, block, v2, v1)))
    return pairs


def spread_sources():
    table = [None] * 128
    for v in range(128):
        core, block, v2, v1 = v // 64, v // 16 % 4, v // 4 % 4, v % 4
        column = [row[v1] for row in square_of(core, block, v2)]
        table[place(core, block, v2, v1)] = [column.index(number) for number in range(4)]
    return table


def line_pairs(step):
    pairs = []
    for v in range(128):
        core, block, v2, v1 = v // 64, v // 16 % 4, v // 4 % 4, v % 4
        pairs.append((place(core, block, v2, v1), place(core, block, (v2 + step) % 4, v1)))
    return pairs


def run_row(core, block, run):
    even = 192 * block + 96 * run
    odd = 192 * lax.rem(block, 2) + 384 * run + 48 + 96 * (block // 2)
    return pl.multiple_of(jnp.where(core == 0, even, odd), 16)


def along(axis_of_core, step):
    pairs = []
    for f in range(128):
        at = [f // 32, f // 8 % 4, f // 2 % 4]
        axis = axis_of_core[f % 2]
        at[axis] = (at[axis] + step) % 4
        pairs.append((f, ((at[0] * 4 + at[1]) * 4 + at[2]) * 2 + f % 2))
    return pairs


A_AXES, B_AXES = (0, 1), (2, 2)
SWAP = [(f, f ^ 1) for f in range(128)]


def permute(value, pairs):
    return lax.ppermute(value, AXES, pairs)


def back(pairs):
    return [(b, a) for a, b in pairs]


def place_scalars():
    x, inner = lax.axis_index("dp"), lax.axis_index("shard")
    y, z, core = inner // 8, inner // 2 % 4, inner % 2
    first = core == 0
    block = jnp.where(first, x + z, y + z) % 4
    other = jnp.where(first, y + z, x + z) % 4
    v2, v1 = jnp.where(first, y, x), jnp.where(first, x, y)
    return [core, block, other, v2, v1]


def mm(a, b):
    return lax.dot_general(a, b, (((1,), (0,)), ((), ())), preferred_element_type=F32)


def mm_nt(a, b):
    return lax.dot_general(a, b, (((1,), (1,)), ((), ())), preferred_element_type=F32)


def mm_tn(a, b):
    return lax.dot_general(a, b, (((0,), (0,)), ((), ())), preferred_element_type=F32)


def exact(a, b):
    return lax.dot_general(
        a, b, (((1,), (0,)), ((), ())), precision=lax.Precision.HIGHEST, preferred_element_type=F32
    )


def iota(shape, axis):
    return lax.broadcasted_iota(jnp.int32, shape, axis)


def onehot(condition):
    return condition.astype(F32).astype(BF16)


def split_hidden():
    source, out = iota((512, 512), 0), iota((512, 512), 1)
    return onehot((source // 4 == out % 128) & (source % 4 == out // 128))


def vmem(n):
    return [pl.BlockSpec(memory_space=pltpu.VMEM)] * n


def anyspace(n):
    return [pl.BlockSpec(memory_space=pl.ANY)] * n


SMEM = pl.BlockSpec(memory_space=pltpu.SMEM)


def params(mebibytes=56):
    return pltpu.CompilerParams(vmem_limit_bytes=mebibytes * 1024 * 1024)


def cost(microseconds):
    return pl.CostEstimate(flops=0, bytes_accessed=int(microseconds * 3.5e6), transcendentals=0)


def shape(*dims, dtype=BF16):
    return jax.ShapeDtypeStruct(dims, dtype)


def prepare_kernel(*refs):
    shards, packed, out = refs[:10], refs[10], refs[11]
    pad = onehot(iota((8, ROW), 0) == iota((8, ROW), 1))
    split = split_hidden()
    for layer in range(2):
        proj_in, proj_out, up, down, vectors = shards[5 * layer : 5 * layer + 5]
        at = 2 * PACKED * layer
        out[:, at : at + OUT_AT] = mm(pad, proj_in[...]).astype(BF16)
        out[:, at + OUT_AT : at + VEC_AT] = mm(pad, proj_out[...]).astype(BF16)
        for group in range(6):
            part = mm(pad, up[:, 512 * group : 512 * group + 512]).astype(BF16)
            part = mm(part, split).astype(BF16)
            for c in range(4):
                lane = at + UP_AT + 768 * c + 128 * group
                out[:, lane : lane + 128] = part[:, 128 * c : 128 * c + 128]
        out[:, at + VEC_AT : at + UP_AT] = jnp.zeros((8, 128), BF16)
        out[:, at + VEC_AT : at + VEC_AT + 13] = mm(pad, vectors[...]).astype(BF16)
        for c in range(4):
            rows = onehot(iota((8, 24), 1) == 4 * iota((8, 24), 0) + c)
            lane = at + DOWN_AT + 768 * c
            out[:, lane : lane + 768] = mm(rows, down[...]).astype(BF16)
        out[:, at + WIDTH : at + 2 * PACKED] = jnp.zeros((8, 2 * PACKED - WIDTH), BF16)
    total = None
    for quarter in range(4):
        rows = onehot((iota((24, 8), 0) - ROW * quarter == iota((24, 8), 1)) & (iota((24, 8), 1) < ROW))
        piece = mm(rows, out[:, PACKED * quarter : PACKED * (quarter + 1)])
        total = piece if total is None else total + piece
    packed[...] = total.astype(BF16)


def prepare(shards):
    return pl.pallas_call(
        prepare_kernel,
        out_shape=shape(24, PACKED),
        in_specs=vmem(10),
        out_specs=vmem(1)[0],
        scratch_shapes=[pltpu.VMEM((8, 4 * PACKED), BF16)],
        compiler_params=params(),
        cost_estimate=cost(4),
    )(*shards[0], *shards[1])


def block_at(digit, quarter):
    wanted, source = iota((24, 24), 0) - ROW * digit, iota((24, 24), 1)
    return onehot((wanted >= 0) & (wanted < ROW) & (wanted + ROW * quarter == source))


def widen_kernel(index, *refs):
    parts, out = refs[:4], refs[4]
    for quarter in range(4):
        layer, half = quarter // 2, quarter % 2
        width = WIDTH - PACKED if half else PACKED
        total = None
        for k in range(4):
            piece = mm(block_at(index[8 + k], quarter), parts[k][:, :width])
            total = piece if total is None else total + piece
        at = WIDTH * layer + PACKED * half
        out[:, at : at + width] = total.astype(BF16)


def widen(index, parts):
    return pl.pallas_call(
        widen_kernel,
        out_shape=shape(24, 2 * WIDTH),
        in_specs=[SMEM] + vmem(4),
        out_specs=vmem(1)[0],
        compiler_params=params(24),
        cost_estimate=cost(4),
    )(index, *parts)


def line_block(index, k):
    v2 = lax.rem(index[3] + k, 4)
    first = jnp.where(index[0] == 0, 0, lax.rem(index[1], 2))
    unit = lax.rem(v2 - first + 4, 4)
    row, source = iota((CHUNK, 24), 0), iota((CHUNK, 24), 1)
    here = (row // 48 == unit // 2) & (row % 12 // 6 == lax.rem(unit, 2))
    return onehot(here & (source == row % 48 // 12 * 6 + row % 6))


def widen_more_kernel(layer, index, *refs):
    parts, (out_a, out_b, both) = refs[:4], refs[-3:]
    places = [line_block(index, k) for k in range(4)]
    for out, start, width in ((out_a, 0, A_WIDTH), (out_b, A_WIDTH, B_WIDTH)):
        total = None
        for k in range(4):
            at = WIDTH * layer + start
            piece = mm(places[k], parts[k][:, at : at + width])
            total = piece if total is None else total + piece
        total = total.astype(BF16)
        out[...] = total
        both[:, start : start + width] = total


def widen_more(layer, index, parts, after=()):
    return pl.pallas_call(
        functools.partial(widen_more_kernel, layer),
        out_shape=[shape(CHUNK, A_WIDTH), shape(CHUNK, B_WIDTH), shape(CHUNK, WIDTH)],
        in_specs=[SMEM] + vmem(4) + anyspace(len(after)),
        out_specs=vmem(3),
        compiler_params=params(24),
        cost_estimate=cost(5),
    )(index, *parts, *after)


def tie(value, *before):
    return lax.optimization_barrier((value, *before))[0]


class Gather:
    def __init__(self, chunk, *before):
        self.a, self.b, both = lax.optimization_barrier((*chunk, *before))[:3]
        self.own_swap = permute(both, SWAP)
        self.near = [permute(self.a, along(A_AXES, -k)) for k in (1, 3)]
        self.near += [permute(self.b, along(B_AXES, -k)) for k in (1, 3)]

    def finish(self, *before):
        far_a, far_b, *near = lax.optimization_barrier(
            (self.a, self.b, *self.near, self.own_swap, *before)
        )
        far = [permute(far_a, along(A_AXES, -2)), permute(far_b, along(B_AXES, -2))]
        swapped = [None, None, permute(near[2], SWAP), permute(near[3], SWAP)]
        for k in range(2):
            swapped[k] = permute(tie(near[k], swapped[k + 2]), SWAP)
        far_a, far_b, *_ = lax.optimization_barrier((*far, *swapped))
        far_swapped = [permute(far_a, SWAP), permute(far_b, SWAP)]
        return [
            *(self.a, self.near[0], far[0], self.near[1]),
            *(swapped[0], far_swapped[0], swapped[1]),
            *(self.b, self.near[2], far[1], self.near[3]),
            *(swapped[2], far_swapped[1], swapped[3]),
            self.own_swap,
        ]


def narrow_kernel(at, count, index, *refs):
    base, *got = refs[:count]
    *outs, stage, sems = refs[-6:]
    places = [line_block(index, k) for k in range(4)]
    width, line = base.shape[1], got[0].shape[1]
    for start, stop, pieces in ((0, line, got[:3]), (line, width, got[3:])):
        if start == stop:
            continue
        one, two, three = [wide(piece[...]) for piece in pieces]
        total = ((wide(base[:, start:stop]) + one) + (two + three)).astype(BF16)
        for k in range(4):
            stage[k, :, start:stop] = mm_tn(places[k], total).astype(BF16)
    copies = []
    for k in range(4):
        copies.append(
            pltpu.make_async_copy(stage.at[k], outs[k].at[:, pl.ds(at, width)], sems.at[k])
        )
        copies[k].start()
    for copy in copies:
        copy.wait()


def narrow(at, index, unit, onto=()):
    width, count = unit[0].shape[1], len(unit)
    return pl.pallas_call(
        functools.partial(narrow_kernel, at, count),
        out_shape=[shape(24, 2 * WIDTH)] * 4,
        in_specs=[SMEM] + vmem(count) + anyspace(len(onto)),
        out_specs=anyspace(4),
        scratch_shapes=[pltpu.VMEM((4, 24, width), BF16), pltpu.SemaphoreType.DMA((4,))],
        input_output_aliases={1 + count + k: k for k in range(len(onto))},
        compiler_params=params(24),
        cost_estimate=cost(4),
    )(index, *unit, *onto)


def wide(value):
    return value.astype(F32)


def narrow_more_kernel(index, *refs):
    parts, outs, held = refs[:4], refs[4:8], refs[8]
    split = split_hidden()
    for layer in range(2):
        at, to = WIDTH * layer, 2 * PACKED * layer
        one, two, three, four = [wide(part[:, at : at + WIDTH]) for part in parts]
        total = ((one + two) + (three + four)).astype(BF16)
        held[:, to : to + UP_AT] = total[:, :UP_AT]
        for group in range(6):
            lanes = [UP_AT + 768 * c + 128 * group for c in range(4)]
            part = jnp.concatenate([total[:, lane : lane + 128] for lane in lanes], 1)
            lane = to + UP_AT + 512 * group
            held[:, lane : lane + 512] = mm_nt(part, split).astype(BF16)
        held[:, to + DOWN_AT : to + WIDTH] = total[:, DOWN_AT:]
        held[:, to + WIDTH : to + 2 * PACKED] = jnp.zeros((24, 2 * PACKED - WIDTH), BF16)
    for k in range(4):
        total = None
        for quarter in range(4):
            lanes = held[:, PACKED * quarter : PACKED * (quarter + 1)]
            piece = mm_tn(block_at(index[8 + k], quarter), lanes)
            total = piece if total is None else total + piece
        outs[k][...] = total.astype(BF16)


def narrow_more(index, parts):
    return pl.pallas_call(
        narrow_more_kernel,
        out_shape=[shape(24, PACKED)] * 4,
        in_specs=[SMEM] + vmem(4),
        out_specs=vmem(4),
        scratch_shapes=[pltpu.VMEM((24, 4 * PACKED), BF16)],
        compiler_params=params(24),
        cost_estimate=cost(6),
    )(index, *parts)


def finish_kernel(*refs):
    (one, two, three, four), outs = [wide(ref[...]) for ref in refs[:4]], refs[4:]
    total = (one + two) + (three + four)
    for layer in range(2):
        proj_in, proj_out, up, down, vectors = outs[5 * layer : 5 * layer + 5]
        first, second = [total[ROW * q : ROW * (q + 1)] for q in (2 * layer, 2 * layer + 1)]
        proj_in[...] = first[:, :OUT_AT]
        proj_out[...] = first[:, OUT_AT:VEC_AT]
        vectors[...] = first[:, VEC_AT : VEC_AT + 13]
        up[:, : PACKED - UP_AT] = first[:, UP_AT:]
        up[:, PACKED - UP_AT :] = second[:, : DOWN_AT - PACKED]
        rows = None
        for c in range(4):
            place_rows = (iota((24, ROW), 0) == 4 * iota((24, ROW), 1) + c).astype(F32)
            lane = DOWN_AT - PACKED + 768 * c
            piece = exact(place_rows, second[:, lane : lane + 768])
            rows = piece if rows is None else rows + piece
        down[...] = rows


def finish(parts):
    one = [shape(ROW, n, dtype=F32) for n in (2304, 768, 3072)]
    one += [shape(24, 768, dtype=F32), shape(ROW, 13, dtype=F32)]
    return pl.pallas_call(
        finish_kernel,
        out_shape=one + one,
        in_specs=vmem(4),
        out_specs=vmem(10),
        compiler_params=params(24),
        cost_estimate=cost(4),
    )(*parts)


def send_sums(parts, axes, steps, *before):
    parts = [parts[k - 1] for k in steps]
    if before:
        parts = lax.optimization_barrier((*parts, *before))[: len(steps)]
    return [permute(part, along(axes, k)) for part, k in zip(parts, steps)]


def send_near(sums, *before):
    near = send_sums(sums[1:4], A_AXES, (1, 3), *before)
    return near + (send_sums(sums[4:7], B_AXES, (1, 3), *before) if len(sums) > 4 else [])


def send_far(sums, *before):
    far = send_sums(sums[1:4], A_AXES, (2,), *before)
    return far + (send_sums(sums[4:7], B_AXES, (2,), *before) if len(sums) > 4 else [])


def received(sums, near, far):
    got = [sums[0], near[0], near[1], far[0]]
    return got + [near[2], near[3], far[1]] if len(sums) > 4 else got


class Weights:
    def __init__(self, index, chunks, scratch, sems):
        self.w_in, self.w_out, self.w_up, self.w_down, self.vec = scratch
        own_a, other_a, own_b, other_b = chunks[:4], chunks[4:7], chunks[7:11], chunks[11:14]
        joined = chunks[14]
        other_a = [joined.at[:, :A_WIDTH], *other_a]
        other_b = [joined.at[:, A_WIDTH:WIDTH], *other_b]
        self.copies = [[] for _ in range(8)]
        for side in range(2):
            core = index[0] if side == 0 else 1 - index[0]
            first = index[1] if side == 0 else index[2]
            a_refs, b_refs = ((own_a, own_b), (other_a, other_b))[side]
            for k in range(4):
                block = lax.rem(first + k, 4)
                for run in range(2):
                    row = run_row(core, block, run)
                    rows = pl.ds(48 * run, 48)
                    a, b = a_refs[k], b_refs[k]
                    targets = [
                        (a, VEC_AT, 128, self.vec, row),
                        (a, 0, 2304, self.w_in, row),
                        (a, OUT_AT, 768, self.w_out, row),
                        (a, UP_AT, 3072, self.w_up, row),
                    ]
                    for c in range(4):
                        target = pl.multiple_of(768 * c + row, 16)
                        targets.append((b, 768 * c, 768, self.w_down, target))
                    for group, (ref, lane, width, out, at) in enumerate(targets):
                        self.copies[group].append(
                            (
                                ref.at[rows, pl.ds(lane, width)],
                                out.at[pl.ds(at, 48), :],
                                sems.at[group, 8 * side + 2 * k + run],
                            )
                        )

    def start(self, groups):
        for group in groups:
            self.copies[group] = [pltpu.make_async_copy(*copy) for copy in self.copies[group]]
            for copy in self.copies[group]:
                copy.start()

    def wait(self, *groups):
        for group in groups:
            for copy in self.copies[group]:
                copy.wait()


VEC, IN, OUT, UP, DOWN = 0, 1, 2, 3, 4
WEIGHT_SCRATCH = [
    pltpu.VMEM((768, 2304), BF16),
    pltpu.VMEM((768, 768), BF16),
    pltpu.VMEM((768, 3072), BF16),
    pltpu.VMEM((3072, 768), BF16),
    pltpu.VMEM((768, 128), BF16),
    pltpu.SemaphoreType.DMA((8, 16)),
]


def bucket_rows(sign=1):
    lane = iota((D, WRAP), 1)
    lane = lane if sign > 0 else lax.rem(WRAP - lane, WRAP)
    distance = jnp.where(lane < WRAP // 2, lane, lane - WRAP)
    bucket = jnp.clip(distance + BUCKETS // 2, 0, BUCKETS - 1)
    return lax.rem(iota((D, WRAP), 0), BUCKETS) == bucket


def head_mask():
    return iota((16, D), 1) // BUCKETS == iota((16, D), 0)


def position_bias(table, stride, keys, bias_ref):
    per_head = jnp.where(head_mask(), table, 0.0).astype(BF16)
    extended = mm(per_head, onehot(bucket_rows()))
    for head in range(HEADS):
        row = jnp.broadcast_to(extended[head : head + 1], (HALF, WRAP))
        rolled = pltpu.roll(row, 0, 1, stride=stride, stride_axis=0)
        bias_ref[head // 2, HALF * (head % 2) : HALF * (head % 2 + 1), :] = rolled[:, :keys]


def by_head(value):
    low = iota(value.shape, 1) < HEAD_DIM
    zero = jnp.zeros_like(value)
    return jnp.concatenate([jnp.where(low, value, zero), jnp.where(low, zero, value)], 0)


def join_heads(value):
    top, bottom = value[:HALF], value[HALF:]
    return jnp.where(iota(top.shape, 1) < HEAD_DIM, top, bottom)


def norm_forward(summed, gain, shift):
    centered = summed - jnp.mean(summed, -1, keepdims=True)
    inverse = lax.rsqrt(jnp.mean(centered * centered, -1, keepdims=True) + EPSILON)
    normal = centered * inverse
    return normal * gain + shift, normal, inverse


def norm_backward(upstream, normal, inverse, gain):
    scaled = upstream * gain
    bracket = (
        scaled
        - jnp.mean(scaled, -1, keepdims=True)
        - normal * jnp.mean(scaled * normal, -1, keepdims=True)
    )
    return inverse * bracket, rowsum(upstream * normal), rowsum(upstream)


def rowsum(value):
    return jnp.sum(value, 0, keepdims=True)


GELU_A, GELU_B = 0.7978845608028654, 0.044715


def gelu(x):
    return 0.5 * x * (1.0 + jnp.tanh(GELU_A * (x + GELU_B * (x * x * x))))


def gelu_slope(x):
    square = x * x
    t = jnp.tanh(GELU_A * (x + GELU_B * (square * x)))
    inner = GELU_A * (1.0 + 3.0 * GELU_B * square)
    return 0.5 * (1.0 + t) + 0.5 * x * (1.0 - t * t) * inner


KEPT = ("q", "k", "v", "prob", "context", "normal1", "inverse1", "low1", "pre", "hidden", "normal2", "inverse2")


def kept_shapes(keys):
    return {
        "q": ((TOKENS, D), BF16),
        "k": ((2 * keys, D), BF16),
        "v": ((2 * keys, D), BF16),
        "prob": ((2 * PAIRS, 128, keys), F32),
        "context": ((TOKENS, D), BF16),
        "normal1": ((TOKENS, D), F32),
        "inverse1": ((TOKENS, 128), F32),
        "low1": ((TOKENS, D), BF16),
        "pre": ((TOKENS, FF), F32),
        "hidden": ((TOKENS, FF), BF16),
        "normal2": ((TOKENS, D), F32),
        "inverse2": ((TOKENS, 128), F32),
    }


def transpose_vectors(w, vt):
    w.wait(VEC)
    vt[...] = jnp.transpose(w.vec[...].astype(F32))[:16]


def layer_forward(w, kept, vt, bias, x_query, x_key, source, valid, stride, keys):
    transpose_vectors(w, vt)
    position_bias(vt[12:13, :], stride, keys, bias)
    w.wait(IN)
    query_low = x_query[...]
    kept["q"][...] = (mm(query_low, w.w_in[:, :D]) + vt[0:1, :]).astype(BF16)
    key_low = x_key[...]
    kept["k"][...] = mm(key_low, w.w_in[:, D : 2 * D]).astype(BF16)
    kept["v"][...] = (mm(key_low, w.w_in[:, 2 * D :]) + vt[1:2, :]).astype(BF16)
    for row in range(2):
        usable = iota((128, keys), 1) < valid[row]
        for pair in range(PAIRS):
            lanes = slice(128 * pair, 128 * pair + 128)
            q = by_head(kept["q"][HALF * row : HALF * (row + 1), lanes])
            k = kept["k"][keys * row : keys * (row + 1), lanes]
            scores = mm_nt(q, k) * 0.125 + bias[pair]
            scores = jnp.where(usable, scores, NEGATIVE)
            unnormed = jnp.exp(scores - jnp.max(scores, -1, keepdims=True))
            prob = unnormed / jnp.sum(unnormed, -1, keepdims=True)
            kept["prob"][PAIRS * row + pair] = prob
            v = kept["v"][keys * row : keys * (row + 1), lanes]
            context = join_heads(mm(prob.astype(BF16), v))
            kept["context"][HALF * row : HALF * (row + 1), lanes] = context.astype(BF16)
    w.wait(OUT)
    attended = mm(kept["context"][...], w.w_out[...]) + vt[2:3, :]
    normed, normal, inverse = norm_forward(source + attended, vt[3:4, :], vt[4:5, :])
    kept["normal1"][...] = normal
    kept["inverse1"][...] = jnp.broadcast_to(inverse, (TOKENS, 128))
    normed_low = normed.astype(BF16)
    kept["low1"][...] = normed_low
    w.wait(UP)
    feed = normed + vt[5:6, :]
    for c in range(4):
        lanes = slice(D * c, D * (c + 1))
        pre = mm(normed_low, w.w_up[:, lanes]) + vt[8 + c : 9 + c, :]
        kept["pre"][:, lanes] = pre
        hidden = gelu(pre).astype(BF16)
        kept["hidden"][:, lanes] = hidden
        w.wait(DOWN + c)
        feed = feed + mm(hidden, w.w_down[lanes, :])
    result, normal, inverse = norm_forward(feed, vt[6:7, :], vt[7:8, :])
    kept["normal2"][...] = normal
    kept["inverse2"][...] = jnp.broadcast_to(inverse, (TOKENS, 128))
    return result


class GradientWriter:
    SLOTS = 3

    def __init__(self, stage, sems):
        self.stage, self.sems, self.flying, self.count = stage, sems, [()] * self.SLOTS, 0

    def write(self, value, line, across, lane):
        slot = self.count % self.SLOTS
        self.count += 1
        self.wait(slot)
        width, limit = value.shape[1], line[1].shape[1]
        self.stage[slot, :, :width] = value.astype(BF16)
        self.flying[slot] = []
        split = min(max(limit - lane, 0), width)
        for k in range(4):
            if k == 0 or split == width:
                parts = [(line[k], 0, width, lane)]
            else:
                parts = [(line[k], 0, split, lane), (across[k], split, width, lane + split - limit)]
            for number, (target, start, stop, at) in enumerate(parts):
                if start == stop:
                    continue
                copy = pltpu.make_async_copy(
                    self.stage.at[slot, pl.ds(CHUNK * k, CHUNK), pl.ds(start, stop - start)],
                    target.at[:, pl.ds(at, stop - start)],
                    self.sems.at[8 * slot + 2 * k + number],
                )
                copy.start()
                self.flying[slot].append(copy)

    def wait(self, slot):
        for copy in self.flying[slot]:
            copy.wait()
        self.flying[slot] = ()

    def finish(self):
        for slot in range(self.SLOTS):
            self.wait(slot)


def turned(index, value, plain, ordered):
    width = value.shape[0]
    plain[:, :width] = jnp.transpose(value)
    for k in range(4):
        for run in range(2):
            row = run_row(index[0], lax.rem(index[1] + k, 4), run)
            at = CHUNK * k + 48 * run
            ordered[at : at + 48, :width] = plain[pl.ds(row, 48), :width]
    return ordered[:, :width]


FEED_ACTS = 2 * D + 2 * FF
ACT_ROWS = TOKENS + 16
ACT_LANES = 4 * D


def feed_gradient_kernel(index, mine, theirs, *refs):
    refs = refs[-14:]
    base, a1, a2, a3, b1, b2, b3, acts, plain, ordered, stage, sems, act_sems = refs[:13]
    line, across = (base, a1, a2, a3), (base, b1, b2, b3)
    copies = []
    for side, ref in enumerate((mine, theirs)):
        target = acts.at[pl.ds(TOKENS * side, TOKENS), :]
        copies.append(pltpu.make_async_copy(ref, target, act_sems.at[side]))
        copies[side].start()
    for copy in copies:
        copy.wait()
    writer = GradientWriter(stage, sems)
    low1 = turned(index, acts[:, :D], plain.at[4], ordered.at[4])
    for c in range(4):
        at = 2 * D + FF + D * c
        writer.write(mm(low1, acts[:, at : at + D]), line, across, D * c)
    feed_grad = acts[:, D + FF : 2 * D + FF]
    for c in range(4):
        hidden = turned(index, acts[:, D + D * c : 2 * D + D * c], plain.at[c], ordered.at[c])
        writer.write(mm(hidden, feed_grad), line, across, FF + D * c)
    writer.finish()


GRADIENT_SCRATCH = [
    pltpu.VMEM((5, 768, 512), BF16),
    pltpu.VMEM((5, 384, 512), BF16),
    pltpu.VMEM((3, 384, 768), BF16),
    pltpu.SemaphoreType.DMA((24,)),
    pltpu.SemaphoreType.DMA((4,)),
]


def feed_gradient(index, mine, theirs, after=()):
    return pl.pallas_call(
        feed_gradient_kernel,
        out_shape=[shape(CHUNK, FEED)] + [shape(CHUNK, FEED_LINE)] * 3 + [shape(CHUNK, FEED - FEED_LINE)] * 3,
        in_specs=[SMEM] + anyspace(2 + len(after)),
        out_specs=anyspace(7),
        scratch_shapes=[pltpu.VMEM((2 * TOKENS, FEED_ACTS), BF16)] + GRADIENT_SCRATCH + [pltpu.VMEM((8, 128), F32)],
        compiler_params=params(28),
        cost_estimate=cost(7),
    )(index, mine, theirs, *after)


def attention_gradient_kernel(keys, outs, index, mine, theirs, *refs):
    refs, scratch = refs[-10 - outs : -10], refs[-10:]
    queries, vectors, keyed, plain, ordered, stage, sems, act_sems, plain_vec, ordered_vec = scratch
    targets = refs[:4], (refs[0], *refs[4:])
    copies = []
    for side, ref in enumerate((mine, theirs)):
        for at, rows, target, sem in (
            (0, TOKENS, queries, act_sems.at[side]),
            (TOKENS, 16, vectors, act_sems.at[2 + side]),
            (ACT_ROWS, keys, keyed, sems.at[side]),
        ):
            lanes = target.shape[1]
            source = ref.at[pl.ds(at, rows), pl.ds(0, lanes)]
            copies.append(pltpu.make_async_copy(source, target.at[pl.ds(rows * side, rows), :], sem))
    for copy in copies:
        copy.start()
    for copy in copies:
        copy.wait()
    writer = GradientWriter(stage, sems)
    context = turned(index, queries[:, :D], plain.at[0], ordered.at[0])
    writer.write(mm(context, queries[:, D : 2 * D]), *targets, OUT_AT)
    query_rows = turned(index, queries[:, 2 * D : 3 * D], plain.at[1], ordered.at[1])
    writer.write(mm(query_rows, queries[:, 3 * D :]), *targets, 0)
    key_rows = turned(index, keyed[:, :D], plain.at[2], ordered.at[2])
    writer.write(mm(key_rows, keyed[:, D : 2 * D]), *targets, D)
    writer.write(mm(key_rows, keyed[:, 2 * D :]), *targets, 2 * D)
    rows = wide(vectors[:16, :]) + wide(vectors[16:, :])
    rows = jnp.concatenate([rows, jnp.zeros((112, D), F32)], 0)
    plain_vec[...] = jnp.transpose(rows)
    for k in range(4):
        for run in range(2):
            row = run_row(index[0], lax.rem(index[1] + k, 4), run)
            at = CHUNK * k + 48 * run
            ordered_vec[at : at + 48, :] = plain_vec[pl.ds(row, 48), :]
    writer.write(ordered_vec[...], *targets, VEC_AT)
    writer.finish()


def attention_gradient(index, mine, theirs, after=()):
    out = [shape(CHUNK, ATTN)] * 4
    keys = mine.shape[0] - ACT_ROWS
    scratch = [
        pltpu.VMEM((2 * TOKENS, ACT_LANES), BF16),
        pltpu.VMEM((32, D), BF16),
        pltpu.VMEM((2 * keys, 3 * D), BF16),
    ]
    vectors = [pltpu.VMEM((768, 128), F32), pltpu.VMEM((384, 128), F32)]
    return pl.pallas_call(
        functools.partial(attention_gradient_kernel, keys, len(out)),
        out_shape=out,
        in_specs=[SMEM] + anyspace(2 + len(after)),
        out_specs=anyspace(len(out)),
        scratch_shapes=scratch + GRADIENT_SCRATCH + vectors,
        compiler_params=params(28),
        cost_estimate=cost(5),
    )(index, mine, theirs, *after)


def feed_backward(w, kept, vt, upstream, acts):
    dsum2, gain2, shift2 = norm_backward(
        upstream, kept["normal2"][...], kept["inverse2"][:, :1], vt[6:7, :]
    )
    feed_grad = dsum2.astype(BF16)
    acts[:, D + FF : 2 * D + FF] = feed_grad
    down_bias = rowsum(wide(feed_grad))
    normed_grad = dsum2
    hidden_bias = []
    for c in range(4):
        lanes = slice(D * c, D * (c + 1))
        w.wait(DOWN + c)
        hidden_grad = mm_nt(feed_grad, w.w_down[lanes, :])
        pre_grad = (gelu_slope(kept["pre"][:, lanes]) * hidden_grad).astype(BF16)
        at = 2 * D + FF + D * c
        acts[:, at : at + D] = pre_grad
        hidden_bias.append(rowsum(wide(pre_grad)))
        if c == 0:
            w.wait(UP)
        normed_grad = normed_grad + mm_nt(pre_grad, w.w_up[:, lanes])
    acts[:, :D] = kept["low1"][...]
    acts[:, D : D + FF] = kept["hidden"][...]
    zero = jnp.zeros((1, D), F32)
    rows = [zero] * 5 + [down_bias, gain2, shift2] + hidden_bias + [zero] * 4
    return normed_grad, jnp.concatenate(rows, 0)


def attention_backward(
    w, kept, vt, x_query, x_key, normed_grad, vector_rows, stride, keys, acts, work
):
    dq, dk, dv, table = work
    dsum1, gain1, shift1 = norm_backward(
        normed_grad, kept["normal1"][...], kept["inverse1"][:, :1], vt[3:4, :]
    )
    attended_grad = dsum1.astype(BF16)
    out_bias = rowsum(wide(attended_grad))
    acts[:TOKENS, :D] = kept["context"][...]
    acts[:TOKENS, D : 2 * D] = attended_grad
    acts[:TOKENS, 2 * D : 3 * D] = x_query[...]
    w.wait(OUT)
    context_grad = mm_nt(attended_grad, w.w_out[...]).astype(BF16)
    table[...] = jnp.zeros((16, WRAP), F32)
    mirror = (2 * keys, WRAP)
    mirror = onehot(lax.rem(lax.rem(iota(mirror, 0), keys) + iota(mirror, 1), WRAP) == 0)
    for pair in range(PAIRS):
        lanes = slice(128 * pair, 128 * pair + 128)
        pair_scores = []
        for row in range(2):
            here = slice(HALF * row, HALF * (row + 1))
            there = slice(keys * row, keys * (row + 1))
            grad = by_head(context_grad[here, lanes])
            prob = kept["prob"][PAIRS * row + pair]
            v = kept["v"][there, lanes]
            prob_grad = mm_nt(grad, v)
            dv[there, lanes] = mm_tn(prob.astype(BF16), grad).astype(BF16)
            score = prob * (prob_grad - jnp.sum(prob_grad * prob, -1, keepdims=True))
            score = score.astype(BF16)
            q = by_head(kept["q"][here, lanes])
            k = kept["k"][there, lanes]
            dq[here, lanes] = (0.125 * join_heads(mm(score, k))).astype(BF16)
            dk[there, lanes] = (0.125 * mm_tn(score, q)).astype(BF16)
            pair_scores.append(score)
        spread = mm(jnp.concatenate(pair_scores, 1), mirror)
        for half in range(2):
            rolled = pltpu.roll(
                spread[HALF * half : HALF * (half + 1)], 0, 1, stride=stride, stride_axis=0
            )
            table[2 * pair + half : 2 * pair + half + 1, :] = rowsum(rolled)
    dq_low, dk_low, dv_low = dq[...], dk[...], dv[...]
    w.wait(IN)
    source_grad = dsum1 + mm_nt(dq_low, w.w_in[:, :D])
    key_side = mm_nt(dk_low, w.w_in[:, D : 2 * D]) + mm_nt(dv_low, w.w_in[:, 2 * D :])
    acts[:TOKENS, 3 * D :] = dq_low
    acts[ACT_ROWS:, :D] = x_key[...]
    acts[ACT_ROWS:, D : 2 * D] = dk_low
    acts[ACT_ROWS:, 2 * D : 3 * D] = dv_low
    buckets = lax.dot_general(
        table[...],
        bucket_rows(-1).astype(F32),
        (((1,), (1,)), ((), ())),
        precision=lax.Precision.HIGHEST,
        preferred_element_type=F32,
    )
    table_grad = rowsum(jnp.where(head_mask(), buckets, 0.0))
    rows = [rowsum(wide(dq_low)), rowsum(wide(dv_low)), out_bias, gain1, shift1]
    rows += [vector_rows[5:12, :], table_grad, jnp.zeros((3, D), F32)]
    acts[TOKENS:ACT_ROWS, :D] = jnp.concatenate(rows, 0).astype(BF16)
    return source_grad, key_side


FOR_ATTENTION = ("q", "k", "v", "prob", "context", "normal1", "inverse1")
FOR_FEED = ("low1", "pre", "hidden", "normal2", "inverse2")


def pooling():
    return 0.5 * (iota((TOKENS, 2 * SEQ), 1) // 2 == iota((TOKENS, 2 * SEQ), 0)).astype(F32)


def one_forward_kernel(index, tokens, *refs):
    chunks = refs[:15]
    middle, pooled_low, *refs = refs[-22:]
    kept = dict(zip(KEPT, refs[:12]))
    vt, bias, *scratch = refs[12:]
    w = Weights(index, chunks, scratch[:5], scratch[5])
    w.start(range(8))
    pooled = mm(pooling().astype(BF16), tokens[...])
    pooled_low[...] = pooled.astype(BF16)
    valid = [index[5], index[6]]
    middle[...] = layer_forward(w, kept, vt, bias, pooled_low, tokens, pooled, valid, 2, SEQ)


def one_forward(index, tokens, chunks, after):
    kept = [shape(*dims, dtype=dtype) for dims, dtype in kept_shapes(SEQ).values()]
    return pl.pallas_call(
        one_forward_kernel,
        out_shape=[shape(TOKENS, D, dtype=F32), shape(TOKENS, D)] + kept,
        in_specs=[SMEM] + vmem(1) + anyspace(15 + len(after)),
        out_specs=vmem(14),
        scratch_shapes=[pltpu.VMEM((16, D), F32), pltpu.VMEM((PAIRS, 128, SEQ), F32)] + WEIGHT_SCRATCH,
        compiler_params=params(),
        cost_estimate=cost(13),
    )(index, tokens, *chunks, *after)


def two_forward_kernel(index, middle, cotangent, *refs):
    chunks, refs = refs[:15], refs[15:]
    result, normed_grad, vector_rows, acts = refs[:4]
    kept = dict(zip(FOR_ATTENTION + FOR_FEED, refs[4:16]))
    vt, bias, middle_low, *scratch = refs[16:]
    w = Weights(index, chunks, scratch[:5], scratch[5])
    w.start(range(8))
    middle_low[...] = middle[...].astype(BF16)
    valid = [(index[5] + 1) // 2, (index[6] + 1) // 2]
    out = layer_forward(w, kept, vt, bias, middle_low, middle_low, middle[...], valid, 1, HALF)
    result[...] = out.astype(BF16)
    w.wait = lambda *groups: None
    normed_grad[...], vector_rows[...] = feed_backward(w, kept, vt, cotangent[...], acts)


def two_forward(index, middle, cotangent, chunks):
    dims = kept_shapes(HALF)
    kept = [shape(*dims[name][0], dtype=dims[name][1]) for name in FOR_ATTENTION]
    scratch = [pltpu.VMEM(*dims[name]) for name in FOR_FEED]
    out = [shape(TOKENS, D), shape(TOKENS, D, dtype=F32), shape(16, D, dtype=F32)]
    outs = pl.pallas_call(
        two_forward_kernel,
        out_shape=out + [shape(TOKENS, FEED_ACTS)] + kept,
        in_specs=[SMEM] + vmem(2) + anyspace(15),
        out_specs=vmem(11),
        scratch_shapes=scratch
        + [pltpu.VMEM((16, D), F32), pltpu.VMEM((PAIRS, 128, HALF), F32), pltpu.VMEM((TOKENS, D), BF16)]
        + WEIGHT_SCRATCH,
        compiler_params=params(),
        cost_estimate=cost(17),
    )(index, middle, cotangent, *chunks)
    return outs[:3], outs[3], outs[4:]


def two_backward_kernel(index, middle, normed_grad, vector_rows, *refs):
    kept = dict(zip(FOR_ATTENTION, refs[:7]))
    chunks, refs = refs[7:22], refs[22:]
    upstream, acts, vt, middle_low, *work = refs[:8]
    scratch = refs[8:]
    w = Weights(index, chunks, scratch[:5], scratch[5])
    w.start((VEC, OUT, IN))
    middle_low[...] = middle[...].astype(BF16)
    transpose_vectors(w, vt)
    source_grad, key_side = attention_backward(
        w, kept, vt, middle_low, middle_low, normed_grad[...], vector_rows, 1, HALF, acts, work
    )
    upstream[...] = source_grad + key_side


def two_backward(index, middle, normed_grad, vector_rows, kept, chunks):
    return pl.pallas_call(
        two_backward_kernel,
        out_shape=[shape(TOKENS, D, dtype=F32), shape(ACT_ROWS + TOKENS, ACT_LANES)],
        in_specs=[SMEM] + vmem(10) + anyspace(15),
        out_specs=vmem(2),
        scratch_shapes=[pltpu.VMEM((16, D), F32)]
        + [pltpu.VMEM((TOKENS, D), BF16)] * 4
        + [pltpu.VMEM((16, WRAP), F32)]
        + WEIGHT_SCRATCH,
        compiler_params=params(),
        cost_estimate=cost(10),
    )(index, middle, normed_grad, vector_rows, *kept, *chunks)


def one_feed_kernel(index, upstream, *refs):
    kept = dict(zip(FOR_FEED, refs[:5]))
    chunks = refs[5:20]
    normed_grad, vector_rows, acts, vt, *scratch = refs[-10:]
    w = Weights(index, chunks, scratch[:5], scratch[5])
    w.start((VEC, DOWN, DOWN + 1, DOWN + 2, DOWN + 3, UP))
    transpose_vectors(w, vt)
    normed_grad[...], vector_rows[...] = feed_backward(w, kept, vt, upstream[...], acts)


def one_feed(index, upstream, kept, chunks, after):
    normed_grad, vector_rows, acts = pl.pallas_call(
        one_feed_kernel,
        out_shape=[shape(TOKENS, D, dtype=F32), shape(16, D, dtype=F32), shape(TOKENS, FEED_ACTS)],
        in_specs=[SMEM] + vmem(6) + anyspace(15 + len(after)),
        out_specs=vmem(3),
        scratch_shapes=[pltpu.VMEM((16, D), F32)] + WEIGHT_SCRATCH,
        compiler_params=params(),
        cost_estimate=cost(9),
    )(index, upstream, *kept, *chunks, *after)
    return (normed_grad, vector_rows), acts


def one_backward_kernel(index, tokens, pooled_low, normed_grad, vector_rows, *refs):
    kept = dict(zip(FOR_ATTENTION, refs[:7]))
    chunks = refs[7:22]
    input_grad, acts, vt, *refs = refs[-13:]
    work, scratch = refs[:4], refs[4:]
    w = Weights(index, chunks, scratch[:5], scratch[5])
    w.start((VEC, OUT, IN))
    transpose_vectors(w, vt)
    source_grad, key_side = attention_backward(
        w, kept, vt, pooled_low, tokens, normed_grad[...], vector_rows, 2, SEQ, acts, work
    )
    repeated = lax.dot_general(
        pooling(),
        source_grad,
        (((0,), (0,)), ((), ())),
        precision=lax.Precision.HIGHEST,
        preferred_element_type=F32,
    )
    input_grad[...] = key_side + repeated


def one_backward(index, tokens, pooled_low, normed_grad, vector_rows, kept, chunks, after):
    return pl.pallas_call(
        one_backward_kernel,
        out_shape=[shape(2 * SEQ, D, dtype=F32), shape(ACT_ROWS + 2 * SEQ, ACT_LANES)],
        in_specs=[SMEM] + vmem(11) + anyspace(15 + len(after)),
        out_specs=vmem(2),
        scratch_shapes=[pltpu.VMEM((16, D), F32), pltpu.VMEM((TOKENS, D), BF16)]
        + [pltpu.VMEM((2 * SEQ, D), BF16)] * 2
        + [pltpu.VMEM((16, WRAP), F32)]
        + WEIGHT_SCRATCH,
        compiler_params=params(),
        cost_estimate=cost(13),
    )(index, tokens, pooled_low, normed_grad, vector_rows, *kept, *chunks, *after)


def local(inputs, lengths, cotangent, *weights):
    device = lax.axis_index("dp") * 32 + lax.axis_index("shard")
    sources = lax.dynamic_index_in_dim(jnp.array(spread_sources(), jnp.int32), device, 0, False)
    scalars = [*place_scalars(), lengths[0, 0], lengths[1, 0], jnp.zeros((), jnp.int32)]
    index = jnp.concatenate([jnp.stack(scalars), sources])
    tokens = inputs.reshape(2 * SEQ, D)

    blob = prepare((weights[:5], weights[5:]))
    line = widen(index, [permute(blob, spread_pairs(k)) for k in range(4)])
    parts = [line] + [permute(line, line_pairs(-k)) for k in (1, 2, 3)]
    gather_one = Gather(widen_more(0, index, parts))
    chunk_two = widen_more(1, index, parts, (gather_one.near[0],))
    one = gather_one.finish()
    gather_two = Gather(chunk_two, one[2], one[9])
    middle, pooled_low, *kept = one_forward(index, tokens, one, (gather_two.own_swap,))
    kept = dict(zip(KEPT, kept))
    two = gather_two.finish(middle)

    (result, *back_two), acts_feed, kept_two = two_forward(
        index, middle, cotangent.reshape(TOKENS, D), two
    )
    acts_feed = acts_feed, permute(acts_feed, SWAP)
    upstream, acts_attn = two_backward(index, middle, *back_two, kept_two, two)
    acts_attn = acts_attn, permute(tie(acts_attn, acts_feed[1]), SWAP)

    feed_two = feed_gradient(index, *acts_feed, (upstream,))
    near_feed_two = send_near(feed_two)
    back_one, acts_feed = one_feed(
        index, upstream, [kept[name] for name in FOR_FEED], one, (feed_two[0],)
    )
    acts_feed = acts_feed, permute(tie(acts_feed, *near_feed_two), SWAP)
    attn_two = attention_gradient(index, *acts_attn, (back_one[0], *near_feed_two))
    far_feed_two = send_far(feed_two, *near_feed_two, attn_two[0])
    near_attn_two = send_near(attn_two)
    feed_one = feed_gradient(index, *acts_feed, (attn_two[0],))
    sent = (*far_feed_two, *near_attn_two, feed_one[0])
    far_attn_two = send_far(attn_two, *sent)
    near_feed_one = send_near(feed_one, *sent)
    input_grad, acts_attn = one_backward(
        index,
        tokens,
        pooled_low,
        *back_one,
        [kept[name] for name in FOR_ATTENTION],
        one,
        sent,
    )
    acts_attn = acts_attn, permute(tie(acts_attn, *near_feed_one, *far_attn_two), SWAP)
    far_feed_one = send_far(feed_one, *near_feed_one, *far_attn_two)
    pieces = narrow(WIDTH + ATTN, index, received(feed_two, near_feed_two, far_feed_two))
    attn_one = attention_gradient(index, *acts_attn, (pieces[0],))
    near_attn_one = send_near(attn_one, *far_feed_one)
    far_attn_one = send_far(attn_one, *far_feed_one)

    pieces = narrow(WIDTH, index, received(attn_two, near_attn_two, far_attn_two), pieces)
    pieces = narrow(ATTN, index, received(feed_one, near_feed_one, far_feed_one), pieces)
    pieces = narrow(0, index, received(attn_one, near_attn_one, far_attn_one), pieces)
    pieces = [pieces[0]] + [permute(pieces[k], line_pairs(k)) for k in (1, 2, 3)]
    pieces = narrow_more(index, pieces)
    grads = finish([permute(pieces[k], back(spread_pairs(k))) for k in range(4)])
    return (
        result.reshape(2, 1, HALF, D),
        input_grad.reshape(2, 1, SEQ, D),
        *grads,
    )


def solution(mesh):
    rows = P(None, AXES, None, None)
    shard = P(AXES, None)
    return jax.shard_map(
        local,
        mesh=mesh,
        in_specs=(rows, P(None, AXES), rows) + (shard,) * 10,
        out_specs=(rows, rows) + (shard,) * 10,
        check_vma=False,
    )
```

```python
import functools
import itertools

import jax
import jax.numpy as jnp
from jax import lax
from jax.experimental import pallas as pl
from jax.experimental.pallas import tpu as pltpu
from jax.sharding import PartitionSpec as P

AXES = ("dp", "shard")
F32, BF16 = jnp.float32, jnp.bfloat16
D, HEADS, HEAD_DIM, FF, BUCKETS = 768, 12, 64, 3072, 64
SEQ, HALF, TOKENS = 128, 64, 128
PAIRS = HEADS // 2
EPSILON = 1e-06
NEGATIVE = -1000000000.0
WRAP = 256

ROW = 6
CHUNK = 96
OUT_AT, VEC_AT, UP_AT, DOWN_AT, WIDTH = 2304, 3072, 3200, 6272, 9344
A_WIDTH, B_WIDTH = DOWN_AT, WIDTH - DOWN_AT
PACKED = 4736
ATTN, FEED = UP_AT, WIDTH - UP_AT
FEED_LINE = 4096


def place(core, block, v2, v1):
    z = (block - v1) % 4
    x, y = (v1, v2) if core == 0 else (v2, v1)
    return ((x * 4 + y) * 4 + z) * 2 + core


def virtual(device):
    x, y, z, half = device // 32, device // 8 % 4, device // 2 % 4, device % 2
    if y % 2 == 0:
        return 0, x, y + half, z
    return 1, x % 2 + 2 * (y // 2), (x + half) % 4, z


def latin_squares():
    rows = list(itertools.permutations(range(4)))
    found = []
    for three in itertools.product(rows, repeat=3):
        if all(len({row[i] for row in three}) == 3 for i in range(4)):
            found.append((*three, tuple(6 - sum(row[i] for row in three) for i in range(4))))
    return found


CHOSEN = (37, 82, 157, 37, 214, 52, 174, 394, 384, 493, 432, 70, 186, 264, 256, 523, 141, 364, 399, 489, 205, 175, 408, 508, 390, 358, 335, 34, 286, 179, 230, 263)
SQUARES = [latin_squares()[number] for number in CHOSEN]


def square_of(core, block, v2):
    return SQUARES[16 * core + 4 * block + v2]


def spread_pairs(number):
    pairs = []
    for f in range(128):
        core, block, v2, j = virtual(f)
        v1 = square_of(core, block, v2)[j].index(number)
        pairs.append((f, place(core, block, v2, v1)))
    return pairs


def spread_sources():
    table = [None] * 128
    for v in range(128):
        core, block, v2, v1 = v // 64, v // 16 % 4, v // 4 % 4, v % 4
        column = [row[v1] for row in square_of(core, block, v2)]
        table[place(core, block, v2, v1)] = [column.index(number) for number in range(4)]
    return table


def line_pairs(step):
    pairs = []
    for v in range(128):
        core, block, v2, v1 = v // 64, v // 16 % 4, v // 4 % 4, v % 4
        pairs.append((place(core, block, v2, v1), place(core, block, (v2 + step) % 4, v1)))
    return pairs


def run_row(core, block, run):
    even = 192 * block + 96 * run
    odd = 192 * lax.rem(block, 2) + 384 * run + 48 + 96 * (block // 2)
    return pl.multiple_of(jnp.where(core == 0, even, odd), 16)


def along(axis_of_core, step):
    pairs = []
    for f in range(128):
        at = [f // 32, f // 8 % 4, f // 2 % 4]
        axis = axis_of_core[f % 2]
        at[axis] = (at[axis] + step) % 4
        pairs.append((f, ((at[0] * 4 + at[1]) * 4 + at[2]) * 2 + f % 2))
    return pairs


A_AXES, B_AXES = (0, 1), (2, 2)
SWAP = [(f, f ^ 1) for f in range(128)]


def permute(value, pairs):
    return lax.ppermute(value, AXES, pairs)


def back(pairs):
    return [(b, a) for a, b in pairs]


def place_scalars():
    x, inner = lax.axis_index("dp"), lax.axis_index("shard")
    y, z, core = inner // 8, inner // 2 % 4, inner % 2
    first = core == 0
    block = jnp.where(first, x + z, y + z) % 4
    other = jnp.where(first, y + z, x + z) % 4
    v2, v1 = jnp.where(first, y, x), jnp.where(first, x, y)
    return [core, block, other, v2, v1]


def mm(a, b):
    return lax.dot_general(a, b, (((1,), (0,)), ((), ())), preferred_element_type=F32)


def mm_nt(a, b):
    return lax.dot_general(a, b, (((1,), (1,)), ((), ())), preferred_element_type=F32)


def mm_tn(a, b):
    return lax.dot_general(a, b, (((0,), (0,)), ((), ())), preferred_element_type=F32)


def exact(a, b):
    return lax.dot_general(
        a, b, (((1,), (0,)), ((), ())), precision=lax.Precision.HIGHEST, preferred_element_type=F32
    )


def iota(shape, axis):
    return lax.broadcasted_iota(jnp.int32, shape, axis)


def onehot(condition):
    return condition.astype(F32).astype(BF16)


def split_hidden():
    source, out = iota((512, 512), 0), iota((512, 512), 1)
    return onehot((source // 4 == out % 128) & (source % 4 == out // 128))


def vmem(n):
    return [pl.BlockSpec(memory_space=pltpu.VMEM)] * n


def anyspace(n):
    return [pl.BlockSpec(memory_space=pl.ANY)] * n


SMEM = pl.BlockSpec(memory_space=pltpu.SMEM)


def params(mebibytes=56):
    return pltpu.CompilerParams(vmem_limit_bytes=mebibytes * 1024 * 1024)


def cost(microseconds):
    return pl.CostEstimate(flops=0, bytes_accessed=int(microseconds * 3.5e6), transcendentals=0)


def shape(*dims, dtype=BF16):
    return jax.ShapeDtypeStruct(dims, dtype)


def prepare_kernel(*refs):
    shards, packed, out = refs[:10], refs[10], refs[11]
    pad = onehot(iota((8, ROW), 0) == iota((8, ROW), 1))
    split = split_hidden()
    for layer in range(2):
        proj_in, proj_out, up, down, vectors = shards[5 * layer : 5 * layer + 5]
        at = 2 * PACKED * layer
        out[:, at : at + OUT_AT] = mm(pad, proj_in[...]).astype(BF16)
        out[:, at + OUT_AT : at + VEC_AT] = mm(pad, proj_out[...]).astype(BF16)
        for group in range(6):
            part = mm(pad, up[:, 512 * group : 512 * group + 512]).astype(BF16)
            part = mm(part, split).astype(BF16)
            for c in range(4):
                lane = at + UP_AT + 768 * c + 128 * group
                out[:, lane : lane + 128] = part[:, 128 * c : 128 * c + 128]
        out[:, at + VEC_AT : at + UP_AT] = jnp.zeros((8, 128), BF16)
        out[:, at + VEC_AT : at + VEC_AT + 13] = mm(pad, vectors[...]).astype(BF16)
        for c in range(4):
            rows = onehot(iota((8, 24), 1) == 4 * iota((8, 24), 0) + c)
            lane = at + DOWN_AT + 768 * c
            out[:, lane : lane + 768] = mm(rows, down[...]).astype(BF16)
        out[:, at + WIDTH : at + 2 * PACKED] = jnp.zeros((8, 2 * PACKED - WIDTH), BF16)
    total = None
    for quarter in range(4):
        rows = onehot((iota((24, 8), 0) - ROW * quarter == iota((24, 8), 1)) & (iota((24, 8), 1) < ROW))
        piece = mm(rows, out[:, PACKED * quarter : PACKED * (quarter + 1)])
        total = piece if total is None else total + piece
    packed[...] = total.astype(BF16)


def prepare(shards):
    return pl.pallas_call(
        prepare_kernel,
        out_shape=shape(24, PACKED),
        in_specs=vmem(10),
        out_specs=vmem(1)[0],
        scratch_shapes=[pltpu.VMEM((8, 4 * PACKED), BF16)],
        compiler_params=params(),
        cost_estimate=cost(4),
    )(*shards[0], *shards[1])


def block_at(digit, quarter):
    wanted, source = iota((24, 24), 0) - ROW * digit, iota((24, 24), 1)
    return onehot((wanted >= 0) & (wanted < ROW) & (wanted + ROW * quarter == source))


def widen_kernel(index, *refs):
    parts, out = refs[:4], refs[4]
    for quarter in range(4):
        layer, half = quarter // 2, quarter % 2
        width = WIDTH - PACKED if half else PACKED
        total = None
        for k in range(4):
            piece = mm(block_at(index[8 + k], quarter), parts[k][:, :width])
            total = piece if total is None else total + piece
        at = WIDTH * layer + PACKED * half
        out[:, at : at + width] = total.astype(BF16)


def widen(index, parts):
    return pl.pallas_call(
        widen_kernel,
        out_shape=shape(24, 2 * WIDTH),
        in_specs=[SMEM] + vmem(4),
        out_specs=vmem(1)[0],
        compiler_params=params(24),
        cost_estimate=cost(4),
    )(index, *parts)


def line_block(index, k):
    v2 = lax.rem(index[3] + k, 4)
    first = jnp.where(index[0] == 0, 0, lax.rem(index[1], 2))
    unit = lax.rem(v2 - first + 4, 4)
    row, source = iota((CHUNK, 24), 0), iota((CHUNK, 24), 1)
    here = (row // 48 == unit // 2) & (row % 12 // 6 == lax.rem(unit, 2))
    return onehot(here & (source == row % 48 // 12 * 6 + row % 6))


def widen_more_kernel(layer, index, *refs):
    parts, (out_a, out_b, both) = refs[:4], refs[-3:]
    places = [line_block(index, k) for k in range(4)]
    for out, start, width in ((out_a, 0, A_WIDTH), (out_b, A_WIDTH, B_WIDTH)):
        total = None
        for k in range(4):
            at = WIDTH * layer + start
            piece = mm(places[k], parts[k][:, at : at + width])
            total = piece if total is None else total + piece
        total = total.astype(BF16)
        out[...] = total
        both[:, start : start + width] = total


def widen_more(layer, index, parts, after=()):
    return pl.pallas_call(
        functools.partial(widen_more_kernel, layer),
        out_shape=[shape(CHUNK, A_WIDTH), shape(CHUNK, B_WIDTH), shape(CHUNK, WIDTH)],
        in_specs=[SMEM] + vmem(4) + anyspace(len(after)),
        out_specs=vmem(3),
        compiler_params=params(24),
        cost_estimate=cost(5),
    )(index, *parts, *after)


def tie(value, *before):
    return lax.optimization_barrier((value, *before))[0]


class Gather:
    def __init__(self, chunk, *before):
        self.a, self.b, both = lax.optimization_barrier((*chunk, *before))[:3]
        self.own_swap = permute(both, SWAP)
        self.near = [permute(self.a, along(A_AXES, -k)) for k in (1, 3)]
        self.near += [permute(self.b, along(B_AXES, -k)) for k in (1, 3)]

    def finish(self, *before):
        far_a, far_b, *near = lax.optimization_barrier(
            (self.a, self.b, *self.near, self.own_swap, *before)
        )
        far = [permute(far_a, along(A_AXES, -2)), permute(far_b, along(B_AXES, -2))]
        swapped = [None, None, permute(near[2], SWAP), permute(near[3], SWAP)]
        for k in range(2):
            swapped[k] = permute(tie(near[k], swapped[k + 2]), SWAP)
        far_a, far_b, *_ = lax.optimization_barrier((*far, *swapped))
        far_swapped = [permute(far_a, SWAP), permute(far_b, SWAP)]
        return [
            *(self.a, self.near[0], far[0], self.near[1]),
            *(swapped[0], far_swapped[0], swapped[1]),
            *(self.b, self.near[2], far[1], self.near[3]),
            *(swapped[2], far_swapped[1], swapped[3]),
            self.own_swap,
        ]


def narrow_kernel(at, count, index, *refs):
    base, *got = refs[:count]
    *outs, stage, sems = refs[-6:]
    places = [line_block(index, k) for k in range(4)]
    width, line = base.shape[1], got[0].shape[1]
    for start, stop, pieces in ((0, line, got[:3]), (line, width, got[3:])):
        if start == stop:
            continue
        one, two, three = [wide(piece[...]) for piece in pieces]
        total = ((wide(base[:, start:stop]) + one) + (two + three)).astype(BF16)
        for k in range(4):
            stage[k, :, start:stop] = mm_tn(places[k], total).astype(BF16)
    copies = []
    for k in range(4):
        copies.append(
            pltpu.make_async_copy(stage.at[k], outs[k].at[:, pl.ds(at, width)], sems.at[k])
        )
        copies[k].start()
    for copy in copies:
        copy.wait()


def narrow(at, index, unit, onto=()):
    width, count = unit[0].shape[1], len(unit)
    return pl.pallas_call(
        functools.partial(narrow_kernel, at, count),
        out_shape=[shape(24, 2 * WIDTH)] * 4,
        in_specs=[SMEM] + vmem(count) + anyspace(len(onto)),
        out_specs=anyspace(4),
        scratch_shapes=[pltpu.VMEM((4, 24, width), BF16), pltpu.SemaphoreType.DMA((4,))],
        input_output_aliases={1 + count + k: k for k in range(len(onto))},
        compiler_params=params(24),
        cost_estimate=cost(4),
    )(index, *unit, *onto)


def wide(value):
    return value.astype(F32)


def narrow_more_kernel(index, *refs):
    parts, outs, held = refs[:4], refs[4:8], refs[8]
    split = split_hidden()
    for layer in range(2):
        at, to = WIDTH * layer, 2 * PACKED * layer
        one, two, three, four = [wide(part[:, at : at + WIDTH]) for part in parts]
        total = ((one + two) + (three + four)).astype(BF16)
        held[:, to : to + UP_AT] = total[:, :UP_AT]
        for group in range(6):
            lanes = [UP_AT + 768 * c + 128 * group for c in range(4)]
            part = jnp.concatenate([total[:, lane : lane + 128] for lane in lanes], 1)
            lane = to + UP_AT + 512 * group
            held[:, lane : lane + 512] = mm_nt(part, split).astype(BF16)
        held[:, to + DOWN_AT : to + WIDTH] = total[:, DOWN_AT:]
        held[:, to + WIDTH : to + 2 * PACKED] = jnp.zeros((24, 2 * PACKED - WIDTH), BF16)
    for k in range(4):
        total = None
        for quarter in range(4):
            lanes = held[:, PACKED * quarter : PACKED * (quarter + 1)]
            piece = mm_tn(block_at(index[8 + k], quarter), lanes)
            total = piece if total is None else total + piece
        outs[k][...] = total.astype(BF16)


def narrow_more(index, parts):
    return pl.pallas_call(
        narrow_more_kernel,
        out_shape=[shape(24, PACKED)] * 4,
        in_specs=[SMEM] + vmem(4),
        out_specs=vmem(4),
        scratch_shapes=[pltpu.VMEM((24, 4 * PACKED), BF16)],
        compiler_params=params(24),
        cost_estimate=cost(6),
    )(index, *parts)


def finish_kernel(*refs):
    (one, two, three, four), outs = [wide(ref[...]) for ref in refs[:4]], refs[4:]
    total = (one + two) + (three + four)
    for layer in range(2):
        proj_in, proj_out, up, down, vectors = outs[5 * layer : 5 * layer + 5]
        first, second = [total[ROW * q : ROW * (q + 1)] for q in (2 * layer, 2 * layer + 1)]
        proj_in[...] = first[:, :OUT_AT]
        proj_out[...] = first[:, OUT_AT:VEC_AT]
        vectors[...] = first[:, VEC_AT : VEC_AT + 13]
        up[:, : PACKED - UP_AT] = first[:, UP_AT:]
        up[:, PACKED - UP_AT :] = second[:, : DOWN_AT - PACKED]
        rows = None
        for c in range(4):
            place_rows = (iota((24, ROW), 0) == 4 * iota((24, ROW), 1) + c).astype(F32)
            lane = DOWN_AT - PACKED + 768 * c
            piece = exact(place_rows, second[:, lane : lane + 768])
            rows = piece if rows is None else rows + piece
        down[...] = rows


def finish(parts):
    one = [shape(ROW, n, dtype=F32) for n in (2304, 768, 3072)]
    one += [shape(24, 768, dtype=F32), shape(ROW, 13, dtype=F32)]
    return pl.pallas_call(
        finish_kernel,
        out_shape=one + one,
        in_specs=vmem(4),
        out_specs=vmem(10),
        compiler_params=params(24),
        cost_estimate=cost(4),
    )(*parts)


def send_sums(parts, axes, steps, *before):
    parts = [parts[k - 1] for k in steps]
    if before:
        parts = lax.optimization_barrier((*parts, *before))[: len(steps)]
    return [permute(part, along(axes, k)) for part, k in zip(parts, steps)]


def send_near(sums, *before):
    near = send_sums(sums[1:4], A_AXES, (1, 3), *before)
    return near + (send_sums(sums[4:7], B_AXES, (1, 3), *before) if len(sums) > 4 else [])


def send_far(sums, *before):
    far = send_sums(sums[1:4], A_AXES, (2,), *before)
    return far + (send_sums(sums[4:7], B_AXES, (2,), *before) if len(sums) > 4 else [])


def received(sums, near, far):
    got = [sums[0], near[0], near[1], far[0]]
    return got + [near[2], near[3], far[1]] if len(sums) > 4 else got


class Weights:
    def __init__(self, index, chunks, scratch, sems):
        attention, self.w_up, self.w_down = scratch
        self.w_in = attention.at[:, pl.ds(0, OUT_AT)]
        self.w_out = attention.at[:, pl.ds(OUT_AT, D)]
        self.vec = attention.at[:, pl.ds(VEC_AT, 128)]
        own_a, other_a, own_b, other_b = chunks[:4], chunks[4:7], chunks[7:11], chunks[11:14]
        joined = chunks[14]
        other_a = [joined.at[:, :A_WIDTH], *other_a]
        other_b = [joined.at[:, A_WIDTH:WIDTH], *other_b]
        self.copies, self.flying = [[] for _ in range(4)], [[] for _ in range(4)]
        for side in range(2):
            core = index[0] if side == 0 else 1 - index[0]
            first = index[1] if side == 0 else index[2]
            a_refs, b_refs = ((own_a, own_b), (other_a, other_b))[side]
            for k in range(4):
                block = lax.rem(first + k, 4)
                for run in range(2):
                    row = run_row(core, block, run)
                    rows = pl.ds(48 * run, 48)
                    a, b = a_refs[k], b_refs[k]
                    targets = [
                        (a, VEC_AT, 128, attention, VEC_AT),
                        (a, 0, UP_AT, attention, 0),
                        (a, UP_AT, FF, self.w_up, 0),
                        (b, 0, FF, self.w_down, 0),
                    ]
                    for group, (ref, lane, width, out, at) in enumerate(targets):
                        self.copies[group].append(
                            (
                                ref.at[rows, pl.ds(lane, width)],
                                out.at[pl.ds(row, 48), pl.ds(at, width)],
                                sems.at[group, 8 * side + 2 * k + run],
                            )
                        )

    def start(self, groups):
        for group in groups:
            self.flying[group] = [pltpu.make_async_copy(*copy) for copy in self.copies[group]]
            for copy in self.flying[group]:
                copy.start()

    def wait(self, *groups):
        for group in groups:
            for copy in self.flying[group]:
                copy.wait()
            self.flying[group] = []


VEC, ATTENTION, UP, DOWN = 0, 1, 2, 3
WEIGHT_SCRATCH = [
    pltpu.VMEM((768, ATTN), BF16),
    pltpu.VMEM((768, FF), BF16),
    pltpu.VMEM((768, FF), BF16),
    pltpu.SemaphoreType.DMA((4, 16)),
]


def bucket_rows(sign=1):
    lane = iota((D, WRAP), 1)
    lane = lane if sign > 0 else lax.rem(WRAP - lane, WRAP)
    distance = jnp.where(lane < WRAP // 2, lane, lane - WRAP)
    bucket = jnp.clip(distance + BUCKETS // 2, 0, BUCKETS - 1)
    return lax.rem(iota((D, WRAP), 0), BUCKETS) == bucket


def head_mask():
    return iota((16, D), 1) // BUCKETS == iota((16, D), 0)


def position_bias(table, stride, keys, bias_ref):
    per_head = jnp.where(head_mask(), table, 0.0).astype(BF16)
    extended = mm(per_head, onehot(bucket_rows()))
    for head in range(HEADS):
        row = jnp.broadcast_to(extended[head : head + 1], (HALF, WRAP))
        rolled = pltpu.roll(row, 0, 1, stride=stride, stride_axis=0)
        bias_ref[head // 2, HALF * (head % 2) : HALF * (head % 2 + 1), :] = rolled[:, :keys]


def by_head(value):
    low = iota(value.shape, 1) < HEAD_DIM
    zero = jnp.zeros_like(value)
    return jnp.concatenate([jnp.where(low, value, zero), jnp.where(low, zero, value)], 0)


def join_heads(value):
    top, bottom = value[:HALF], value[HALF:]
    return jnp.where(iota(top.shape, 1) < HEAD_DIM, top, bottom)


def norm_forward(summed, gain, shift):
    centered = summed - jnp.mean(summed, -1, keepdims=True)
    inverse = lax.rsqrt(jnp.mean(centered * centered, -1, keepdims=True) + EPSILON)
    normal = centered * inverse
    return normal * gain + shift, normal, inverse


def norm_backward(upstream, normal, inverse, gain):
    scaled = upstream * gain
    bracket = (
        scaled
        - jnp.mean(scaled, -1, keepdims=True)
        - normal * jnp.mean(scaled * normal, -1, keepdims=True)
    )
    return inverse * bracket, rowsum(upstream * normal), rowsum(upstream)


def rowsum(value):
    return jnp.sum(value, 0, keepdims=True)


GELU_A, GELU_B = 0.7978845608028654, 0.044715


def gelu(x):
    return 0.5 * x * (1.0 + jnp.tanh(GELU_A * (x + GELU_B * (x * x * x))))


def gelu_slope(x):
    square = x * x
    t = jnp.tanh(GELU_A * (x + GELU_B * (square * x)))
    inner = GELU_A * (1.0 + 3.0 * GELU_B * square)
    return 0.5 * (1.0 + t) + 0.5 * x * (1.0 - t * t) * inner


KEPT = ("q", "k", "v", "prob", "context", "normal1", "inverse1", "low1", "pre", "hidden", "normal2", "inverse2")


def kept_shapes(keys):
    return {
        "q": ((TOKENS, D), BF16),
        "k": ((2 * keys, D), BF16),
        "v": ((2 * keys, D), BF16),
        "prob": ((2 * PAIRS, 128, keys), F32),
        "context": ((TOKENS, D), BF16),
        "normal1": ((TOKENS, D), F32),
        "inverse1": ((TOKENS, 128), F32),
        "low1": ((TOKENS, D), BF16),
        "pre": ((TOKENS, FF), F32),
        "hidden": ((TOKENS, FF), BF16),
        "normal2": ((TOKENS, D), F32),
        "inverse2": ((TOKENS, 128), F32),
    }


def transpose_vectors(w, vt):
    w.wait(VEC, ATTENTION)
    vt[...] = jnp.transpose(w.vec[...].astype(F32))[:16]


def layer_forward(w, kept, vt, bias, x_query, x_key, source, valid, stride, keys):
    transpose_vectors(w, vt)
    position_bias(vt[12:13, :], stride, keys, bias)
    query_low = x_query[...]
    kept["q"][...] = (mm(query_low, w.w_in[:, :D]) + vt[0:1, :]).astype(BF16)
    key_low = x_key[...]
    kept["k"][...] = mm(key_low, w.w_in[:, D : 2 * D]).astype(BF16)
    kept["v"][...] = (mm(key_low, w.w_in[:, 2 * D :]) + vt[1:2, :]).astype(BF16)
    for row in range(2):
        usable = iota((128, keys), 1) < valid[row]
        for pair in range(PAIRS):
            lanes = slice(128 * pair, 128 * pair + 128)
            q = by_head(kept["q"][HALF * row : HALF * (row + 1), lanes])
            k = kept["k"][keys * row : keys * (row + 1), lanes]
            scores = mm_nt(q, k) * 0.125 + bias[pair]
            scores = jnp.where(usable, scores, NEGATIVE)
            unnormed = jnp.exp(scores - jnp.max(scores, -1, keepdims=True))
            prob = unnormed / jnp.sum(unnormed, -1, keepdims=True)
            kept["prob"][PAIRS * row + pair] = prob
            v = kept["v"][keys * row : keys * (row + 1), lanes]
            context = join_heads(mm(prob.astype(BF16), v))
            kept["context"][HALF * row : HALF * (row + 1), lanes] = context.astype(BF16)
    attended = mm(kept["context"][...], w.w_out[...]) + vt[2:3, :]
    normed, normal, inverse = norm_forward(source + attended, vt[3:4, :], vt[4:5, :])
    kept["normal1"][...] = normal
    kept["inverse1"][...] = jnp.broadcast_to(inverse, (TOKENS, 128))
    normed_low = normed.astype(BF16)
    kept["low1"][...] = normed_low
    w.wait(UP)
    feed = normed + vt[5:6, :]
    for c in range(4):
        lanes = slice(D * c, D * (c + 1))
        pre = mm(normed_low, w.w_up[:, lanes]) + vt[8 + c : 9 + c, :]
        kept["pre"][:, lanes] = pre
        hidden = gelu(pre).astype(BF16)
        kept["hidden"][:, lanes] = hidden
        w.wait(DOWN)
        feed = feed + mm(hidden, w.w_down[:, lanes])
    result, normal, inverse = norm_forward(feed, vt[6:7, :], vt[7:8, :])
    kept["normal2"][...] = normal
    kept["inverse2"][...] = jnp.broadcast_to(inverse, (TOKENS, 128))
    return result


class GradientWriter:
    SLOTS = 3

    def __init__(self, stage, sems):
        self.stage, self.sems, self.flying, self.count = stage, sems, [()] * self.SLOTS, 0

    def write(self, value, line, across, lane):
        slot = self.count % self.SLOTS
        self.count += 1
        self.wait(slot)
        width, limit = value.shape[1], line[1].shape[1]
        self.stage[slot, :, :width] = value.astype(BF16)
        self.flying[slot] = []
        split = min(max(limit - lane, 0), width)
        for k in range(4):
            if k == 0 or split == width:
                parts = [(line[k], 0, width, lane)]
            else:
                parts = [(line[k], 0, split, lane), (across[k], split, width, lane + split - limit)]
            for number, (target, start, stop, at) in enumerate(parts):
                if start == stop:
                    continue
                copy = pltpu.make_async_copy(
                    self.stage.at[slot, pl.ds(CHUNK * k, CHUNK), pl.ds(start, stop - start)],
                    target.at[:, pl.ds(at, stop - start)],
                    self.sems.at[8 * slot + 2 * k + number],
                )
                copy.start()
                self.flying[slot].append(copy)

    def wait(self, slot):
        for copy in self.flying[slot]:
            copy.wait()
        self.flying[slot] = ()

    def finish(self):
        for slot in range(self.SLOTS):
            self.wait(slot)


def turned(index, value, plain, ordered):
    width = value.shape[0]
    plain[:, :width] = jnp.transpose(value)
    for k in range(4):
        for run in range(2):
            row = run_row(index[0], lax.rem(index[1] + k, 4), run)
            at = CHUNK * k + 48 * run
            ordered[at : at + 48, :width] = plain[pl.ds(row, 48), :width]
    return ordered[:, :width]


FEED_ACTS = 2 * D + 2 * FF
ACT_ROWS = TOKENS + 16
ACT_LANES = 4 * D


def feed_gradient_kernel(index, mine, theirs, *refs):
    refs = refs[-14:]
    base, a1, a2, a3, b1, b2, b3, acts, plain, ordered, stage, sems, act_sems = refs[:13]
    line, across = (base, a1, a2, a3), (base, b1, b2, b3)
    copies = []
    for side, ref in enumerate((mine, theirs)):
        target = acts.at[pl.ds(TOKENS * side, TOKENS), :]
        copies.append(pltpu.make_async_copy(ref, target, act_sems.at[side]))
        copies[side].start()
    for copy in copies:
        copy.wait()
    writer = GradientWriter(stage, sems)
    low1 = turned(index, acts[:, :D], plain.at[4], ordered.at[4])
    for c in range(4):
        at = 2 * D + FF + D * c
        writer.write(mm(low1, acts[:, at : at + D]), line, across, D * c)
    feed_grad = acts[:, D + FF : 2 * D + FF]
    for c in range(4):
        hidden = turned(index, acts[:, D + D * c : 2 * D + D * c], plain.at[c], ordered.at[c])
        writer.write(mm(hidden, feed_grad), line, across, FF + D * c)
    writer.finish()


GRADIENT_SCRATCH = [
    pltpu.VMEM((5, 768, 512), BF16),
    pltpu.VMEM((5, 384, 512), BF16),
    pltpu.VMEM((3, 384, 768), BF16),
    pltpu.SemaphoreType.DMA((24,)),
    pltpu.SemaphoreType.DMA((4,)),
]


def feed_gradient(index, mine, theirs, after=()):
    return pl.pallas_call(
        feed_gradient_kernel,
        out_shape=[shape(CHUNK, FEED)] + [shape(CHUNK, FEED_LINE)] * 3 + [shape(CHUNK, FEED - FEED_LINE)] * 3,
        in_specs=[SMEM] + anyspace(2 + len(after)),
        out_specs=anyspace(7),
        scratch_shapes=[pltpu.VMEM((2 * TOKENS, FEED_ACTS), BF16)] + GRADIENT_SCRATCH + [pltpu.VMEM((8, 128), F32)],
        compiler_params=params(28),
        cost_estimate=cost(7),
    )(index, mine, theirs, *after)


def attention_gradient_kernel(keys, outs, index, mine, theirs, *refs):
    refs, scratch = refs[-10 - outs : -10], refs[-10:]
    queries, vectors, keyed, plain, ordered, stage, sems, act_sems, plain_vec, ordered_vec = scratch
    targets = refs[:4], (refs[0], *refs[4:])
    copies = []
    for side, ref in enumerate((mine, theirs)):
        for at, rows, target, sem in (
            (0, TOKENS, queries, act_sems.at[side]),
            (TOKENS, 16, vectors, act_sems.at[2 + side]),
            (ACT_ROWS, keys, keyed, sems.at[side]),
        ):
            lanes = target.shape[1]
            source = ref.at[pl.ds(at, rows), pl.ds(0, lanes)]
            copies.append(pltpu.make_async_copy(source, target.at[pl.ds(rows * side, rows), :], sem))
    for copy in copies:
        copy.start()
    for copy in copies:
        copy.wait()
    writer = GradientWriter(stage, sems)
    context = turned(index, queries[:, :D], plain.at[0], ordered.at[0])
    writer.write(mm(context, queries[:, D : 2 * D]), *targets, OUT_AT)
    query_rows = turned(index, queries[:, 2 * D : 3 * D], plain.at[1], ordered.at[1])
    writer.write(mm(query_rows, queries[:, 3 * D :]), *targets, 0)
    key_rows = turned(index, keyed[:, :D], plain.at[2], ordered.at[2])
    writer.write(mm(key_rows, keyed[:, D : 2 * D]), *targets, D)
    writer.write(mm(key_rows, keyed[:, 2 * D :]), *targets, 2 * D)
    rows = wide(vectors[:16, :]) + wide(vectors[16:, :])
    rows = jnp.concatenate([rows, jnp.zeros((112, D), F32)], 0)
    plain_vec[...] = jnp.transpose(rows)
    for k in range(4):
        for run in range(2):
            row = run_row(index[0], lax.rem(index[1] + k, 4), run)
            at = CHUNK * k + 48 * run
            ordered_vec[at : at + 48, :] = plain_vec[pl.ds(row, 48), :]
    writer.write(ordered_vec[...], *targets, VEC_AT)
    writer.finish()


def attention_gradient(index, mine, theirs, after=()):
    out = [shape(CHUNK, ATTN)] * 4
    keys = mine.shape[0] - ACT_ROWS
    scratch = [
        pltpu.VMEM((2 * TOKENS, ACT_LANES), BF16),
        pltpu.VMEM((32, D), BF16),
        pltpu.VMEM((2 * keys, 3 * D), BF16),
    ]
    vectors = [pltpu.VMEM((768, 128), F32), pltpu.VMEM((384, 128), F32)]
    return pl.pallas_call(
        functools.partial(attention_gradient_kernel, keys, len(out)),
        out_shape=out,
        in_specs=[SMEM] + anyspace(2 + len(after)),
        out_specs=anyspace(len(out)),
        scratch_shapes=scratch + GRADIENT_SCRATCH + vectors,
        compiler_params=params(28),
        cost_estimate=cost(5),
    )(index, mine, theirs, *after)


def feed_backward(w, kept, vt, upstream, acts):
    dsum2, gain2, shift2 = norm_backward(
        upstream, kept["normal2"][...], kept["inverse2"][:, :1], vt[6:7, :]
    )
    feed_grad = dsum2.astype(BF16)
    acts[:, D + FF : 2 * D + FF] = feed_grad
    down_bias = rowsum(wide(feed_grad))
    normed_grad = dsum2
    hidden_bias = []
    for c in range(4):
        lanes = slice(D * c, D * (c + 1))
        w.wait(DOWN)
        hidden_grad = mm_nt(feed_grad, w.w_down[:, lanes])
        pre_grad = (gelu_slope(kept["pre"][:, lanes]) * hidden_grad).astype(BF16)
        at = 2 * D + FF + D * c
        acts[:, at : at + D] = pre_grad
        hidden_bias.append(rowsum(wide(pre_grad)))
        if c == 0:
            w.wait(UP)
        normed_grad = normed_grad + mm_nt(pre_grad, w.w_up[:, lanes])
    acts[:, :D] = kept["low1"][...]
    acts[:, D : D + FF] = kept["hidden"][...]
    zero = jnp.zeros((1, D), F32)
    rows = [zero] * 5 + [down_bias, gain2, shift2] + hidden_bias + [zero] * 4
    return normed_grad, jnp.concatenate(rows, 0)


def attention_backward(
    w, kept, vt, x_query, x_key, normed_grad, vector_rows, stride, keys, acts, work
):
    dq, dk, dv, table = work
    dsum1, gain1, shift1 = norm_backward(
        normed_grad, kept["normal1"][...], kept["inverse1"][:, :1], vt[3:4, :]
    )
    attended_grad = dsum1.astype(BF16)
    out_bias = rowsum(wide(attended_grad))
    acts[:TOKENS, :D] = kept["context"][...]
    acts[:TOKENS, D : 2 * D] = attended_grad
    acts[:TOKENS, 2 * D : 3 * D] = x_query[...]
    context_grad = mm_nt(attended_grad, w.w_out[...]).astype(BF16)
    table[...] = jnp.zeros((16, WRAP), F32)
    mirror = (2 * keys, WRAP)
    mirror = onehot(lax.rem(lax.rem(iota(mirror, 0), keys) + iota(mirror, 1), WRAP) == 0)
    for pair in range(PAIRS):
        lanes = slice(128 * pair, 128 * pair + 128)
        pair_scores = []
        for row in range(2):
            here = slice(HALF * row, HALF * (row + 1))
            there = slice(keys * row, keys * (row + 1))
            grad = by_head(context_grad[here, lanes])
            prob = kept["prob"][PAIRS * row + pair]
            v = kept["v"][there, lanes]
            prob_grad = mm_nt(grad, v)
            dv[there, lanes] = mm_tn(prob.astype(BF16), grad).astype(BF16)
            score = prob * (prob_grad - jnp.sum(prob_grad * prob, -1, keepdims=True))
            score = score.astype(BF16)
            q = by_head(kept["q"][here, lanes])
            k = kept["k"][there, lanes]
            dq[here, lanes] = (0.125 * join_heads(mm(score, k))).astype(BF16)
            dk[there, lanes] = (0.125 * mm_tn(score, q)).astype(BF16)
            pair_scores.append(score)
        spread = mm(jnp.concatenate(pair_scores, 1), mirror)
        for half in range(2):
            rolled = pltpu.roll(
                spread[HALF * half : HALF * (half + 1)], 0, 1, stride=stride, stride_axis=0
            )
            table[2 * pair + half : 2 * pair + half + 1, :] = rowsum(rolled)
    dq_low, dk_low, dv_low = dq[...], dk[...], dv[...]
    source_grad = dsum1 + mm_nt(dq_low, w.w_in[:, :D])
    key_side = mm_nt(dk_low, w.w_in[:, D : 2 * D]) + mm_nt(dv_low, w.w_in[:, 2 * D :])
    acts[:TOKENS, 3 * D :] = dq_low
    acts[ACT_ROWS:, :D] = x_key[...]
    acts[ACT_ROWS:, D : 2 * D] = dk_low
    acts[ACT_ROWS:, 2 * D : 3 * D] = dv_low
    buckets = lax.dot_general(
        table[...],
        bucket_rows(-1).astype(F32),
        (((1,), (1,)), ((), ())),
        precision=lax.Precision.HIGHEST,
        preferred_element_type=F32,
    )
    table_grad = rowsum(jnp.where(head_mask(), buckets, 0.0))
    rows = [rowsum(wide(dq_low)), rowsum(wide(dv_low)), out_bias, gain1, shift1]
    rows += [vector_rows[5:12, :], table_grad, jnp.zeros((3, D), F32)]
    acts[TOKENS:ACT_ROWS, :D] = jnp.concatenate(rows, 0).astype(BF16)
    return source_grad, key_side


FOR_ATTENTION = ("q", "k", "v", "prob", "context", "normal1", "inverse1")
FOR_FEED = ("low1", "pre", "hidden", "normal2", "inverse2")


def pooling():
    return 0.5 * (iota((TOKENS, 2 * SEQ), 1) // 2 == iota((TOKENS, 2 * SEQ), 0)).astype(F32)


def one_forward_kernel(index, tokens, *refs):
    chunks = refs[:15]
    middle, pooled_low, *refs = refs[-20:]
    kept = dict(zip(KEPT, refs[:12]))
    vt, bias, *scratch = refs[12:]
    w = Weights(index, chunks, scratch[:3], scratch[3])
    w.start((ATTENTION, UP, DOWN))
    pooled = mm(pooling().astype(BF16), tokens[...])
    pooled_low[...] = pooled.astype(BF16)
    valid = [index[5], index[6]]
    middle[...] = layer_forward(w, kept, vt, bias, pooled_low, tokens, pooled, valid, 2, SEQ)


def one_forward(index, tokens, chunks, after):
    kept = [shape(*dims, dtype=dtype) for dims, dtype in kept_shapes(SEQ).values()]
    return pl.pallas_call(
        one_forward_kernel,
        out_shape=[shape(TOKENS, D, dtype=F32), shape(TOKENS, D)] + kept,
        in_specs=[SMEM] + vmem(1) + anyspace(15 + len(after)),
        out_specs=vmem(14),
        scratch_shapes=[pltpu.VMEM((16, D), F32), pltpu.VMEM((PAIRS, 128, SEQ), F32)] + WEIGHT_SCRATCH,
        compiler_params=params(),
        cost_estimate=cost(13),
    )(index, tokens, *chunks, *after)


def two_forward_kernel(index, middle, cotangent, *refs):
    chunks, refs = refs[:15], refs[15:]
    result, normed_grad, vector_rows, acts = refs[:4]
    kept = dict(zip(FOR_ATTENTION + FOR_FEED, refs[4:16]))
    vt, bias, middle_low, *scratch = refs[16:]
    w = Weights(index, chunks, scratch[:3], scratch[3])
    w.start((ATTENTION, UP, DOWN))
    middle_low[...] = middle[...].astype(BF16)
    valid = [(index[5] + 1) // 2, (index[6] + 1) // 2]
    out = layer_forward(w, kept, vt, bias, middle_low, middle_low, middle[...], valid, 1, HALF)
    result[...] = out.astype(BF16)
    w.wait = lambda *groups: None
    normed_grad[...], vector_rows[...] = feed_backward(w, kept, vt, cotangent[...], acts)


def two_forward(index, middle, cotangent, chunks):
    dims = kept_shapes(HALF)
    kept = [shape(*dims[name][0], dtype=dims[name][1]) for name in FOR_ATTENTION]
    scratch = [pltpu.VMEM(*dims[name]) for name in FOR_FEED]
    out = [shape(TOKENS, D), shape(TOKENS, D, dtype=F32), shape(16, D, dtype=F32)]
    outs = pl.pallas_call(
        two_forward_kernel,
        out_shape=out + [shape(TOKENS, FEED_ACTS)] + kept,
        in_specs=[SMEM] + vmem(2) + anyspace(15),
        out_specs=vmem(11),
        scratch_shapes=scratch
        + [pltpu.VMEM((16, D), F32), pltpu.VMEM((PAIRS, 128, HALF), F32), pltpu.VMEM((TOKENS, D), BF16)]
        + WEIGHT_SCRATCH,
        compiler_params=params(),
        cost_estimate=cost(17),
    )(index, middle, cotangent, *chunks)
    return outs[:3], outs[3], outs[4:]


def two_backward_kernel(index, middle, normed_grad, vector_rows, *refs):
    kept = dict(zip(FOR_ATTENTION, refs[:7]))
    chunks, refs = refs[7:22], refs[22:]
    upstream, acts, vt, middle_low, *work = refs[:8]
    scratch = refs[8:]
    w = Weights(index, chunks, scratch[:3], scratch[3])
    w.start((ATTENTION,))
    middle_low[...] = middle[...].astype(BF16)
    transpose_vectors(w, vt)
    source_grad, key_side = attention_backward(
        w, kept, vt, middle_low, middle_low, normed_grad[...], vector_rows, 1, HALF, acts, work
    )
    upstream[...] = source_grad + key_side


def two_backward(index, middle, normed_grad, vector_rows, kept, chunks):
    return pl.pallas_call(
        two_backward_kernel,
        out_shape=[shape(TOKENS, D, dtype=F32), shape(ACT_ROWS + TOKENS, ACT_LANES)],
        in_specs=[SMEM] + vmem(10) + anyspace(15),
        out_specs=vmem(2),
        scratch_shapes=[pltpu.VMEM((16, D), F32)]
        + [pltpu.VMEM((TOKENS, D), BF16)] * 4
        + [pltpu.VMEM((16, WRAP), F32)]
        + WEIGHT_SCRATCH,
        compiler_params=params(),
        cost_estimate=cost(10),
    )(index, middle, normed_grad, vector_rows, *kept, *chunks)


def one_feed_kernel(index, upstream, *refs):
    kept = dict(zip(FOR_FEED, refs[:5]))
    chunks = refs[5:20]
    normed_grad, vector_rows, acts, vt, *scratch = refs[-8:]
    w = Weights(index, chunks, scratch[:3], scratch[3])
    w.start((VEC, DOWN, UP))
    transpose_vectors(w, vt)
    normed_grad[...], vector_rows[...] = feed_backward(w, kept, vt, upstream[...], acts)


def one_feed(index, upstream, kept, chunks, after):
    normed_grad, vector_rows, acts = pl.pallas_call(
        one_feed_kernel,
        out_shape=[shape(TOKENS, D, dtype=F32), shape(16, D, dtype=F32), shape(TOKENS, FEED_ACTS)],
        in_specs=[SMEM] + vmem(6) + anyspace(15 + len(after)),
        out_specs=vmem(3),
        scratch_shapes=[pltpu.VMEM((16, D), F32)] + WEIGHT_SCRATCH,
        compiler_params=params(),
        cost_estimate=cost(9),
    )(index, upstream, *kept, *chunks, *after)
    return (normed_grad, vector_rows), acts


def one_backward_kernel(index, tokens, pooled_low, normed_grad, vector_rows, *refs):
    kept = dict(zip(FOR_ATTENTION, refs[:7]))
    chunks = refs[7:22]
    input_grad, acts, vt, *refs = refs[-11:]
    work, scratch = refs[:4], refs[4:]
    w = Weights(index, chunks, scratch[:3], scratch[3])
    w.start((ATTENTION,))
    transpose_vectors(w, vt)
    source_grad, key_side = attention_backward(
        w, kept, vt, pooled_low, tokens, normed_grad[...], vector_rows, 2, SEQ, acts, work
    )
    repeated = lax.dot_general(
        pooling(),
        source_grad,
        (((0,), (0,)), ((), ())),
        precision=lax.Precision.HIGHEST,
        preferred_element_type=F32,
    )
    input_grad[...] = key_side + repeated


def one_backward(index, tokens, pooled_low, normed_grad, vector_rows, kept, chunks, after):
    return pl.pallas_call(
        one_backward_kernel,
        out_shape=[shape(2 * SEQ, D, dtype=F32), shape(ACT_ROWS + 2 * SEQ, ACT_LANES)],
        in_specs=[SMEM] + vmem(11) + anyspace(15 + len(after)),
        out_specs=vmem(2),
        scratch_shapes=[pltpu.VMEM((16, D), F32), pltpu.VMEM((TOKENS, D), BF16)]
        + [pltpu.VMEM((2 * SEQ, D), BF16)] * 2
        + [pltpu.VMEM((16, WRAP), F32)]
        + WEIGHT_SCRATCH,
        compiler_params=params(),
        cost_estimate=cost(13),
    )(index, tokens, pooled_low, normed_grad, vector_rows, *kept, *chunks, *after)


def local(inputs, lengths, cotangent, *weights):
    device = lax.axis_index("dp") * 32 + lax.axis_index("shard")
    sources = lax.dynamic_index_in_dim(jnp.array(spread_sources(), jnp.int32), device, 0, False)
    scalars = [*place_scalars(), lengths[0, 0], lengths[1, 0], jnp.zeros((), jnp.int32)]
    index = jnp.concatenate([jnp.stack(scalars), sources])
    tokens = inputs.reshape(2 * SEQ, D)

    blob = prepare((weights[:5], weights[5:]))
    line = widen(index, [permute(blob, spread_pairs(k)) for k in range(4)])
    parts = [line] + [permute(line, line_pairs(-k)) for k in (1, 2, 3)]
    gather_one = Gather(widen_more(0, index, parts))
    chunk_two = widen_more(1, index, parts, (gather_one.near[0],))
    one = gather_one.finish()
    gather_two = Gather(chunk_two, one[2], one[9])
    middle, pooled_low, *kept = one_forward(index, tokens, one, (gather_two.own_swap,))
    kept = dict(zip(KEPT, kept))
    two = gather_two.finish(middle)

    (result, *back_two), acts_feed, kept_two = two_forward(
        index, middle, cotangent.reshape(TOKENS, D), two
    )
    acts_feed = acts_feed, permute(acts_feed, SWAP)
    upstream, acts_attn = two_backward(index, middle, *back_two, kept_two, two)
    acts_attn = acts_attn, permute(tie(acts_attn, acts_feed[1]), SWAP)

    feed_two = feed_gradient(index, *acts_feed, (upstream,))
    near_feed_two = send_near(feed_two)
    back_one, acts_feed = one_feed(
        index, upstream, [kept[name] for name in FOR_FEED], one, (feed_two[0],)
    )
    acts_feed = acts_feed, permute(tie(acts_feed, *near_feed_two), SWAP)
    attn_two = attention_gradient(index, *acts_attn, (back_one[0], *near_feed_two))
    far_feed_two = send_far(feed_two, *near_feed_two, attn_two[0])
    near_attn_two = send_near(attn_two)
    feed_one = feed_gradient(index, *acts_feed, (attn_two[0],))
    sent = (*far_feed_two, *near_attn_two, feed_one[0])
    far_attn_two = send_far(attn_two, *sent)
    near_feed_one = send_near(feed_one, *sent)
    input_grad, acts_attn = one_backward(
        index,
        tokens,
        pooled_low,
        *back_one,
        [kept[name] for name in FOR_ATTENTION],
        one,
        sent,
    )
    acts_attn = acts_attn, permute(tie(acts_attn, *near_feed_one, *far_attn_two), SWAP)
    far_feed_one = send_far(feed_one, *near_feed_one, *far_attn_two)
    pieces = narrow(WIDTH + ATTN, index, received(feed_two, near_feed_two, far_feed_two))
    attn_one = attention_gradient(index, *acts_attn, (pieces[0],))
    near_attn_one = send_near(attn_one, *far_feed_one)
    far_attn_one = send_far(attn_one, *far_feed_one)

    pieces = narrow(WIDTH, index, received(attn_two, near_attn_two, far_attn_two), pieces)
    pieces = narrow(ATTN, index, received(feed_one, near_feed_one, far_feed_one), pieces)
    pieces = narrow(0, index, received(attn_one, near_attn_one, far_attn_one), pieces)
    pieces = [pieces[0]] + [permute(pieces[k], line_pairs(k)) for k in (1, 2, 3)]
    pieces = narrow_more(index, pieces)
    grads = finish([permute(pieces[k], back(spread_pairs(k))) for k in range(4)])
    return (
        result.reshape(2, 1, HALF, D),
        input_grad.reshape(2, 1, SEQ, D),
        *grads,
    )


def solution(mesh):
    rows = P(None, AXES, None, None)
    shard = P(AXES, None)
    return jax.shard_map(
        local,
        mesh=mesh,
        in_specs=(rows, P(None, AXES), rows) + (shard,) * 10,
        out_specs=(rows, rows) + (shard,) * 10,
        check_vma=False,
    )
```
